32 devices in a mesh: dp: 8 (over z, y), mp: 4 (over x, core).
Axes of the slice: x: 2, y: 2, z: 4, core: 2. Of those that a mesh axis runs over, the one named last changes fastest.
Arguments:
- tokens_in: bfloat16 [8192, 768], P('dp'), may hold values from -6 to 6
- first_values: bfloat16 [8192, 768], P('dp', 'mp'), may hold values from -8 to 8
- skip_source: int32 [12], replicated, may hold values from 0 to 12, as said below
- grad_out: bfloat16 [8192, 768], P('dp'), may hold values from -6 to 6
- qkv_weight: float32 [768, 2304], P('dp', 'mp'), may hold values from -0.3125 to 0.3125
- proj_weight: float32 [768, 768], P('mp', 'dp'), may hold values from -0.875 to 0.875
- fc_weight: float32 [768, 3072], P('dp', 'mp'), may hold values from -0.21875 to 0.21875
- down_weight: float32 [3072, 768], P('mp', 'dp'), may hold values from -0.15625 to 0.15625
- norm_params: float32 [4, 768], P(None, 'dp'), may hold values from -0.5 to 1.5, as said below
- qkv_moment: float32 [768, 2304], P('dp', 'mp'), may hold values from -128 to 128
- proj_moment: float32 [768, 768], P('mp', 'dp'), may hold values from -20 to 20
- fc_moment: float32 [768, 3072], P('dp', 'mp'), may hold values from -32 to 32
- down_moment: float32 [3072, 768], P('mp', 'dp'), may hold values from -40 to 40
- norm_moment: float32 [4, 768], P(None, 'dp'), may hold values from -128 to 128
- qkv_second: float32 [768, 2304], P('dp', 'mp'), may hold values from 32.768 to 131.072
- proj_second: float32 [768, 768], P('mp', 'dp'), may hold values from 1.007616 to 4.01408
- fc_second: float32 [768, 3072], P('dp', 'mp'), may hold values from 2.048 to 8.192
- down_second: float32 [3072, 768], P('mp', 'dp'), may hold values from 3.44064 to 13.9264
- norm_second: float32 [4, 768], P(None, 'dp'), may hold values from 32.768 to 131.072
Outputs:
- block_out: bfloat16 [8192, 768], P(('dp', 'mp'))
- input_grad: float32 [8192, 768], P(('dp', 'mp'))
- first_grad: float32 [8192, 768], P('dp', 'mp')
- qkv_weight_out: float32 [768, 2304], P('dp', 'mp')
- qkv_moment_out: float32 [768, 2304], P('dp', 'mp')
- qkv_second_out: float32 [768, 2304], P('dp', 'mp')
- proj_weight_out: float32 [768, 768], P('mp', 'dp')
- proj_moment_out: float32 [768, 768], P('mp', 'dp')
- proj_second_out: float32 [768, 768], P('mp', 'dp')
- fc_weight_out: float32 [768, 3072], P('dp', 'mp')
- fc_moment_out: float32 [768, 3072], P('dp', 'mp')
- fc_second_out: float32 [768, 3072], P('dp', 'mp')
- down_weight_out: float32 [3072, 768], P('mp', 'dp')
- down_moment_out: float32 [3072, 768], P('mp', 'dp')
- down_second_out: float32 [3072, 768], P('mp', 'dp')
- norm_params_out: float32 [4, 768], P(None, 'dp')
- norm_moment_out: float32 [4, 768], P(None, 'dp')
- norm_second_out: float32 [4, 768], P(None, 'dp')
The draws below stay inside these ranges and needn't reach their ends.
Inputs may be any that keep to these rules, and one draw needn't show every extreme that they name: `skip_source`: exactly 6 entries are below 12, and these are distinct; which heads reuse first-layer values is drawn. `norm_params`: rows 0 and 2 are gains, rows 1 and 3 shifts.
All inputs are finite; a program needn't handle non-finite values.
Results may differ from the reference program's by a relative error of at most 0.012.
The reference program's roundings to bfloat16 on the way count: a program that leaves them out, or rounds other values in their place, can miss the bound.
Values may be sent and summed in bfloat16 or wider, within the bound.
No kernel may reach another device: no remote copies, remote signals or barrier semaphores. Data moves between devices by JAX's collectives and lax.ppermute only.
A program may use at most 128 MiB of HBM per device.

```python
import math
import jax
import jax.numpy as jnp
from jax import lax

D = 768
H = 12
HD = 64
FF = 3072
SEQ = 1024
ADAM_STEP = 5
TOKENS = 8192


def draw_skip_source(key, part):
    order_key, source_key = jax.random.split(jax.random.fold_in(key, 7))
    order = jax.random.permutation(order_key, H)
    sources = jax.random.permutation(source_key, H)
    base = jnp.full((H,), H, dtype=jnp.int32)
    return base.at[order[:H // 2]].set(sources[:H // 2].astype(jnp.int32)).astype(jnp.int32)


def draw_norm_params(key, part):
    base = jax.random.uniform(jax.random.fold_in(key, 3), (4, D), dtype=jnp.float32)
    rows = lax.broadcasted_iota(jnp.int32, (4, D), 0)
    gains = 0.6 + 0.8 * base
    shifts = 0.8 * (base - 0.5)
    return jnp.where(rows % 2 == 0, gains, shifts).astype(jnp.float32)


def steps_of(stream_key, extent, cuts, least, top_value):
    loudness, own = 1.0, jax.random.fold_in(stream_key, 6)
    for axis_at, parts in cuts:
        heights = jnp.exp(jax.random.uniform(jax.random.fold_in(own, axis_at), (parts,), jnp.float32, least / len(cuts), top_value / len(cuts)))
        loudness = loudness * jnp.repeat(heights, extent[axis_at] // parts).reshape([-1 if axis == axis_at else 1 for axis in range(len(extent))])
    return loudness


def scatter_about(stream_key, shape, scale, most, cuts=(), kind=jnp.bfloat16):
    values = scale * jax.random.normal(stream_key, shape, jnp.float32)
    if cuts:
        values = values * steps_of(stream_key, shape, cuts, -0.22, 0.18)
    return jnp.clip(values, -most, most).astype(kind)


def setup_inputs(seed: int = 0) -> dict:
    streams_of = jax.random.split(jax.random.key(seed), 20)
    return {
        "tokens_in": scatter_about(streams_of[0], (TOKENS, D), 1.0, 6.0, ((0, 8),)),
        "first_values": scatter_about(streams_of[1], (TOKENS, D), 1.4, 8.0, ((0, 8), (1, 4))),
        "skip_source": draw_skip_source(jax.random.fold_in(streams_of[19], 71), 0),
        "grad_out": scatter_about(streams_of[3], (TOKENS, D), 1.0, 6.0, ((0, 8),)),
        "qkv_weight": scatter_about(streams_of[4], (D, 3 * D), (D // 2) ** -0.5, 0.3125, ((0, 8), (1, 4)), jnp.float32),
        "proj_weight": scatter_about(streams_of[5], (D, D), (D // 16) ** -0.5, 0.875, ((0, 4), (1, 8)), jnp.float32),
        "fc_weight": scatter_about(streams_of[6], (D, FF), D ** -0.5, 0.21875, ((0, 8), (1, 4)), jnp.float32),
        "down_weight": scatter_about(streams_of[7], (FF, D), (FF // 2) ** -0.5, 0.15625, ((0, 4), (1, 8)), jnp.float32),
        "norm_params": draw_norm_params(jax.random.fold_in(streams_of[19], 71), 0),
        "qkv_moment": scatter_about(streams_of[9], (D, 3 * D), (0.22 * TOKENS ** 0.5), 128.0, ((0, 8), (1, 4)), jnp.float32),
        "proj_moment": scatter_about(streams_of[10], (D, D), (0.039 * TOKENS ** 0.5), 20.0, ((0, 4), (1, 8)), jnp.float32),
        "fc_moment": scatter_about(streams_of[11], (D, FF), (0.055 * TOKENS ** 0.5), 32.0, ((0, 8), (1, 4)), jnp.float32),
        "down_moment": scatter_about(streams_of[12], (FF, D), (0.072 * TOKENS ** 0.5), 40.0, ((0, 4), (1, 8)), jnp.float32),
        "norm_moment": scatter_about(streams_of[13], (4, D), (0.22 * TOKENS ** 0.5), 128.0, ((1, 8),), jnp.float32),
        "qkv_second": jnp.clip(jnp.exp(math.log(131.072) - 1.3862944 * jax.random.uniform(streams_of[14], (D, 3 * D), jnp.float32) ** steps_of(streams_of[14], (D, 3 * D), ((0, 8), (1, 4)), -0.2, 0.2)), 32.768, 131.072),
        "proj_second": jnp.clip(jnp.exp(math.log(4.01408) - 1.382221 * jax.random.uniform(streams_of[15], (D, D), jnp.float32) ** steps_of(streams_of[15], (D, D), ((0, 4), (1, 8)), -0.2, 0.2)), 1.007616, 4.01408),
        "fc_second": jnp.clip(jnp.exp(math.log(8.192) - 1.3862944 * jax.random.uniform(streams_of[16], (D, FF), jnp.float32) ** steps_of(streams_of[16], (D, FF), ((0, 8), (1, 4)), -0.2, 0.2)), 2.048, 8.192),
        "down_second": jnp.clip(jnp.exp(math.log(13.9264) - 1.39812884 * jax.random.uniform(streams_of[17], (FF, D), jnp.float32) ** steps_of(streams_of[17], (FF, D), ((0, 4), (1, 8)), -0.2, 0.2)), 3.44064, 13.9264),
        "norm_second": jnp.clip(jnp.exp(math.log(131.072) - 1.3862944 * jax.random.uniform(streams_of[18], (4, D), jnp.float32) ** steps_of(streams_of[18], (4, D), ((1, 8),), -0.2, 0.2)), 32.768, 131.072),
    }


@jax.custom_vjp
def low(v):
    return lax.optimization_barrier(v.astype(jnp.bfloat16)).astype(jnp.float32)

@jax.custom_vjp
def low_back(v):
    return v

def low_keep(v):
    return (low(v), None)

def low_pass(kept, grad):
    return (grad,)

def back_keep(v):
    return (v, None)

def back_low(kept, grad):
    return (low(grad),)
low.defvjp(low_keep, low_pass)
low_back.defvjp(back_keep, back_low)

def rounded_both(value):
    return low(low_back(value))

def layer_norm(values, gain, shift):
    center = values - lax.optimization_barrier(jnp.mean(values, axis=-1, keepdims=True))
    spread = lax.optimization_barrier(jnp.mean(center * center, axis=-1, keepdims=True))
    return center * lax.rsqrt(spread + 1e-05) * gain + shift

def gelu_tanh(values):
    return jax.nn.gelu(values, approximate=True)

def forward(params, tokens, firsts, selector, reuse):
    highest = lax.Precision.HIGHEST
    qkv_w, proj_w, fc_w, down_w, norms = [low(item) for item in params]
    count = tokens.shape[0]
    normed_one = low(layer_norm(tokens, norms[0], norms[1]))
    mixed = jnp.dot(normed_one, qkv_w, precision=highest).reshape(count, H, 3, HD)
    queries = rounded_both(mixed[:, :, 0])
    keys = rounded_both(mixed[:, :, 1])
    fresh = rounded_both(mixed[:, :, 2])
    chosen = jnp.einsum('tgd,hg->thd', firsts, selector, precision=highest)
    values = jnp.where(reuse[None, :, None], chosen, fresh)
    scores = low_back(jnp.einsum('qhd,khd->hqk', queries, keys, precision=highest) * HD ** (-0.5))
    rows = lax.broadcasted_iota(jnp.int32, (count, count), 0)
    cols = lax.broadcasted_iota(jnp.int32, (count, count), 1)
    scores = jnp.where((cols <= rows)[None], scores, -1e+30)
    probs = low(jax.nn.softmax(scores, axis=-1))
    context = rounded_both(jnp.einsum('hqk,khd->qhd', probs, values, precision=highest).reshape(count, H * HD))
    middle = tokens + low_back(jnp.dot(context, proj_w, precision=highest))
    normed_two = low(layer_norm(middle, norms[2], norms[3]))
    hidden = low(gelu_tanh(low_back(jnp.dot(normed_two, fc_w, precision=highest))))
    return middle + low_back(jnp.dot(hidden, down_w, precision=highest))

def adamw(master, moment, second, grad, rate, weighted):
    moment_new = 0.9 * moment + 0.1 * grad
    second_new = 0.999 * second + 0.001 * grad * grad
    mean_hat = moment_new / (1.0 - 0.9 ** ADAM_STEP)
    var_hat = second_new / (1.0 - 0.999 ** ADAM_STEP)
    master_new = master - rate * (mean_hat / (jnp.sqrt(var_hat) + 1e-08) + weighted * master)
    return (master_new, moment_new, second_new)

def add_pair(first, second):
    return first + second

def reference(tokens_in, first_values, skip_source, grad_out, qkv_weight, proj_weight, fc_weight, down_weight, norm_params, qkv_moment, proj_moment, fc_moment, down_moment, norm_moment, qkv_second, proj_second, fc_second, down_second, norm_second):
    params = (qkv_weight, proj_weight, fc_weight, down_weight, norm_params)
    heads = jnp.arange(H, dtype=jnp.int32)
    selector = (skip_source.astype(jnp.int32)[:, None] == heads[None, :]).astype(jnp.float32)
    reuse = skip_source.astype(jnp.int32) < H
    sequences = tokens_in.shape[0] // SEQ
    tokens = tokens_in.astype(jnp.float32).reshape(sequences, SEQ, D)
    firsts = first_values.astype(jnp.float32).reshape(sequences, SEQ, H, HD)
    upstream = grad_out.astype(jnp.float32).reshape(sequences, SEQ, D)

    def one_sequence(totals, group):
        seq_tokens, seq_firsts, seq_up = group

        def run(weights, tok, fir):
            return forward(weights, tok, fir, selector, reuse)
        result, pullback = jax.vjp(run, params, seq_tokens, seq_firsts)
        grad_params, grad_tokens, grad_firsts = pullback(seq_up)
        totals = jax.tree.map(add_pair, totals, grad_params)
        return (totals, (result.astype(jnp.bfloat16), grad_tokens, grad_firsts))
    zeros = jax.tree.map(jnp.zeros_like, params)
    grads, outputs = lax.scan(one_sequence, zeros, (tokens, firsts, upstream))
    block_out = outputs[0].reshape(sequences * SEQ, D)
    input_grad = outputs[1].reshape(sequences * SEQ, D)
    first_grad = outputs[2].reshape(sequences * SEQ, D)
    qkv_new = adamw(qkv_weight, qkv_moment, qkv_second, grads[0], 0.06, 0.1)
    proj_new = adamw(proj_weight, proj_moment, proj_second, grads[1], 0.15, 0.1)
    fc_new = adamw(fc_weight, fc_moment, fc_second, grads[2], 0.04, 0.1)
    down_new = adamw(down_weight, down_moment, down_second, grads[3], 0.03, 0.1)
    norm_new = adamw(norm_params, norm_moment, norm_second, grads[4], 0.3, 0.0)
    return (block_out, input_grad, first_grad, qkv_new[0], qkv_new[1], qkv_new[2], proj_new[0], proj_new[1], proj_new[2], fc_new[0], fc_new[1], fc_new[2], down_new[0], down_new[1], down_new[2], norm_new[0], norm_new[1], norm_new[2])
```

```python
import functools

import jax
import jax.numpy as jnp
import numpy as np
from jax import lax
from jax.experimental import pallas as pl
from jax.experimental.pallas import tpu as pltpu
from jax.sharding import PartitionSpec as P

H = 12
HD = 64
ADAM_STEP = 5
EPS = 1e-05
MASKED = -1e30
RB = 256
LANES = 128
RING = (0, 2, 4, 6, 7, 5, 3, 1)
OFFSETS = (0, -1, -2, -3, -4, 1, 2, 3)
GELU_A = 0.7978845608028654
GELU_B = 0.044715

bf16 = jnp.bfloat16
f32 = jnp.float32


def dot(a, b):
    return jnp.dot(a, b, preferred_element_type=f32)


def dot_nt(a, b):
    return lax.dot_general(a, b, (((1,), (1,)), ((), ())), preferred_element_type=f32)


def dot_tn(a, b):
    return lax.dot_general(a, b, (((0,), (0,)), ((), ())), preferred_element_type=f32)


def call(kernel, name, grid, scalars, ins, outs, flops, moved, scratch=(), exps=0, vmem=32):
    def spec(shape, given):
        if given is not None:
            return given
        return pl.BlockSpec(shape, lambda *_: (0,) * len(shape))

    return pl.pallas_call(
        kernel,
        grid_spec=pltpu.PrefetchScalarGridSpec(
            num_scalar_prefetch=len(scalars),
            grid=grid,
            in_specs=[spec(a.shape, s) for a, s in ins],
            out_specs=[spec(sh, s) for sh, _, s in outs],
            scratch_shapes=list(scratch),
        ),
        out_shape=[jax.ShapeDtypeStruct(sh, dt) for sh, dt, _ in outs],
        compiler_params=pltpu.CompilerParams(
            dimension_semantics=("arbitrary",) * len(grid), vmem_limit_bytes=vmem * 1024 * 1024
        ),
        cost_estimate=pl.CostEstimate(flops=flops, bytes_accessed=moved, transcendentals=exps),
        name=name,
    )(*scalars, *[a for a, _ in ins])


def assemble(info, pieces, target, lanes=None):
    rows = target.shape[0] // len(pieces)
    for k, piece in enumerate(pieces):
        at = pl.multiple_of(info[4 + k] * rows, rows)
        target[pl.ds(at, rows), :] = piece[...] if lanes is None else piece[:, lanes[0] : lanes[1]]


def norm_stats(values):
    center = values - jnp.mean(values, axis=-1, keepdims=True)
    scale = lax.rsqrt(jnp.mean(center * center, axis=-1, keepdims=True) + EPS)
    return center * scale, scale


def selection(sources, owner, heads, of_rows):
    width = heads * HD
    rows = lax.broadcasted_iota(jnp.int32, (width, width), 0)
    cols = lax.broadcasted_iota(jnp.int32, (width, width), 1)
    held, user = (cols, rows) if of_rows else (rows, cols)
    source = jnp.full((width, width), H, jnp.int32)
    for j in range(heads):
        source = jnp.where(user // HD == j, sources[j], source)
    hit = (owner * heads + held // HD == source) & (rows % HD == cols % HD)
    return jnp.where(hit, 1.0, 0.0).astype(bf16)


def qkv_kernel(n, heads, info, src, x_ref, f0, f1, f2, f3, *refs):
    pieces, (a1_ref, m_ref, v_ref, w_ref, norm_ref) = refs[:n], refs[n:]
    cols = m_ref.shape[1]

    @pl.when(pl.program_id(0) == 0)
    def _():
        assemble(info, pieces, w_ref)
        base = cols // LANES * LANES
        turned = w_ref[:, base : base + LANES].astype(f32).T
        norm_ref[...] = turned[cols - base : cols - base + 8]

    unit, _ = norm_stats(x_ref[...].astype(f32))
    a1 = (unit * norm_ref[0:1] + norm_ref[1:2]).astype(bf16)
    a1_ref[...] = a1
    mixed = dot(a1, w_ref[:, :cols]).astype(bf16)
    m_ref[...] = mixed
    mp = info[2]
    sources = [src[mp * heads + j] for j in range(heads)]
    chosen = jnp.zeros(v_ref.shape, f32)
    for r, first in enumerate((f0, f1, f2, f3)):
        chosen += dot(first[...], selection(sources, mp ^ r, heads, False))
    lane = lax.broadcasted_iota(jnp.int32, v_ref.shape, 1) // HD
    reuse = jnp.zeros(v_ref.shape, jnp.int32)
    for j in range(heads):
        reuse = jnp.where(lane == j, jnp.where(sources[j] < H, 1, 0), reuse)
    fresh = jnp.concatenate(
        [mixed[:, (3 * j + 2) * HD : (3 * j + 3) * HD].astype(f32) for j in range(heads)], 1
    )
    v_ref[...] = jnp.where(reuse == 1, chosen, fresh).astype(bf16)


def masked_tile():
    keys = lax.broadcasted_iota(jnp.int32, (RB, RB), 0)
    queries = lax.broadcasted_iota(jnp.int32, (RB, RB), 1)
    return keys <= queries


def attend_kernel(heads, base, m_ref, v_ref, c_ref, lse_ref):
    keep = masked_tile()
    blocks = c_ref.shape[0] // RB
    turned = [[None] * heads for _ in range(blocks)]
    lse_ref[...] = jnp.zeros(lse_ref.shape, f32)
    for h in range(heads):
        keys = m_ref[:, (3 * h + 1) * HD : (3 * h + 2) * HD]
        values_t = v_ref[:, h * HD : (h + 1) * HD].T
        for i in range(blocks):
            lo = base + i * RB
            hi = lo + RB
            query = m_ref[lo:hi, 3 * h * HD : (3 * h + 1) * HD] * bf16(HD**-0.5)
            diag = jnp.where(keep, dot_nt(keys[lo:hi], query), MASKED)
            peak = jnp.max(diag, 0, keepdims=True)
            if lo:
                left = dot_nt(keys[:lo], query)
                peak = jnp.maximum(peak, jnp.max(left, 0, keepdims=True))
            diag = jnp.exp(diag - peak)
            total = jnp.sum(diag, 0, keepdims=True)
            if lo:
                left = jnp.exp(left - peak)
                total += jnp.sum(left, 0, keepdims=True)
            inverse = 1.0 / total
            context = dot(values_t[:, lo:hi], (diag * inverse).astype(bf16))
            if lo:
                context += dot(values_t[:, :lo], (left * inverse).astype(bf16))
            turned[i][h] = context
            lse_ref[h : h + 1, i * RB : (i + 1) * RB] = peak + jnp.log(total)
    for i in range(blocks):
        c_ref[i * RB : (i + 1) * RB] = jnp.concatenate(turned[i], 0).T.astype(bf16)


def mlp_kernel(n, info, x_ref, e_ref, norm_ref, c0, c1, c2, c3, wpc_ref, *refs):
    fused, down = refs[:n], refs[n : 2 * n]
    (a2_ref, g_ref, du_ref, dsend, dkeep, ysend, ykeep, rkeep, nacc, wp_out) = refs[2 * n : 2 * n + 10]
    wf, wd, w2, w1, w3 = refs[2 * n + 10 :]
    w0 = wp_out
    step = pl.program_id(0)
    hid, cw = wf.shape[1], w0.shape[1]

    @pl.when(step == 0)
    def _():
        assemble(info, fused, wf, (0, hid))
        assemble(info, fused, w0, (hid, hid + cw))
        assemble(info, fused, w2, (hid + cw, hid + 2 * cw))
        rows = wf.shape[0] // n
        for k in range(n):
            at = pl.multiple_of(info[4 + k] * rows, rows)
            w1[pl.ds(at, rows), :] = wpc_ref[k * rows : (k + 1) * rows, :cw]
            w3[pl.ds(at, rows), :] = wpc_ref[k * rows : (k + 1) * rows, cw:]
        assemble(info, down, wd)
        nacc[...] = jnp.zeros(nacc.shape, f32)

    resid = x_ref[...].astype(f32) + (
        (dot_nt(c0[...], w0[...]) + dot_nt(c1[...], w1[...]))
        + (dot_nt(c2[...], w2[...]) + dot_nt(c3[...], w3[...]))
    )
    unit, _ = norm_stats(resid)
    a2 = (unit * norm_ref[2:3] + norm_ref[3:4]).astype(bf16)
    a2_ref[...] = a2
    u = dot(a2, wf[...])
    square = u * u
    t = jnp.tanh(GELU_A * u * (1.0 + GELU_B * square))
    g = (0.5 * u * (1.0 + t)).astype(bf16)
    slope = 0.5 * (1.0 + t) + 0.5 * u * (1.0 - t * t) * (GELU_A * (1.0 + 3.0 * GELU_B * square))
    g_ref[...] = g
    du = (dot(e_ref[...], wd[...]) * slope).astype(bf16)
    du_ref[...] = du
    grad = dot_nt(du, wf[...])
    out = dot_nt(g, wd[...])
    nacc[2:3] += jnp.sum(grad * unit, 0, keepdims=True)
    nacc[3:4] += jnp.sum(grad, 0, keepdims=True)

    @pl.when(step == 0)
    def _():
        dsend[...] = grad.astype(bf16)
        ysend[...] = out.astype(bf16)

    @pl.when(step == 1)
    def _():
        dkeep[...] = grad
        ykeep[...] = out
        rkeep[...] = resid


def mlp_grad_kernel(a2a, a2b, dua, dub, ea, eb, ga, gb, out):
    hid = dua.shape[1]
    out[:, :hid] = (dot_tn(a2a[...], dua[...]) + dot_tn(a2b[...], dub[...])).astype(bf16)
    out[:, hid:] = (dot_tn(ea[...], ga[...]) + dot_tn(eb[...], gb[...])).astype(bf16)


def norm_back(unit, scale, gain, grad):
    dy = grad * gain
    return scale * (
        dy - jnp.mean(dy, -1, keepdims=True) - unit * jnp.mean(dy * unit, -1, keepdims=True)
    )


def norm_two_kernel(info, r_ref, own, received, e_ref, norm_ref, dr_ref, ab_ref):
    unit, scale = norm_stats(r_ref[...])
    grad = own[...].astype(f32) + received[...].astype(f32)
    dr = e_ref[...].astype(f32) + norm_back(unit, scale, norm_ref[2:3], grad)
    dr_ref[...] = dr
    ab_ref[...] = dr.astype(bf16)


def attend_back_kernel(heads, base, last, info, src, m_ref, v_ref, own, part, wp, lse_ref, *refs):
    if last:
        dqa, dka, dva, ab_ref, dm_ref, dvr_ref = refs
    else:
        ab_ref, dq_ref, dk_ref, dv_ref = refs
    keep = masked_tile()
    core = info[0]
    rows = 2 * RB
    blocks = 2
    at = pl.multiple_of(core * RB, RB)
    ab_ref[pl.ds(at, RB), :] = own[...]
    at = pl.multiple_of((1 - core) * RB, RB)
    ab_ref[pl.ds(at, RB), :] = part[...]
    tiles = (base + rows) // RB
    dctx = [dot(ab_ref[i * RB : (i + 1) * RB], wp[...]).astype(bf16) for i in range(blocks)]
    dq_t = [[None] * heads for _ in range(blocks)]
    dks, dvs = [], []
    for h in range(heads):
        keys = m_ref[:, (3 * h + 1) * HD : (3 * h + 2) * HD]
        keys_t = keys.T
        values = v_ref[:, h * HD : (h + 1) * HD]
        dk = [None] * tiles
        dv = [None] * tiles
        for i in range(blocks):
            lo = base + i * RB
            count = lo // RB + 1
            query = m_ref[lo : lo + RB, 3 * h * HD : (3 * h + 1) * HD] * bf16(HD**-0.5)
            dc = dctx[i][:, h * HD : (h + 1) * HD]
            lse = lse_ref[h : h + 1, i * RB : (i + 1) * RB]
            probs, dprobs = [], []
            inner = jnp.zeros((1, RB), f32)
            for t in range(count):
                spot = slice(t * RB, (t + 1) * RB)
                score = dot_nt(keys[spot], query)
                prob = jnp.exp(score - lse)
                if t == count - 1:
                    prob = jnp.where(keep, prob, 0.0)
                dprob = dot_nt(values[spot], dc)
                inner += jnp.sum(prob * dprob, 0, keepdims=True)
                more = dot(prob.astype(bf16), dc)
                dv[t] = more if dv[t] is None else dv[t] + more
                probs.append(prob)
                dprobs.append(dprob)
            total = None
            for t in range(count):
                spot = slice(t * RB, (t + 1) * RB)
                ds = (probs[t] * (dprobs[t] - inner)).astype(bf16)
                more = dot(ds, query)
                dk[t] = more if dk[t] is None else dk[t] + more
                more = dot(keys_t[:, spot], ds)
                total = more if total is None else total + more
            dq_t[i][h] = total * HD**-0.5
        dks.append(dk)
        dvs.append(dv)
    dq = [jnp.concatenate(dq_t[i], 0).T for i in range(blocks)]
    if not last:
        for i in range(blocks):
            dq_ref[i * RB : (i + 1) * RB] = dq[i]
        for t in range(tiles):
            dk_ref[t * RB : (t + 1) * RB] = jnp.concatenate([dks[h][t] for h in range(heads)], 1)
            dv_ref[t * RB : (t + 1) * RB] = jnp.concatenate([dvs[h][t] for h in range(heads)], 1)
        return
    mp = info[2]
    fresh = [jnp.where(src[mp * heads + h] < H, 0.0, 1.0) for h in range(heads)]
    reuse = [jnp.where(src[mp * heads + h] < H, 1.0, 0.0) for h in range(heads)]
    for t in range(tiles):
        spot = slice(t * RB, (t + 1) * RB)
        first = t * RB < base
        parts, reused = [], []
        for h in range(heads):
            lane = slice(h * HD, (h + 1) * HD)
            dqh = dqa[spot, lane] if first else dq[t - base // RB][:, lane]
            dkh = dks[h][t] + dka[spot, lane] if first else dks[h][t]
            dvh = dvs[h][t] + dva[spot, lane] if first else dvs[h][t]
            parts += [dqh, dkh, dvh * fresh[h]]
            reused.append(dvh * reuse[h])
        pad = dm_ref.shape[1] - 3 * HD * heads
        parts.append(jnp.zeros((RB, pad), f32))
        dm_ref[spot, :] = jnp.concatenate(parts, 1).astype(bf16)
        dvr_ref[spot, :] = jnp.concatenate(reused, 1).astype(bf16)


def input_kernel(info, dm_ref, w_ref, x_ref, na, nb, send, keep, norm_out):
    step = pl.program_id(0)

    @pl.when(step == 0)
    def _():
        norm_out[...] = na[...] + nb[...]

    grad = dot_nt(dm_ref[...], w_ref[...])
    unit, _ = norm_stats(x_ref[...].astype(f32))
    norm_out[0:1] += jnp.sum(grad * unit, 0, keepdims=True)
    norm_out[1:2] += jnp.sum(grad, 0, keepdims=True)

    @pl.when(step < 2)
    def _():
        send[...] = grad.astype(bf16)

    @pl.when(step >= 2)
    def _():
        keep[...] = grad


def qkv_grad_kernel(cols, a1_ref, dm_ref, aba, abb, ca, cb, norm_ref, out):
    width = dm_ref.shape[1]
    base = cols // LANES * LANES
    grad = dot_tn(a1_ref[...], dm_ref[...])
    rows = norm_ref.shape[1]
    turned = jnp.concatenate(
        [jnp.zeros((cols - base, rows), f32), norm_ref[...], jnp.zeros((LANES - 8 - cols + base, rows), f32)], 0
    ).T
    out[:, :base] = grad[:, :base].astype(bf16)
    out[:, base:width] = (grad[:, base:] + turned).astype(bf16)
    out[:, width:] = (dot_tn(aba[...], ca[...]) + dot_tn(abb[...], cb[...])).astype(bf16)


def norm_one_kernel(info, x_ref, own, received, dra, drb, norm_ref, out):
    unit, scale = norm_stats(x_ref[...].astype(f32))
    grad = own[...] + received[...].astype(f32)
    dr = jnp.where(info[1] == 0, dra[...], drb[...])
    out[...] = dr + norm_back(unit, scale, norm_ref[0:1], grad)


def first_kernel(heads, info, src, d0, d1, d2, d3, out):
    mp = info[2]
    total = jnp.zeros(out.shape, f32)
    for r, ref in enumerate((d0, d1, d2, d3)):
        sources = [src[(mp ^ r) * heads + j] for j in range(heads)]
        total += dot(ref[...], selection(sources, mp, heads, True))
    out[...] = total


def swap_core(value):
    return lax.ppermute(value, "mp", [(i, i ^ 1) for i in range(4)])


def swap_x(value):
    return lax.ppermute(value, "mp", [(i, i ^ 2) for i in range(4)])


def gather_four(value):
    across = swap_x(value)
    return [value, swap_core(value), across, swap_core(across)]


FORWARD = [(RING[i], RING[(i + 1) % 8]) for i in range(8)]
BACKWARD = [(b, a) for a, b in FORWARD]


def gather_ring(piece):
    if lax.axis_size("dp") != len(RING):
        return [lax.all_gather(piece, "dp", axis=0, tiled=True)]
    ahead, behind = [], []
    a = b = piece
    for k in range(4):
        a = lax.ppermute(a, "dp", FORWARD)
        ahead.append(a)
        if k < 3:
            b = lax.ppermute(b, "dp", BACKWARD)
            behind.append(b)
    return [piece] + ahead + behind


def scatter_ring(full, info):
    n = lax.axis_size("dp")
    if n != len(RING):
        return lax.psum_scatter(full.astype(f32), "dp", scatter_dimension=0, tiled=True)
    rows = full.shape[0] // n

    def part(offset):
        at = info[4 + OFFSETS.index(offset)] * rows
        return lax.dynamic_slice_in_dim(full, at, rows, 0)

    a, b = part(-4), part(-3)
    for k in (3, 2, 1, 0):
        a = lax.ppermute(a, "dp", FORWARD)
        if k:
            a = (a.astype(f32) + part(k).astype(f32)).astype(bf16)
            b = lax.ppermute(b, "dp", BACKWARD)
            if k > 1:
                b = (b.astype(f32) + part(1 - k).astype(f32)).astype(bf16)
    return a.astype(f32) + b.astype(f32) + part(0).astype(f32)


def after(value, *others):
    return lax.optimization_barrier((value,) + others)[0]


def adamw(master, moment, second, grad, rate, weighted):
    moment_new = 0.9 * moment + 0.1 * grad
    second_new = 0.999 * second + 0.001 * grad * grad
    mean_hat = moment_new / (1.0 - 0.9**ADAM_STEP)
    var_hat = second_new / (1.0 - 0.999**ADAM_STEP)
    master_new = master - rate * (mean_hat / (jnp.sqrt(var_hat) + 1e-08) + weighted * master)
    return (master_new, moment_new, second_new)


def device_table(n):
    table = np.zeros((n * 4, 16), np.int32)
    for dp in range(n):
        for mp in range(4):
            table[dp * 4 + mp, :3] = (mp % 2, mp // 2, mp)
            if n == len(RING):
                at = RING.index(dp)
                for k, offset in enumerate(OFFSETS):
                    table[dp * 4 + mp, 4 + k] = RING[(at + offset) % n]
    return table


def local(
    tokens_in,
    first_values,
    skip_source,
    grad_out,
    qkv_weight,
    proj_weight,
    fc_weight,
    down_weight,
    norm_params,
    qkv_moment,
    proj_moment,
    fc_moment,
    down_moment,
    norm_moment,
    qkv_second,
    proj_second,
    fc_second,
    down_second,
    norm_second,
):
    n = lax.axis_size("dp")
    pieces = n if n == len(RING) else 1
    count, width = tokens_in.shape
    cols = qkv_weight.shape[1]
    heads = cols // (3 * HD)
    cw = heads * HD
    hid = fc_weight.shape[1]
    wide = -(-(cols + 4) // LANES) * LANES
    half = count // 2
    me = lax.axis_index("dp") * 4 + lax.axis_index("mp")
    info = lax.dynamic_slice_in_dim(jnp.asarray(device_table(n)), me, 1, 0)[0]
    src = skip_source

    shard = qkv_weight.shape[0]
    ring_one = jnp.concatenate(
        [
            qkv_weight.astype(bf16),
            norm_params.T.astype(bf16),
            jnp.zeros((shard, wide - cols - 4), bf16),
        ],
        1,
    )
    one = gather_ring(ring_one)
    firsts = gather_four(first_values)
    proj_t = proj_weight.T.astype(bf16)
    proj_pair = jnp.concatenate([proj_t, swap_x(proj_t)], 1)
    ring_two = jnp.concatenate([fc_weight.astype(bf16), proj_pair], 1)
    ring_two = after(ring_two, one[-1])
    two = gather_ring(ring_two)
    ring_three = after(down_weight.T.astype(bf16), two[len(two) // 8])
    three = gather_ring(ring_three)
    proj_other = swap_core(jnp.concatenate([p[:, hid:] for p in two], 0))

    row = lambda w: pl.BlockSpec((RB, w), lambda i, *_: (i, 0))
    a1, mixed, values, qkv_full, norms = call(
        functools.partial(qkv_kernel, pieces, heads),
        "qkv",
        (count // RB,),
        (info, src),
        [(tokens_in, row(width))] + [(f, row(cw)) for f in firsts] + [(p, None) for p in one],
        [
            ((count, width), bf16, row(width)),
            ((count, cols), bf16, row(cols)),
            ((count, cw), bf16, row(cw)),
            ((width, wide), bf16, None),
            ((8, width), f32, None),
        ],
        flops=2 * count * width * cols,
        moved=2 * count * (2 * width + 2 * cols),
    )

    def attend(part):
        keys = (part + 1) * half
        top = lambda w: pl.BlockSpec((keys, w), lambda i: (0, 0))
        return call(
            functools.partial(attend_kernel, heads, part * half),
            f"attend{part}",
            (1,),
            (),
            [(mixed, top(cols)), (values, top(cw))],
            [((half, cw), bf16, None), ((8, half), f32, None)],
            flops=4 * half * keys * 256 * heads,
            moved=2 * keys * (cols + cw),
            exps=half * keys * heads,
        )

    context, lse = zip(*[attend(part) for part in range(2)])
    contexts = [gather_four(c) for c in context]

    def mlp(part):
        block = lambda w: pl.BlockSpec((RB, w), lambda i, s: ((1 - s[0]) ^ i, 0))
        whole = lambda w: pl.BlockSpec((RB, w), lambda i, s: (2 * part + ((1 - s[0]) ^ i), 0))
        weights = lambda w: pltpu.VMEM((width, w), bf16)
        return call(
            functools.partial(mlp_kernel, pieces),
            f"mlp{part}",
            (2,),
            (info,),
            [(tokens_in, whole(width)), (grad_out, whole(width)), (norms, None)]
            + [(c, block(cw)) for c in contexts[part]]
            + [(proj_other, None)]
            + [(p, None) for p in two]
            + [(p, None) for p in three],
            [
                ((half, width), bf16, block(width)),
                ((half, hid), bf16, block(hid)),
                ((half, hid), bf16, block(hid)),
                ((RB, width), bf16, None),
                ((RB, width), f32, None),
                ((RB, width), bf16, None),
                ((RB, width), f32, None),
                ((RB, width), f32, None),
                ((8, width), f32, None),
                ((width, cw), bf16, None),
            ],
            flops=2 * half * width * (width + 4 * hid),
            moved=2 * half * width * 8 + 2 * width * 3 * hid,
            exps=half * hid,
            scratch=[weights(hid), weights(hid), weights(cw), weights(cw), weights(cw)],
            vmem=40,
        )

    a2, act, dpre, dsend, dkeep, ysend, ykeep, rkeep, nacc, wp_own = zip(
        *[mlp(part) for part in range(2)]
    )

    grads_r, grads_b = [], []
    for part in range(2):
        mine = (dkeep[part] + swap_core(dsend[part]).astype(f32)).astype(bf16)
        other = swap_x(mine)
        dr, ab = call(
            norm_two_kernel,
            f"norm_two{part}",
            (1,),
            (info,),
            [
                (rkeep[part], None),
                (mine, None),
                (other, None),
                (grad_out, pl.BlockSpec((RB, width), lambda i, s, part=part: (2 * part + s[0], 0))),
                (norms, None),
            ],
            [((RB, width), f32, None), ((RB, width), bf16, None)],
            flops=0,
            moved=RB * width * 16,
        )
        grads_r.append(dr)
        grads_b.append((ab, swap_core(ab)))

    turn = lambda: pl.BlockSpec((half, RB), lambda j: (0, j))
    down_half = lambda part: pl.BlockSpec((half, RB), lambda j: (part, j))
    (mlp_grad,) = call(
        mlp_grad_kernel,
        "mlp_grad",
        (width // RB,),
        (),
        [(a2[0], turn()), (a2[1], turn()), (dpre[0], None), (dpre[1], None)]
        + [(grad_out, down_half(0)), (grad_out, down_half(1)), (act[0], None), (act[1], None)],
        [((width, 2 * hid), bf16, pl.BlockSpec((RB, 2 * hid), lambda j: (j, 0)))],
        flops=4 * count * width * hid,
        moved=2 * (4 * count * width + 2 * width * hid),
    )
    mlp_shard = scatter_ring(mlp_grad, info)

    low = lax.axis_index("mp") < 2

    def to_rows(keep, received):
        sums = [k + r.astype(f32) for k, r in zip(keep, received)]
        mine = jnp.where(low, sums[0], sums[1])
        sent = jnp.where(low, sums[1], sums[0]).astype(bf16)
        return mine, swap_x(sent)

    mine, received = to_rows(ykeep, [swap_core(y) for y in ysend])
    block_out = (jnp.where(low, rkeep[0], rkeep[1]) + mine + received.astype(f32)).astype(bf16)

    def attend_back(part, before):
        keys = (part + 1) * half
        top = lambda w: pl.BlockSpec((keys, w), lambda i, *_: (0, 0))
        outs = [((half, width), bf16, None)]
        if part:
            outs += [((count, wide), bf16, None), ((count, cw), bf16, None)]
        else:
            outs += [((half, cw), f32, None)] * 3
        return call(
            functools.partial(attend_back_kernel, heads, part * half, bool(part)),
            f"attend_back{part}",
            (1,),
            (info, src),
            [(mixed, top(cols)), (values, top(cw)), (grads_b[part][0], None), (grads_b[part][1], None)]
            + [(wp_own[0], None), (lse[part], None)]
            + [(v, None) for v in before],
            outs,
            flops=10 * half * keys * 256 * heads,
            moved=2 * keys * (cols + cw) * 3,
            exps=half * keys * heads,
        )

    ab_one, dq, dk, dv = attend_back(0, [])
    ab_two, dmixed, dreused = attend_back(1, [dq, dk, dv])

    order = lambda i, s: 2 * (i % 2) + ((1 - s[0]) ^ (i // 2))
    spread = lambda w: pl.BlockSpec((RB, w), lambda i, s: (order(i, s), 0))
    isend, ikeep, norm_grad = call(
        input_kernel,
        "input",
        (4,),
        (info,),
        [(dmixed, spread(wide)), (qkv_full, None), (tokens_in, spread(width)), (nacc[0], None), (nacc[1], None)],
        [
            ((half, width), bf16, pl.BlockSpec((RB, width), lambda i, s: (jnp.minimum(i, 1), 0))),
            ((half, width), f32, pl.BlockSpec((RB, width), lambda i, s: (jnp.maximum(i - 2, 0), 0))),
            ((8, width), f32, None),
        ],
        flops=2 * count * width * wide,
        moved=2 * count * (wide + 3 * width),
    )
    (qkv_grad,) = call(
        functools.partial(qkv_grad_kernel, cols),
        "qkv_grad",
        (width // RB,),
        (),
        [
            (a1, pl.BlockSpec((count, RB), lambda j: (0, j))),
            (dmixed, None),
            (ab_one, turn()),
            (ab_two, turn()),
            (context[0], None),
            (context[1], None),
            (norm_grad, pl.BlockSpec((8, RB), lambda j: (0, j))),
        ],
        [((width, wide + cw), bf16, pl.BlockSpec((RB, wide + cw), lambda j: (j, 0)))],
        flops=2 * count * width * (wide + cw),
        moved=2 * count * (2 * width + wide + cw),
    )
    qkv_shard = scatter_ring(qkv_grad, info)
    theirs = swap_core(isend)
    mine, received = to_rows((ikeep[:RB], ikeep[RB:]), (theirs[:RB], theirs[RB:]))
    (input_grad,) = call(
        norm_one_kernel,
        "norm_one",
        (1,),
        (info,),
        [
            (tokens_in, pl.BlockSpec((RB, width), lambda i, s: (s[2], 0))),
            (mine, None),
            (received, None),
            (grads_r[0], None),
            (grads_r[1], None),
            (norms, None),
        ],
        [((RB, width), f32, None)],
        flops=0,
        moved=RB * width * 20,
    )
    (first_grad,) = call(
        functools.partial(first_kernel, heads),
        "first",
        (count // RB,),
        (info, src),
        [(d, row(cw)) for d in gather_four(dreused)],
        [((count, cw), f32, row(cw))],
        flops=8 * count * cw * cw,
        moved=count * cw * 12,
    )

    norm_part = qkv_shard[:, cols : cols + 4].T
    norm_part = norm_part + swap_core(norm_part)
    norm_part = norm_part + swap_x(norm_part)

    fc_new = adamw(fc_weight, fc_moment, fc_second, mlp_shard[:, :hid], 0.04, 0.1)
    down_new = adamw(down_weight, down_moment, down_second, mlp_shard[:, hid:].T, 0.03, 0.1)
    qkv_new = adamw(qkv_weight, qkv_moment, qkv_second, qkv_shard[:, :cols], 0.06, 0.1)
    proj_new = adamw(proj_weight, proj_moment, proj_second, qkv_shard[:, wide:].T, 0.15, 0.1)
    norm_new = adamw(norm_params, norm_moment, norm_second, norm_part, 0.3, 0.0)
    return (block_out, input_grad, first_grad) + qkv_new + proj_new + fc_new + down_new + norm_new


def solution(mesh):
    both = P("dp", "mp")
    turned = P("mp", "dp")
    rows = P("dp", None)
    every = P(None, "dp")
    state = (both, turned, both, turned, every)
    return jax.shard_map(
        local,
        mesh=mesh,
        in_specs=(rows, both, P(), rows) + state * 3,
        out_specs=(P(("dp", "mp"), None), P(("dp", "mp"), None), both)
        + (both,) * 3
        + (turned,) * 3
        + (both,) * 3
        + (turned,) * 3
        + (every,) * 3,
        check_vma=False,
    )
```

```python
import functools

import jax
import jax.numpy as jnp
import numpy as np
from jax import lax
from jax.experimental import pallas as pl
from jax.experimental.pallas import tpu as pltpu
from jax.sharding import PartitionSpec as P

H = 12
HD = 64
ADAM_STEP = 5
EPS = 1e-05
MASKED = -1e30
RB = 256
LANES = 128
RING = (0, 2, 4, 6, 7, 5, 3, 1)
OFFSETS = (0, -1, -2, -3, -4, 1, 2, 3)
GELU_A = 0.7978845608028654
GELU_B = 0.044715
RATES = {"qkv": 0.06, "proj": 0.15, "fc": 0.04, "down": 0.03, "norm": 0.3}

bf16 = jnp.bfloat16
f32 = jnp.float32


def dot(a, b):
    return jnp.dot(a, b, preferred_element_type=f32)


def dot_nt(a, b):
    return lax.dot_general(a, b, (((1,), (1,)), ((), ())), preferred_element_type=f32)


def dot_tn(a, b):
    return lax.dot_general(a, b, (((0,), (0,)), ((), ())), preferred_element_type=f32)


class Place:
    def __init__(self):
        self.mp, self.dp = lax.axis_index("mp"), lax.axis_index("dp")

    def __getitem__(self, k):
        if k < 4:
            return (self.mp % 2, self.mp // 2, self.mp, self.dp)[k]
        if lax.axis_size("dp") != len(RING):
            return 0
        z, y = self.dp // 2, self.dp % 2
        at = (jnp.where(y == 0, z, 7 - z) + OFFSETS[k - 4] + 8) % 8
        return jnp.where(at < 4, 2 * at, 2 * (7 - at) + 1)


HERE = object()


def call(kernel, name, scalars, ins, outs, scratch=(), vmem=16, far=False):
    if HERE in scalars:
        inner = kernel
        kernel = lambda *refs: inner(Place(), *refs)
        scalars = scalars[1:]
    smem = pl.BlockSpec(memory_space=pltpu.SMEM)
    full = pl.BlockSpec(memory_space=pltpu.VMEM)
    given = pl.BlockSpec(memory_space=pltpu.HBM) if far else full
    return pl.pallas_call(
        kernel,
        in_specs=[smem] * len(scalars) + [given] * len(ins),
        out_specs=[full] * len(outs),
        out_shape=[jax.ShapeDtypeStruct(sh, dt) for sh, dt in outs],
        scratch_shapes=list(scratch),
        compiler_params=pltpu.CompilerParams(vmem_limit_bytes=vmem * 1024 * 1024),
        cost_estimate=pl.CostEstimate(flops=1, bytes_accessed=1, transcendentals=0),
        name=name,
    )(*scalars, *ins)


def block(index, size=RB):
    return pl.ds(pl.multiple_of(index * size, size), size)


def fetch(pairs, sems):
    copies = [pltpu.make_async_copy(src, dst, sems.at[k]) for k, (src, dst) in enumerate(pairs)]
    for copy in copies:
        copy.start()
    for copy in copies:
        copy.wait()


def prep_one_kernel(q_ref, n_ref, out, q, norms, turn, sems):
    rows, cols = q.shape
    turn[...] = jnp.zeros(turn.shape, f32)
    fetch([(q_ref, q), (n_ref, norms)], sems)
    turn[: norms.shape[0], :rows] = norms[...]
    out[:, :cols] = q[...].astype(bf16)
    out[:, cols:] = turn[...].T[:rows, : out.shape[1] - cols].astype(bf16)


def prep_two_kernel(p_ref, f_ref, d_ref, proj, fc, down, p, f, d, turn, sems):
    rows = proj.shape[0]
    turn[...] = jnp.zeros(turn.shape, f32)
    fetch([(p_ref, p), (f_ref, f), (d_ref, d)], sems)
    turn[:, :rows] = p[...]
    proj[...] = turn[...].T[:rows].astype(bf16)
    fc[...] = f[...].astype(bf16)
    down[...] = d[...].astype(bf16)


def join_kernel(f_ref, own, across, out):
    hid, cw = f_ref.shape[1], own.shape[1]
    out[:, :hid] = f_ref[...]
    out[:, hid:] = jnp.concatenate([own[...], across[...]], 1)


def norm_stats(values):
    center = values - jnp.mean(values, axis=-1, keepdims=True)
    scale = lax.rsqrt(jnp.mean(center * center, axis=-1, keepdims=True) + EPS)
    return center * scale, scale


def unit_kernel(x_ref, unit_ref):
    for i in range(x_ref.shape[0] // RB):
        at = slice(i * RB, (i + 1) * RB)
        unit_ref[at] = norm_stats(x_ref[at].astype(f32))[0]


def loop(count, body):
    lax.fori_loop(0, count, lambda i, carry: (body(i), carry)[1], 0)


def qkv_kernel(n, heads, info, unit_ref, *refs):
    pieces, (a1_ref, m_ref, v_ref, w_ref, norm_ref) = refs[:n], refs[n:]
    cols = m_ref.shape[1]
    base = cols // LANES * LANES
    rows = w_ref.shape[0] // n
    for k, piece in enumerate(pieces):
        w_ref[block(info[4 + k], rows), :] = piece[...]
    turned = w_ref[:, base : base + LANES].astype(f32).T
    norm_ref[...] = turned[cols - base : cols - base + 8]

    def step(i):
        at = block(i)
        a1 = (unit_ref[at, :] * norm_ref[0:1] + norm_ref[1:2]).astype(bf16)
        a1_ref[at, :] = a1
        mixed = dot(a1, w_ref[:, :cols])
        m_ref[at, :] = mixed.astype(bf16)
        for h in range(heads):
            fresh = mixed[:, (3 * h + 2) * HD : (3 * h + 3) * HD]
            v_ref[h * HD : (h + 1) * HD, at] = fresh.T.astype(bf16)

    loop(m_ref.shape[0] // RB, step)


def values_kernel(heads, info, src, fresh, f0, f1, f2, f3, v_ref):
    mp = info[2]
    for h in range(heads):
        source = src[mp * heads + h]
        held = source // heads
        mine = slice(h * HD, (h + 1) * HD)

        @pl.when(source >= H)
        def _():
            v_ref[mine, :] = fresh[mine, :]

        for r, first in enumerate((f0, f1, f2, f3)):

            @pl.when((source < H) & (held == mp ^ r))
            def _():
                v_ref[mine, :] = first[block(source - held * heads, HD), :]


def masked_tile():
    keys = lax.broadcasted_iota(jnp.int32, (RB, RB), 0)
    queries = lax.broadcasted_iota(jnp.int32, (RB, RB), 1)
    return keys <= queries


def attend_kernel(heads, base, m_ref, v_ref, c_ref, lse_ref):
    keep = masked_tile()
    blocks = c_ref.shape[0] // RB
    turned = [[None] * heads for _ in range(blocks)]
    lse_ref[...] = jnp.zeros(lse_ref.shape, f32)
    for h in range(heads):
        top = base + blocks * RB
        keys = m_ref[:top, (3 * h + 1) * HD : (3 * h + 2) * HD]
        values_t = v_ref[h * HD : (h + 1) * HD, :top]
        for i in range(blocks):
            lo = base + i * RB
            hi = lo + RB
            query = m_ref[lo:hi, 3 * h * HD : (3 * h + 1) * HD] * bf16(HD**-0.5)
            diag = jnp.where(keep, dot_nt(keys[lo:hi], query), MASKED)
            peak = jnp.max(diag, 0, keepdims=True)
            if lo:
                left = dot_nt(keys[:lo], query)
                peak = jnp.maximum(peak, jnp.max(left, 0, keepdims=True))
            diag = jnp.exp(diag - peak)
            total = jnp.sum(diag, 0, keepdims=True)
            if lo:
                left = jnp.exp(left - peak)
                total += jnp.sum(left, 0, keepdims=True)
            inverse = 1.0 / total
            context = dot(values_t[:, lo:hi], (diag * inverse).astype(bf16))
            if lo:
                context += dot(values_t[:, :lo], (left * inverse).astype(bf16))
            turned[i][h] = context
            lse_ref[h : h + 1, i * RB : (i + 1) * RB] = peak + jnp.log(total)
    for i in range(blocks):
        c_ref[i * RB : (i + 1) * RB] = jnp.concatenate(turned[i], 0).T.astype(bf16)


def assemble_two_kernel(n, info, *refs):
    pieces, (wf, own, across, turn) = refs[:n], refs[n:]
    width, hid = wf.shape
    cw = own.shape[0]
    rows = width // n
    for k, piece in enumerate(pieces):
        at = block(info[4 + k], rows)
        wf[at, :] = piece[:, :hid]
        turn[at, :] = piece[:, hid:]
    pair = turn[...].T
    own[...] = pair[:cw]
    across[...] = pair[cw:]


def assemble_three_kernel(n, info, *refs):
    pieces, (wd,) = refs[:n], refs[n:]
    rows = wd.shape[0] // n
    for k, piece in enumerate(pieces):
        wd[block(info[4 + k], rows), :] = piece[...]


def mlp_kernel(part, x_ref, norm_ref, c0, c1, c2, c3, w0, w1, w2, w3, wf, r_ref, unit_ref, a2_ref, g_ref, slope_ref):
    def step(i):
        at = block(i)
        resid = x_ref[block(2 * part + i), :].astype(f32) + (
            (dot(c0[at, :], w0[...]) + dot(c1[at, :], w1[...]))
            + (dot(c2[at, :], w2[...]) + dot(c3[at, :], w3[...]))
        )
        r_ref[at, :] = resid
        unit, _ = norm_stats(resid)
        unit_ref[at, :] = unit
        a2 = (unit * norm_ref[2:3] + norm_ref[3:4]).astype(bf16)
        a2_ref[at, :] = a2
        u = dot(a2, wf[...])
        square = u * u
        t = jnp.tanh(GELU_A * u * (1.0 + GELU_B * square))
        g_ref[at, :] = (0.5 * u * (1.0 + t)).astype(bf16)
        slope_ref[at, :] = 0.5 * (1.0 + t) + 0.5 * u * (1.0 - t * t) * (
            GELU_A * (1.0 + 3.0 * GELU_B * square)
        )

    loop(2, step)


def mlp_back_kernel(part, info, e_ref, unit_ref, slope_ref, wf, wd, du_ref, top, bottom, keep, nacc):
    core = info[0]
    nacc[...] = jnp.zeros(nacc.shape, f32)

    def step(i):
        spot = jnp.where(i == 1, core, 1 - core)
        at = block(spot)
        du = (dot(e_ref[block(2 * part + spot), :], wd[...]) * slope_ref[at, :]).astype(bf16)
        du_ref[at, :] = du
        grad = dot_nt(du, wf[...])
        nacc[2:3] += jnp.sum(grad * unit_ref[at, :], 0, keepdims=True)
        nacc[3:4] += jnp.sum(grad, 0, keepdims=True)
        keep[...] = grad

        @pl.when(i == 0)
        def _():
            top[...] = grad[: RB // 2].astype(bf16)
            bottom[...] = grad[RB // 2 :].astype(bf16)

    loop(2, step)


def mlp_out_kernel(info, g_ref, wd, ysend, ykeep):
    ykeep[...] = dot_nt(g_ref[block(info[0]), :], wd[...])
    ysend[...] = dot_nt(g_ref[block(1 - info[0]), :], wd[...]).astype(bf16)


def add_kernel(keep, top, bottom, out):
    out[: RB // 2] = (keep[: RB // 2] + top[...].astype(f32)).astype(bf16)
    out[RB // 2 :] = (keep[RB // 2 :] + bottom[...].astype(f32)).astype(bf16)


def starts(info, full, fw, bw):
    rows = fw.shape[0]
    fw[...] = full[block(info[4 + OFFSETS.index(-4)], rows), :].astype(bf16)
    bw[...] = full[block(info[4 + OFFSETS.index(-3)], rows), :].astype(bf16)


def mlp_grad_kernel(info, a2a, a2b, dua, dub, e_ref, ga, gb, out, fw, bw):
    hid = dua.shape[1]
    half = dua.shape[0]

    def step(j):
        at = block(j)
        out[at, :hid] = (dot_tn(a2a[:, at], dua[...]) + dot_tn(a2b[:, at], dub[...])).astype(out.dtype)
        out[at, hid:] = (dot_tn(e_ref[:half, at], ga[...]) + dot_tn(e_ref[half:, at], gb[...])).astype(out.dtype)

    loop(out.shape[0] // RB, step)
    starts(info, out, fw, bw)


def hop_kernel(ahead, behind, info, full, a, b, a_out, b_out):
    rows = a.shape[0]
    for offset, value, out in ((ahead, a, a_out), (behind, b, b_out)):
        term = full[block(info[4 + OFFSETS.index(offset)], rows), :]
        out[...] = (value[...].astype(f32) + term.astype(f32)).astype(bf16)


def hop_last_kernel(info, full, a, a_out):
    term = full[block(info[4 + OFFSETS.index(1)], a.shape[0]), :]
    a_out[...] = (a[...].astype(f32) + term.astype(f32)).astype(bf16)


def norm_back(unit, scale, gain, grad):
    dy = grad * gain
    return scale * (
        dy - jnp.mean(dy, -1, keepdims=True) - unit * jnp.mean(dy * unit, -1, keepdims=True)
    )


def norm_two_kernel(part, info, r_ref, own, received, e_ref, norm_ref, dr_ref, top, bottom):
    unit, scale = norm_stats(r_ref[block(info[0]), :])
    grad = own[...].astype(f32) + received[...].astype(f32)
    e = e_ref[block(2 * part + info[0]), :].astype(f32)
    dr = e + norm_back(unit, scale, norm_ref[2:3], grad)
    dr_ref[...] = dr
    top[...] = dr[: RB // 2].astype(bf16)
    bottom[...] = dr[RB // 2 :].astype(bf16)


def attend_back_kernel(heads, base, last, info, src, m_ref, v_ref, o0, o1, p0, p1, wp, lse_ref, *refs):
    if last:
        dqa, dka, dva, ab_ref, dm_ref, dvr_ref = refs
    else:
        ab_ref, dq_ref, dk_ref, dv_ref = refs
    keep = masked_tile()
    core = info[0]
    rows = 2 * RB
    blocks = 2
    for k, (own, partner) in enumerate(((o0, p0), (o1, p1))):
        ab_ref[block(2 * core + k, RB // 2), :] = own[...]
        ab_ref[block(2 * (1 - core) + k, RB // 2), :] = partner[...]
    top = base + rows
    tiles = top // RB
    dctx = [dot_nt(ab_ref[i * RB : (i + 1) * RB], wp[...]).astype(bf16) for i in range(blocks)]
    dq_t = [[None] * heads for _ in range(blocks)]
    dks, dvs = [], []
    for h in range(heads):
        keys = m_ref[:top, (3 * h + 1) * HD : (3 * h + 2) * HD]
        keys_t = keys.T
        values = v_ref[h * HD : (h + 1) * HD, :top].T
        dk = [None] * tiles
        dv = [None] * tiles
        for i in range(blocks):
            lo = base + i * RB
            count = lo // RB + 1
            query = m_ref[lo : lo + RB, 3 * h * HD : (3 * h + 1) * HD] * bf16(HD**-0.5)
            dc = dctx[i][:, h * HD : (h + 1) * HD]
            lse = lse_ref[h : h + 1, i * RB : (i + 1) * RB]
            probs, dprobs = [], []
            inner = jnp.zeros((1, RB), f32)
            for t in range(count):
                spot = slice(t * RB, (t + 1) * RB)
                score = dot_nt(keys[spot], query)
                prob = jnp.exp(score - lse)
                if t == count - 1:
                    prob = jnp.where(keep, prob, 0.0)
                dprob = dot_nt(values[spot], dc)
                inner += jnp.sum(prob * dprob, 0, keepdims=True)
                more = dot(prob.astype(bf16), dc)
                dv[t] = more if dv[t] is None else dv[t] + more
                probs.append(prob)
                dprobs.append(dprob)
            total = None
            for t in range(count):
                spot = slice(t * RB, (t + 1) * RB)
                ds = (probs[t] * (dprobs[t] - inner)).astype(bf16)
                more = dot(ds, query)
                dk[t] = more if dk[t] is None else dk[t] + more
                more = dot(keys_t[:, spot], ds)
                total = more if total is None else total + more
            dq_t[i][h] = total * HD**-0.5
        dks.append(dk)
        dvs.append(dv)
    dq = [jnp.concatenate(dq_t[i], 0).T for i in range(blocks)]
    if not last:
        for i in range(blocks):
            dq_ref[i * RB : (i + 1) * RB] = dq[i]
        for t in range(tiles):
            dk_ref[t * RB : (t + 1) * RB] = jnp.concatenate([dks[h][t] for h in range(heads)], 1)
            dv_ref[t * RB : (t + 1) * RB] = jnp.concatenate([dvs[h][t] for h in range(heads)], 1)
        return
    mp = info[2]
    fresh = [jnp.where(src[mp * heads + h] < H, 0.0, 1.0) for h in range(heads)]
    for t in range(tiles):
        spot = slice(t * RB, (t + 1) * RB)
        first = t * RB < base
        parts = []
        for h in range(heads):
            lane = slice(h * HD, (h + 1) * HD)
            dqh = dqa[spot, lane] if first else dq[t - base // RB][:, lane]
            dkh = dks[h][t] + dka[spot, lane] if first else dks[h][t]
            dvh = dvs[h][t] + dva[spot, lane] if first else dvs[h][t]
            parts += [dqh, dkh, dvh * fresh[h]]
            dvr_ref[h * HD : (h + 1) * HD, spot] = dvh.T.astype(bf16)
        dm_ref[spot, :] = jnp.concatenate(parts, 1).astype(bf16)


def input_kernel(info, dm_ref, w_ref, unit_ref, na, nb, send, keep):
    core = info[0]
    cols = dm_ref.shape[1]
    sums = na[...] + nb[...]
    keep[2 * RB :] = jnp.concatenate([sums, jnp.zeros(sums.shape, f32)], 0)

    def step(i):
        half = i % 2
        spot = jnp.where(i < 2, 1 - core, core)
        at = block(2 * half + spot)
        grad = dot_nt(dm_ref[at, :], w_ref[:, :cols])
        keep[2 * RB : 2 * RB + 1] += jnp.sum(grad * unit_ref[at, :], 0, keepdims=True)
        keep[2 * RB + 1 : 2 * RB + 2] += jnp.sum(grad, 0, keepdims=True)
        keep[block(half), :] = grad

        @pl.when(i < 2)
        def _():
            send[block(half), :] = grad.astype(bf16)

    loop(4, step)
    send[2 * RB :] = keep[2 * RB :].astype(bf16)


def to_rows_kernel(info, keep, received, mine, sent):
    own = info[1]
    for out, half in ((mine, own), (sent, 1 - own)):
        at = block(half)
        out[:RB] = (keep[at, :] + received[at, :].astype(f32)).astype(out.dtype)
        if out.shape[0] > RB:
            out[RB:] = (keep[2 * RB :] + received[2 * RB :].astype(f32)).astype(out.dtype)


def output_rows_kernel(info, ka, kb, ra, rb, mine, sent):
    low = info[1] == 0
    first = ka[...] + ra[...].astype(f32)
    second = kb[...] + rb[...].astype(f32)
    mine[...] = jnp.where(low, first, second)
    sent[...] = jnp.where(low, second, first).astype(bf16)


def output_kernel(info, ra, rb, mine, received, out):
    at = block(info[0])
    resid = jnp.where(info[1] == 0, ra[at, :], rb[at, :])
    out[...] = (resid + mine[...] + received[...].astype(f32)).astype(bf16)


def qkv_grad_kernel(info, a1_ref, dm_ref, aba, abb, ca, cb, out, fw, bw):
    def step(j):
        at = block(j)
        grad = dot_tn(a1_ref[:, at], dm_ref[...])
        proj = dot_tn(aba[:, at], ca[...]) + dot_tn(abb[:, at], cb[...])
        out[at, :] = jnp.concatenate([grad, proj], 1).astype(out.dtype)

    loop(out.shape[0] // RB, step)
    starts(info, out, fw, bw)


def norm_one_kernel(info, x_ref, own, received, dra, drb, norm_ref, out, sums):
    unit, scale = norm_stats(x_ref[block(info[2]), :].astype(f32))
    grad = own[:RB] + received[:RB].astype(f32)
    dr = jnp.where(info[1] == 0, dra[...], drb[...])
    out[...] = dr + norm_back(unit, scale, norm_ref[0:1], grad)
    total = own[RB:] + received[RB:].astype(f32)
    sums[...] = total[:8]


def first_kernel(heads, info, src, d0, d1, d2, d3, out):
    mp = info[2]
    out[...] = jnp.zeros(out.shape, f32)
    for g in range(heads):
        user = jnp.int32(H)
        for h in range(H):
            user = jnp.where(src[h] == mp * heads + g, h, user)
        held = user // heads
        for r, ref in enumerate((d0, d1, d2, d3)):

            @pl.when((user < H) & (held == mp ^ r))
            def _():
                out[g * HD : (g + 1) * HD, :] = ref[block(user - held * heads, HD), :].astype(f32)


def adamw(master, moment, second, grad, rate, weighted):
    moment_new = 0.9 * moment + 0.1 * grad
    second_new = 0.999 * second + 0.001 * grad * grad
    mean_hat = moment_new / (1.0 - 0.9**ADAM_STEP)
    var_hat = second_new / (1.0 - 0.999**ADAM_STEP)
    master_new = master - rate * (mean_hat / (jnp.sqrt(var_hat) + 1e-08) + weighted * master)
    return (master_new, moment_new, second_new)


def adam_kernel(names, turned, info, full, a, b, *refs):
    ins, outs = refs[:6], refs[6:12]
    rows = a.shape[0]
    grad = a[...].astype(f32) + b[...].astype(f32)
    grad += full[block(info[4], rows), :].astype(f32)
    cols = ins[0].shape[1]
    second = grad[:, cols:]
    if turned:
        second = jnp.concatenate([second, jnp.zeros((LANES - rows, second.shape[1]), f32)], 0).T[:, :rows]
    for k, (name, part) in enumerate(zip(names, (grad[:, :cols], second))):
        new = adamw(*[r[...] for r in ins[3 * k : 3 * k + 3]], part, RATES[name], 0.1)
        for ref, value in zip(outs[3 * k : 3 * k + 3], new):
            ref[...] = value


def norm_adam_kernel(info, sums, received, w, m, s, w_out, m_out, s_out):
    total = sums[...] + received[...]
    cols = w.shape[1]
    shift = total.shape[1] - info[3] * cols
    grad = pltpu.roll(total, shift, 1)[:4, :cols]
    new = adamw(w[...], m[...], s[...], grad, RATES["norm"], 0.0)
    for ref, value in zip((w_out, m_out, s_out), new):
        ref[...] = value


def sum_kernel(a, b, out):
    out[...] = a[...] + b[...]


def swap_core(value):
    return lax.ppermute(value, "mp", [(i, i ^ 1) for i in range(4)])


def swap_x(value):
    return lax.ppermute(value, "mp", [(i, i ^ 2) for i in range(4)])


FORWARD = [(RING[i], RING[(i + 1) % 8]) for i in range(8)]
BACKWARD = [(b, a) for a, b in FORWARD]


def ahead(value):
    return lax.ppermute(value, "dp", FORWARD)


def behind(value):
    return lax.ppermute(value, "dp", BACKWARD)


def after(value, *others):
    return lax.optimization_barrier((value,) + others)[0]


class Gather:
    def __init__(self, piece):
        self.ring = lax.axis_size("dp") == len(RING)
        self.start = self.a = self.b = piece
        self.ahead, self.behind = [], []

    def step(self, *gates):
        if not self.ring:
            return
        self.a, self.b = lax.optimization_barrier((self.a, self.b) + gates)[:2]
        self.a = ahead(self.a)
        self.ahead.append(self.a)
        if len(self.behind) < 3:
            self.b = behind(self.b)
            self.behind.append(self.b)

    def pieces(self):
        if not self.ring:
            return [lax.all_gather(self.start, "dp", axis=0, tiled=True)]
        return [self.start] + self.ahead + self.behind


class Scatter:
    def __init__(self, name, info, full, fw, bw):
        self.ring = lax.axis_size("dp") == len(RING)
        self.name, self.info, self.full, self.a, self.b = name, info, full, fw, bw
        self.steps = 0

    def step(self, *gates):
        if not self.ring:
            return
        self.a = after(self.a, *gates)
        k = 4 - self.steps
        shape = (self.a.shape, bf16)
        if k in (3, 2):
            kernel = functools.partial(hop_kernel, k, 1 - k)
            self.a, self.b = call(kernel, f"{self.name}_hop{k}", (self.info,), [self.full, self.a, self.b], [shape] * 2)
        if k == 1:
            (self.a,) = call(hop_last_kernel, f"{self.name}_hop1", (self.info,), [self.full, self.a], [shape])
        self.last = self.a
        self.a = ahead(self.a)
        if k > 1:
            self.b = behind(self.b)
        self.steps += 1

    def ends(self):
        return (self.a, self.b) if self.ring else None


def update(name, info, full, ends, firsts, seconds, turned):
    first, second = name
    outs = [(w.shape, f32) for w in firsts + seconds]
    if ends is not None:
        new = call(
            functools.partial(adam_kernel, name, turned),
            f"adam_{first}",
            (info,),
            [full, *ends, *firsts, *seconds],
            outs,
        )
        return tuple(new[:3]), tuple(new[3:])
    grad = lax.psum_scatter(full.astype(f32), "dp", scatter_dimension=0, tiled=True)
    cols = firsts[0].shape[1]
    other = grad[:, cols:]
    return (
        adamw(*firsts, grad[:, :cols], RATES[first], 0.1),
        adamw(*seconds, other.T if turned else other, RATES[second], 0.1),
    )


def local(
    tokens_in,
    first_values,
    skip_source,
    grad_out,
    qkv_weight,
    proj_weight,
    fc_weight,
    down_weight,
    norm_params,
    qkv_moment,
    proj_moment,
    fc_moment,
    down_moment,
    norm_moment,
    qkv_second,
    proj_second,
    fc_second,
    down_second,
    norm_second,
):
    n = lax.axis_size("dp")
    ring = n == len(RING)
    pieces = n if ring else 1
    count, width = tokens_in.shape
    cols = qkv_weight.shape[1]
    heads = cols // (3 * HD)
    cw = heads * HD
    hid = fc_weight.shape[1]
    wide = -(-(cols + 4) // LANES) * LANES
    half = count // 2
    shard = qkv_weight.shape[0]
    info = HERE
    src = skip_source

    if ring:
        (ring_one,) = call(
            prep_one_kernel,
            "prep_one",
            (),
            [qkv_weight, norm_params],
            [((shard, wide), bf16)],
            scratch=[
                pltpu.VMEM((shard, cols), f32),
                pltpu.VMEM(norm_params.shape, f32),
                pltpu.VMEM((LANES, LANES), f32),
                pltpu.SemaphoreType.DMA((2,)),
            ],
            far=True,
        )
        proj_t, fc_low, down_t = call(
            prep_two_kernel,
            "prep_two",
            (),
            [after(proj_weight, ring_one), fc_weight, down_weight.T],
            [((shard, cw), bf16), ((shard, hid), bf16), ((shard, hid), bf16)],
            scratch=[
                pltpu.VMEM((cw, shard), f32),
                pltpu.VMEM((shard, hid), f32),
                pltpu.VMEM((shard, hid), f32),
                pltpu.VMEM((cw, LANES), f32),
                pltpu.SemaphoreType.DMA((3,)),
            ],
            far=True,
        )
    else:
        blank = jnp.zeros((shard, wide - cols - 4), bf16)
        ring_one = jnp.concatenate([qkv_weight.astype(bf16), norm_params.T.astype(bf16), blank], 1)
        proj_t, fc_low, down_t = proj_weight.T.astype(bf16), fc_weight.astype(bf16), down_weight.T.astype(bf16)
    fence = lambda *values: lax.optimization_barrier(values)
    fence = lambda *values: lax.optimization_barrier(values)
    one = Gather(ring_one)
    one.step()
    one.a, one.b, proj_t, tokens = fence(one.a, one.b, proj_t, tokens_in)
    one.step()
    proj_x = swap_x(proj_t)
    (unit_one,) = call(unit_kernel, "unit", (), [tokens], [((count, width), f32)])
    one.a, one.b, proj_x, unit_one = fence(one.a, one.b, proj_x, unit_one)
    one.step()
    if ring:
        (ring_two,) = call(
            join_kernel, "join", (), [fc_low, proj_t, proj_x], [((shard, hid + 2 * cw), bf16)]
        )
    else:
        ring_two = jnp.concatenate([fc_low, proj_t, proj_x], 1)
    two, three = Gather(ring_two), Gather(down_t)
    two.step()
    first_t = first_values.T
    first_x, first_c = swap_x(first_t), swap_core(first_t)
    one.a, one.b = fence(one.a, one.b)
    one.step()
    one.a, two.a, two.b, unit_one, first_x, three.a = fence(one.a, two.a, two.b, unit_one, first_x, three.a)
    if ring:
        one.ahead[-1] = one.a
    first_xc = swap_core(first_x)
    two.step()
    three.step()

    a1, mixed, fresh, qkv_full, norms = call(
        functools.partial(qkv_kernel, pieces, heads),
        "qkv",
        (info,),
        [unit_one, *one.pieces()],
        [
            ((count, width), bf16),
            ((count, cols), bf16),
            ((cw, count), bf16),
            ((width, wide), bf16),
            ((8, width), f32),
        ],
    )
    (values,) = call(
        functools.partial(values_kernel, heads),
        "values",
        (info, src),
        [fresh, first_t, first_c, first_x, first_xc],
        [((cw, count), bf16)],
    )

    def attend(part, mixed):
        return call(
            functools.partial(attend_kernel, heads, part * half),
            f"attend{part}",
            (),
            [mixed, values],
            [((half, cw), bf16), ((8, half), f32)],
        )

    ctx_a, lse_a = attend(0, mixed)
    xa, ca = swap_x(ctx_a), swap_core(ctx_a)
    ctx_b, lse_b = attend(1, after(mixed, ctx_a))
    xb, cb = swap_x(ctx_b), swap_core(ctx_b)
    xca, xcb = swap_core(xa), swap_core(xb)
    two.step()
    three.step()
    two.step()
    three.step()
    start, xca, xcb, two_last, three.a, three.b = fence(two.start, xca, xcb, two.a, three.a, three.b)
    three.step()
    context, lse = (ctx_a, ctx_b), (lse_a, lse_b)
    wf, own_w, across_w = call(
        functools.partial(assemble_two_kernel, pieces),
        "assemble_two",
        (info,),
        [start, *two.pieces()[1:]] if ring else two.pieces(),
        [((width, hid), bf16), ((cw, width), bf16), ((cw, width), bf16)],
        scratch=[pltpu.VMEM((width, 2 * cw), bf16)],
    )
    pair = own_w, swap_core(own_w), across_w, swap_core(across_w)

    def mlp(part, norms, contexts):
        return call(
            functools.partial(mlp_kernel, part),
            f"mlp{part}",
            (),
            [tokens, norms, *contexts, *pair, wf],
            [
                ((half, width), f32),
                ((half, width), f32),
                ((half, width), bf16),
                ((half, hid), bf16),
                ((half, hid), f32),
            ],
        )

    def mlp_back(part, grad):
        return call(
            functools.partial(mlp_back_kernel, part),
            f"mlp_back{part}",
            (info,),
            [grad, unit_two[part], slope[part], wf, wd],
            [((half, hid), bf16)] + [((RB // 2, width), bf16)] * 2 + [((RB, width), f32), ((8, width), f32)],
        )

    def mlp_out(part, gate):
        return call(
            mlp_out_kernel,
            f"mlp_out{part}",
            (info,),
            [after(act[part], gate), wd],
            [((RB, width), bf16), ((RB, width), f32)],
        )

    def add(part, keep, *received):
        return call(add_kernel, f"add{part}", (), [keep, *received], [((RB, width), bf16)])[0]

    forward_a = mlp(0, norms, (ctx_a, ca, xa, xca))
    forward_b = mlp(1, after(norms, forward_a[0]), (ctx_b, cb, xb, xcb))
    resid, unit_two, a2, act, slope = zip(forward_a, forward_b)
    start, last = fence(three.start, act[1])
    (wd,) = call(
        functools.partial(assemble_three_kernel, pieces),
        "assemble_three",
        (info,),
        [start, *three.pieces()[1:]] if ring else three.pieces(),
        [((width, hid), bf16)],
    )
    dpre_a, top_a, bottom_a, dkeep_a, nacc_a = mlp_back(0, after(grad_out, act[1]))
    received_a = swap_core(top_a), swap_core(bottom_a)
    dpre_b, top_b, bottom_b, dkeep_b, nacc_b = mlp_back(1, after(grad_out, dpre_a))
    mine_a = add(0, after(dkeep_a, dpre_b), *received_a)
    received_b = swap_core(top_b), swap_core(bottom_b)
    across_a = swap_x(mine_a)

    piece = lambda w: [((width // pieces if ring else 16, w), bf16)] * 2
    mlp_grad, mlp_fw, mlp_bw = call(
        mlp_grad_kernel,
        "mlp_grad",
        (info,),
        [after(a2[0], mine_a), a2[1], dpre_a, dpre_b, grad_out, act[0], act[1]],
        [((width, 2 * hid), bf16 if ring else f32)] + piece(2 * hid),
    )
    mlp_sum = Scatter("mlp", info, mlp_grad, mlp_fw, mlp_bw)
    mlp_sum.step()
    mine_b = add(1, after(dkeep_b, mlp_grad), *received_b)
    ysend_a, ykeep_a = mlp_out(0, mine_b)
    ysend_b, ykeep_b = mlp_out(1, ysend_a)
    yreceived_a, yreceived_b = swap_core(ysend_a), swap_core(ysend_b)
    across_a, mine_b, ykeep_b = fence(across_a, mine_b, ykeep_b)
    across_b = swap_x(mine_b)

    def norm_two(part, mine, across):
        return call(
            functools.partial(norm_two_kernel, part),
            f"norm_two{part}",
            (info,),
            [resid[part], mine, across, grad_out, norms],
            [((RB, width), f32)] + [((RB // 2, width), bf16)] * 2,
        )

    def attend_back(part, own, partner, before):
        outs = [((half, width), bf16)]
        if part:
            outs += [((count, cols), bf16), ((cw, count), bf16)]
        else:
            outs += [((half, cw), f32)] * 3
        return call(
            functools.partial(attend_back_kernel, heads, part * half, bool(part)),
            f"attend_back{part}",
            (info, src),
            [mixed, values, *own, *partner, own_w, lse[part], *before],
            outs,
            vmem=24,
        )

    dr_a, *ab_a = norm_two(0, after(mine_a, mine_b), across_a)

    rows_mine, rows_sent = call(
        output_rows_kernel,
        "output_rows",
        (info,),
        [after(ykeep_a, dr_a), ykeep_b, yreceived_a, yreceived_b],
        [((RB, width), f32), ((RB, width), bf16)],
    )
    partner = [swap_core(v) for v in ab_a]
    mlp_sum.a, mlp_sum.b, rows_sent, *partner = fence(mlp_sum.a, mlp_sum.b, rows_sent, *partner)
    ab_one, dq, dk, dv = attend_back(0, ab_a, partner, [])
    mlp_sum.step()
    dr_b, *ab_b = norm_two(1, after(mine_b, dq), across_b)
    rows_received = swap_x(after(rows_sent, dr_b))
    ab_two, dmixed, dreused = attend_back(1, ab_b, [swap_core(v) for v in ab_b], [dq, dk, dv])
    mlp_sum.a, mlp_sum.b, dmixed, rows_received = fence(mlp_sum.a, mlp_sum.b, dmixed, rows_received)
    mlp_sum.step()

    qkv_grad, qkv_fw, qkv_bw = call(
        qkv_grad_kernel,
        "qkv_grad",
        (info,),
        [a1, after(dmixed, mlp_sum.last) if ring else dmixed, ab_one, ab_two, context[0], context[1]],
        [((width, cols + cw), bf16 if ring else f32)] + piece(cols + cw),
    )
    qkv_sum = Scatter("qkv", info, qkv_grad, qkv_fw, qkv_bw)
    qkv_sum.step()
    isend, ikeep = call(
        input_kernel,
        "input",
        (info,),
        [after(dmixed, qkv_fw), qkv_full, unit_one, nacc_a, nacc_b],
        [((half + 16, width), bf16), ((half + 16, width), f32)],
    )
    mine, sent = call(
        to_rows_kernel,
        "to_rows",
        (info,),
        [ikeep, swap_core(isend)],
        [((RB + 16, width), f32), ((RB + 16, width), bf16)],
    )
    across = swap_x(sent)
    mlp_sum.a, mlp_sum.b, qkv_sum.a, qkv_sum.b = fence(mlp_sum.a, mlp_sum.b, qkv_sum.a, qkv_sum.b)
    qkv_sum.step()
    mlp_sum.step()
    qkv_sum.a, qkv_sum.b = fence(qkv_sum.a, qkv_sum.b)
    qkv_sum.step()
    dx, dc = swap_x(dreused), swap_core(dreused)
    qkv_sum.a, qkv_sum.b, across = fence(qkv_sum.a, qkv_sum.b, across)
    qkv_sum.step()
    input_grad, sums = call(
        norm_one_kernel,
        "norm_one",
        (info,),
        [tokens, mine, across, dr_a, dr_b, norms],
        [((RB, width), f32), ((8, width), f32)],
    )
    (block_out,) = call(
        output_kernel,
        "output",
        (info,),
        [resid[0], resid[1], after(rows_mine, input_grad), rows_received],
        [((RB, width), bf16)],
    )
    dxc = swap_core(dx)
    mlp_ends = mlp_sum.ends()
    if ring:
        hop = lambda value, bit: lax.ppermute(value, "dp", [(i, i ^ bit) for i in range(n)])
        for bit in (1, 2):
            (sums,) = call(sum_kernel, f"sum{bit}", (), [sums, hop(sums, bit)], [(sums.shape, f32)])
        received = hop(sums, 4)
    fc_new, down_new = update(
        ("fc", "down"),
        info,
        mlp_grad,
        mlp_ends,
        [fc_weight, fc_moment, fc_second],
        [down_weight.T, down_moment.T, down_second.T],
        False,
    )
    down_new = tuple(v.T for v in down_new)
    (first_grad,) = call(
        functools.partial(first_kernel, heads),
        "first",
        (info, src),
        [dreused, dc, dx, dxc],
        [((cw, count), f32)],
    )
    qkv_new, proj_new = update(
        ("qkv", "proj"),
        info,
        qkv_grad,
        qkv_sum.ends(),
        [after(qkv_weight, first_grad), qkv_moment, qkv_second],
        [proj_weight, proj_moment, proj_second],
        True,
    )
    if ring:
        norm_new = call(
            norm_adam_kernel,
            "adam_norm",
            (info,),
            [sums, received, norm_params, norm_moment, norm_second],
            [(norm_params.shape, f32)] * 3,
        )
    else:
        own = lax.psum_scatter(sums, "dp", scatter_dimension=1, tiled=True)[:4]
        norm_new = adamw(norm_params, norm_moment, norm_second, own, RATES["norm"], 0.0)
    return (block_out, input_grad, first_grad.T, *qkv_new, *proj_new, *fc_new, *down_new, *norm_new)


def solution(mesh):
    both = P("dp", "mp")
    turned = P("mp", "dp")
    rows = P("dp", None)
    every = P(None, "dp")
    state = (both, turned, both, turned, every)
    return jax.shard_map(
        local,
        mesh=mesh,
        in_specs=(rows, both, P(), rows) + state * 3,
        out_specs=(P(("dp", "mp"), None), P(("dp", "mp"), None), both)
        + (both,) * 3
        + (turned,) * 3
        + (both,) * 3
        + (turned,) * 3
        + (every,) * 3,
        check_vma=False,
    )
```

```python
import functools

import jax
import jax.numpy as jnp
import numpy as np
from jax import lax
from jax.experimental import pallas as pl
from jax.experimental.pallas import tpu as pltpu
from jax.sharding import PartitionSpec as P

H = 12
HD = 64
ADAM_STEP = 5
EPS = 1e-05
MASKED = -1e30
RB = 256
LANES = 128
RING = (0, 2, 4, 6, 7, 5, 3, 1)
OFFSETS = (0, -1, -2, -3, -4, 1, 2, 3)
GELU_A = 0.7978845608028654
GELU_B = 0.044715
RATES = {"qkv": 0.06, "proj": 0.15, "fc": 0.04, "down": 0.03, "norm": 0.3}

bf16 = jnp.bfloat16
f32 = jnp.float32


def dot(a, b):
    return jnp.dot(a, b, preferred_element_type=f32)


def dot_nt(a, b):
    return lax.dot_general(a, b, (((1,), (1,)), ((), ())), preferred_element_type=f32)


def dot_tn(a, b):
    return lax.dot_general(a, b, (((0,), (0,)), ((), ())), preferred_element_type=f32)


class Place:
    def __init__(self):
        self.mp, self.dp = lax.axis_index("mp"), lax.axis_index("dp")

    def __getitem__(self, k):
        if k < 4:
            return (self.mp % 2, self.mp // 2, self.mp, self.dp)[k]
        if lax.axis_size("dp") != len(RING):
            return 0
        z, y = self.dp // 2, self.dp % 2
        at = (jnp.where(y == 0, z, 7 - z) + OFFSETS[k - 4] + 8) % 8
        return jnp.where(at < 4, 2 * at, 2 * (7 - at) + 1)


HERE = object()


def call(kernel, name, scalars, ins, outs, scratch=(), vmem=16, far=False):
    if HERE in scalars:
        inner = kernel
        kernel = lambda *refs: inner(Place(), *refs)
        scalars = scalars[1:]
    smem = pl.BlockSpec(memory_space=pltpu.SMEM)
    full = pl.BlockSpec(memory_space=pltpu.VMEM)
    given = pl.BlockSpec(memory_space=pltpu.HBM) if far else full
    return pl.pallas_call(
        kernel,
        in_specs=[smem] * len(scalars) + [given] * len(ins),
        out_specs=[full] * len(outs),
        out_shape=[jax.ShapeDtypeStruct(sh, dt) for sh, dt in outs],
        scratch_shapes=list(scratch),
        compiler_params=pltpu.CompilerParams(vmem_limit_bytes=vmem * 1024 * 1024),
        cost_estimate=pl.CostEstimate(flops=1, bytes_accessed=1, transcendentals=0),
        name=name,
    )(*scalars, *ins)


def block(index, size=RB):
    return pl.ds(pl.multiple_of(index * size, size), size)


def fetch(pairs, sems):
    copies = [pltpu.make_async_copy(src, dst, sems.at[k]) for k, (src, dst) in enumerate(pairs)]
    for copy in copies:
        copy.start()
    for copy in copies:
        copy.wait()


def prep_one_kernel(q_ref, n_ref, out, q, norms, turn, sems):
    rows, cols = q.shape
    turn[...] = jnp.zeros(turn.shape, f32)
    fetch([(q_ref, q), (n_ref, norms)], sems)
    turn[: norms.shape[0], :rows] = norms[...]
    out[:, :cols] = q[...].astype(bf16)
    out[:, cols:] = turn[...].T[:rows, : out.shape[1] - cols].astype(bf16)


def prep_two_kernel(p_ref, f_ref, d_ref, proj, fc, down, p, f, d, turn, sems):
    rows = proj.shape[0]
    turn[...] = jnp.zeros(turn.shape, f32)
    fetch([(p_ref, p), (f_ref, f), (d_ref, d)], sems)
    turn[:, :rows] = p[...]
    proj[...] = turn[...].T[:rows].astype(bf16)
    fc[...] = f[...].astype(bf16)
    down[...] = d[...].astype(bf16)


def join_kernel(f_ref, own, across, out):
    hid, cw = f_ref.shape[1], own.shape[1]
    out[:, :hid] = f_ref[...]
    out[:, hid:] = jnp.concatenate([own[...], across[...]], 1)


def norm_stats(values):
    center = values - jnp.mean(values, axis=-1, keepdims=True)
    scale = lax.rsqrt(jnp.mean(center * center, axis=-1, keepdims=True) + EPS)
    return center * scale, scale


def unit_kernel(x_ref, unit_ref):
    for i in range(x_ref.shape[0] // RB):
        at = slice(i * RB, (i + 1) * RB)
        unit_ref[at] = norm_stats(x_ref[at].astype(f32))[0]


def fetch_kernel(src, out, sem):
    copy = pltpu.make_async_copy(src, out, sem)
    copy.start()
    copy.wait()


def loop(count, body):
    lax.fori_loop(0, count, lambda i, carry: (body(i), carry)[1], 0)


def qkv_kernel(n, heads, info, unit_ref, *refs):
    pieces, (a1_ref, m_ref, v_ref, w_ref, norm_ref) = refs[:n], refs[n:]
    cols = m_ref.shape[1]
    base = cols // LANES * LANES
    rows = w_ref.shape[0] // n
    for k, piece in enumerate(pieces):
        w_ref[block(info[4 + k], rows), :] = piece[...]
    turned = w_ref[:, base : base + LANES].astype(f32).T
    norm_ref[...] = turned[cols - base : cols - base + 8]

    def step(i):
        at = block(i)
        a1 = (unit_ref[at, :] * norm_ref[0:1] + norm_ref[1:2]).astype(bf16)
        a1_ref[at, :] = a1
        mixed = dot(a1, w_ref[:, :cols])
        m_ref[at, :] = mixed.astype(bf16)
        for h in range(heads):
            fresh = mixed[:, (3 * h + 2) * HD : (3 * h + 3) * HD]
            v_ref[h * HD : (h + 1) * HD, at] = fresh.T.astype(bf16)

    loop(m_ref.shape[0] // RB, step)


def values_kernel(heads, info, src, fresh, f0, f1, f2, f3, v_ref):
    mp = info[2]
    for h in range(heads):
        source = src[mp * heads + h]
        held = source // heads
        mine = slice(h * HD, (h + 1) * HD)

        @pl.when(source >= H)
        def _():
            v_ref[mine, :] = fresh[mine, :]

        for r, first in enumerate((f0, f1, f2, f3)):

            @pl.when((source < H) & (held == mp ^ r))
            def _():
                v_ref[mine, :] = first[block(source - held * heads, HD), :]


def masked_tile():
    keys = lax.broadcasted_iota(jnp.int32, (RB, RB), 0)
    queries = lax.broadcasted_iota(jnp.int32, (RB, RB), 1)
    return keys <= queries


def attend_kernel(heads, base, m_ref, v_ref, c_ref, lse_ref):
    keep = masked_tile()
    blocks = c_ref.shape[0] // RB
    turned = [[None] * heads for _ in range(blocks)]
    lse_ref[...] = jnp.zeros(lse_ref.shape, f32)
    for h in range(heads):
        top = base + blocks * RB
        keys = m_ref[:top, (3 * h + 1) * HD : (3 * h + 2) * HD]
        values_t = v_ref[h * HD : (h + 1) * HD, :top]
        for i in range(blocks):
            lo = base + i * RB
            hi = lo + RB
            query = m_ref[lo:hi, 3 * h * HD : (3 * h + 1) * HD] * bf16(HD**-0.5)
            diag = jnp.where(keep, dot_nt(keys[lo:hi], query), MASKED)
            peak = jnp.max(diag, 0, keepdims=True)
            if lo:
                left = dot_nt(keys[:lo], query)
                peak = jnp.maximum(peak, jnp.max(left, 0, keepdims=True))
            diag = jnp.exp(diag - peak)
            total = jnp.sum(diag, 0, keepdims=True)
            if lo:
                left = jnp.exp(left - peak)
                total += jnp.sum(left, 0, keepdims=True)
            inverse = 1.0 / total
            context = dot(values_t[:, lo:hi], (diag * inverse).astype(bf16))
            if lo:
                context += dot(values_t[:, :lo], (left * inverse).astype(bf16))
            turned[i][h] = context
            lse_ref[h : h + 1, i * RB : (i + 1) * RB] = peak + jnp.log(total)
    for i in range(blocks):
        c_ref[i * RB : (i + 1) * RB] = jnp.concatenate(turned[i], 0).T.astype(bf16)


def assemble_two_kernel(n, info, *refs):
    pieces, (wf, own, across, turn) = refs[:n], refs[n:]
    width, hid = wf.shape
    cw = own.shape[0]
    rows = width // n
    for k, piece in enumerate(pieces):
        at = block(info[4 + k], rows)
        wf[at, :] = piece[:, :hid]
        turn[at, :] = piece[:, hid:]
    pair = turn[...].T
    own[...] = pair[:cw]
    across[...] = pair[cw:]


def assemble_three_kernel(n, info, *refs):
    pieces, (wd,) = refs[:n], refs[n:]
    rows = wd.shape[0] // n
    for k, piece in enumerate(pieces):
        wd[block(info[4 + k], rows), :] = piece[...]


def mlp_kernel(part, x_ref, norm_ref, c0, c1, c2, c3, w0, w1, w2, w3, wf, r_ref, unit_ref, a2_ref, g_ref, slope_ref):
    def step(i):
        at = block(i)
        resid = x_ref[block(2 * part + i), :].astype(f32) + (
            (dot(c0[at, :], w0[...]) + dot(c1[at, :], w1[...]))
            + (dot(c2[at, :], w2[...]) + dot(c3[at, :], w3[...]))
        )
        r_ref[at, :] = resid
        unit, _ = norm_stats(resid)
        unit_ref[at, :] = unit
        a2 = (unit * norm_ref[2:3] + norm_ref[3:4]).astype(bf16)
        a2_ref[at, :] = a2
        u = dot(a2, wf[...])
        square = u * u
        t = jnp.tanh(GELU_A * u * (1.0 + GELU_B * square))
        g_ref[at, :] = (0.5 * u * (1.0 + t)).astype(bf16)
        slope_ref[at, :] = 0.5 * (1.0 + t) + 0.5 * u * (1.0 - t * t) * (
            GELU_A * (1.0 + 3.0 * GELU_B * square)
        )

    loop(2, step)


def mlp_back_kernel(part, info, e_ref, unit_ref, slope_ref, wf, wd, du_ref, top, bottom, keep, nacc):
    core = info[0]
    nacc[...] = jnp.zeros(nacc.shape, f32)

    def step(i):
        spot = jnp.where(i == 1, core, 1 - core)
        at = block(spot)
        du = (dot(e_ref[block(2 * part + spot), :], wd[...]) * slope_ref[at, :]).astype(bf16)
        du_ref[at, :] = du
        grad = dot_nt(du, wf[...])
        nacc[2:3] += jnp.sum(grad * unit_ref[at, :], 0, keepdims=True)
        nacc[3:4] += jnp.sum(grad, 0, keepdims=True)
        keep[...] = grad

        @pl.when(i == 0)
        def _():
            top[...] = grad[: RB // 2].astype(bf16)
            bottom[...] = grad[RB // 2 :].astype(bf16)

    loop(2, step)


def mlp_out_kernel(info, g_ref, wd, ysend, ykeep):
    ykeep[...] = dot_nt(g_ref[block(info[0]), :], wd[...])
    ysend[...] = dot_nt(g_ref[block(1 - info[0]), :], wd[...]).astype(bf16)


def add_kernel(keep, top, bottom, out):
    out[: RB // 2] = (keep[: RB // 2] + top[...].astype(f32)).astype(bf16)
    out[RB // 2 :] = (keep[RB // 2 :] + bottom[...].astype(f32)).astype(bf16)


def starts(info, full, fw, bw):
    rows = fw.shape[0]
    fw[...] = full[block(info[4 + OFFSETS.index(-4)], rows), :].astype(bf16)
    bw[...] = full[block(info[4 + OFFSETS.index(-3)], rows), :].astype(bf16)


def mlp_grad_kernel(info, a2a, a2b, dua, dub, e_ref, ga, gb, out, fw, bw):
    hid = dua.shape[1]
    half = dua.shape[0]

    def step(j):
        at = block(j)
        out[at, :hid] = (dot_tn(a2a[:, at], dua[...]) + dot_tn(a2b[:, at], dub[...])).astype(out.dtype)
        out[at, hid:] = (dot_tn(e_ref[:half, at], ga[...]) + dot_tn(e_ref[half:, at], gb[...])).astype(out.dtype)

    loop(out.shape[0] // RB, step)
    starts(info, out, fw, bw)


def hop_kernel(ahead, behind, info, full, a, b, a_out, b_out):
    rows = a.shape[0]
    for offset, value, out in ((ahead, a, a_out), (behind, b, b_out)):
        term = full[block(info[4 + OFFSETS.index(offset)], rows), :]
        out[...] = (value[...].astype(f32) + term.astype(f32)).astype(bf16)


def hop_last_kernel(info, full, a, a_out):
    term = full[block(info[4 + OFFSETS.index(1)], a.shape[0]), :]
    a_out[...] = (a[...].astype(f32) + term.astype(f32)).astype(bf16)


def norm_back(unit, scale, gain, grad):
    dy = grad * gain
    return scale * (
        dy - jnp.mean(dy, -1, keepdims=True) - unit * jnp.mean(dy * unit, -1, keepdims=True)
    )


def norm_two_kernel(part, info, r_ref, own, received, e_ref, norm_ref, dr_ref, top, bottom):
    unit, scale = norm_stats(r_ref[block(info[0]), :])
    grad = own[...].astype(f32) + received[...].astype(f32)
    e = e_ref[block(2 * part + info[0]), :].astype(f32)
    dr = e + norm_back(unit, scale, norm_ref[2:3], grad)
    dr_ref[...] = dr
    top[...] = dr[: RB // 2].astype(bf16)
    bottom[...] = dr[RB // 2 :].astype(bf16)


def attend_back_kernel(heads, base, blocks, stage, info, src, m_ref, v_ref, *refs):
    if stage < 2:
        halves, refs = refs[:4], refs[4:]
    else:
        ab_in, refs = refs[0], refs[1:]
    wp, lse_ref, *refs = refs
    if stage:
        dk_in, dv_in, *refs = refs
    if stage == 0:
        ab_ref, dq_ref, dk_ref, dv_ref = refs
    elif stage == 1:
        ab_ref, dq_ref, dk_ref, dv_ref = refs
    else:
        dq_first, dq_second, dm_ref, dvr_ref = refs
    keep = masked_tile()
    core = info[0]
    if stage < 2:
        for k in range(2):
            ab_ref[block(2 * core + k, RB // 2), :] = halves[k][...]
            ab_ref[block(2 * (1 - core) + k, RB // 2), :] = halves[2 + k][...]
        source, skip = ab_ref, 0
    else:
        source, skip = ab_in, ab_in.shape[0] - blocks * RB
    top = base + blocks * RB
    tiles = top // RB
    dctx = [dot_nt(source[skip + i * RB : skip + (i + 1) * RB], wp[...]).astype(bf16) for i in range(blocks)]
    dq_t = [[None] * heads for _ in range(blocks)]
    dks, dvs = [], []
    for h in range(heads):
        lane = slice(h * HD, (h + 1) * HD)
        keys = m_ref[:top, (3 * h + 1) * HD : (3 * h + 2) * HD]
        keys_t = keys.T
        values = v_ref[h * HD : (h + 1) * HD, :top].T
        dk = [None] * tiles
        dv = [None] * tiles
        if stage:
            for t in range(base // RB):
                dk[t] = dk_in[t * RB : (t + 1) * RB, lane]
                dv[t] = dv_in[t * RB : (t + 1) * RB, lane]
        for i in range(blocks):
            lo = base + i * RB
            count = lo // RB + 1
            query = m_ref[lo : lo + RB, 3 * h * HD : (3 * h + 1) * HD] * bf16(HD**-0.5)
            dc = dctx[i][:, lane]
            first = lse_ref.shape[1] - blocks * RB if stage == 2 else 0
            lse = lse_ref[h : h + 1, first + i * RB : first + (i + 1) * RB]
            probs, dprobs = [], []
            inner = jnp.zeros((1, RB), f32)
            for t in range(count):
                spot = slice(t * RB, (t + 1) * RB)
                score = dot_nt(keys[spot], query)
                prob = jnp.exp(score - lse)
                if t == count - 1:
                    prob = jnp.where(keep, prob, 0.0)
                dprob = dot_nt(values[spot], dc)
                inner += jnp.sum(prob * dprob, 0, keepdims=True)
                more = dot(prob.astype(bf16), dc)
                dv[t] = more if dv[t] is None else dv[t] + more
                probs.append(prob)
                dprobs.append(dprob)
            total = None
            for t in range(count):
                spot = slice(t * RB, (t + 1) * RB)
                ds = (probs[t] * (dprobs[t] - inner)).astype(bf16)
                more = dot(ds, query)
                dk[t] = more if dk[t] is None else dk[t] + more
                more = dot(keys_t[:, spot], ds)
                total = more if total is None else total + more
            dq_t[i][h] = total * HD**-0.5
        dks.append(dk)
        dvs.append(dv)
    dq = [jnp.concatenate(dq_t[i], 0).T for i in range(blocks)]
    if stage < 2:
        for i in range(blocks):
            dq_ref[i * RB : (i + 1) * RB] = dq[i]
        for t in range(tiles):
            dk_ref[t * RB : (t + 1) * RB] = jnp.concatenate([dks[h][t] for h in range(heads)], 1)
            dv_ref[t * RB : (t + 1) * RB] = jnp.concatenate([dvs[h][t] for h in range(heads)], 1)
        return
    mp = info[2]
    fresh = [jnp.where(src[mp * heads + h] < H, 0.0, 1.0) for h in range(heads)]
    split = dq_first.shape[0]
    for t in range(tiles):
        spot = slice(t * RB, (t + 1) * RB)
        parts = []
        for h in range(heads):
            lane = slice(h * HD, (h + 1) * HD)
            if t * RB < split:
                dqh = dq_first[spot, lane]
            elif t * RB < base:
                dqh = dq_second[t * RB - split : (t + 1) * RB - split, lane]
            else:
                dqh = dq[t - base // RB][:, lane]
            parts += [dqh, dks[h][t], dvs[h][t] * fresh[h]]
            dvr_ref[h * HD : (h + 1) * HD, spot] = dvs[h][t].T.astype(bf16)
        dm_ref[spot, :] = jnp.concatenate(parts, 1).astype(bf16)


def input_kernel(info, dm_ref, w_ref, unit_ref, na, nb, s0, s1, keep, sums):
    core = info[0]
    cols = dm_ref.shape[1]
    sums[...] = na[...] + nb[...]

    def step(i):
        half = i % 2
        spot = jnp.where(i < 2, 1 - core, core)
        at = block(2 * half + spot)
        grad = dot_nt(dm_ref[at, :], w_ref[:, :cols])
        sums[0:1] += jnp.sum(grad * unit_ref[at, :], 0, keepdims=True)
        sums[1:2] += jnp.sum(grad, 0, keepdims=True)
        keep[block(half), :] = grad
        for k, out in enumerate((s0, s1)):

            @pl.when(i == k)
            def _():
                out[...] = grad.astype(bf16)

    loop(4, step)


def to_rows_kernel(info, keep, r0, r1, mine, sent):
    low = info[1] == 0
    first = keep[:RB] + r0[...].astype(f32)
    second = keep[RB:] + r1[...].astype(f32)
    mine[...] = jnp.where(low, first, second)
    sent[...] = jnp.where(low, second, first).astype(bf16)


def output_rows_kernel(info, ka, kb, ra, rb, mine, sent):
    low = info[1] == 0
    first = ka[...] + ra[...].astype(f32)
    second = kb[...] + rb[...].astype(f32)
    mine[...] = jnp.where(low, first, second)
    sent[...] = jnp.where(low, second, first).astype(bf16)


def output_kernel(info, ra, rb, mine, received, out):
    at = block(info[0])
    resid = jnp.where(info[1] == 0, ra[at, :], rb[at, :])
    out[...] = (resid + mine[...] + received[...].astype(f32)).astype(bf16)


def qkv_grad_kernel(info, a1_ref, dm_ref, aba, abb, ca, cb, sums, out, fw, bw, turn):
    cols, width = dm_ref.shape[1], sums.shape[1]
    turn[...] = jnp.zeros(turn.shape, f32)
    turn[: sums.shape[0]] = sums[...]

    def step(j):
        at = block(j)
        grad = dot_tn(a1_ref[:, at], dm_ref[...])
        proj = dot_tn(aba[:, at], ca[...]) + dot_tn(abb[:, at], cb[...])
        out[at, : out.shape[1] - LANES] = jnp.concatenate([grad, proj], 1).astype(out.dtype)
        out[at, out.shape[1] - LANES :] = turn[:, at].T.astype(out.dtype)

    loop(out.shape[0] // RB, step)
    starts(info, out, fw, bw)


def norm_one_kernel(info, x_ref, own, received, dra, drb, norm_ref, out):
    unit, scale = norm_stats(x_ref[block(info[2]), :].astype(f32))
    grad = own[...] + received[...].astype(f32)
    dr = jnp.where(info[1] == 0, dra[...], drb[...])
    out[...] = dr + norm_back(unit, scale, norm_ref[0:1], grad)


def first_kernel(heads, info, src, d0, d1, d2, d3, out):
    mp = info[2]
    out[...] = jnp.zeros(out.shape, f32)
    for g in range(heads):
        user = jnp.int32(H)
        for h in range(H):
            user = jnp.where(src[h] == mp * heads + g, h, user)
        held = user // heads
        for r, ref in enumerate((d0, d1, d2, d3)):

            @pl.when((user < H) & (held == mp ^ r))
            def _():
                out[g * HD : (g + 1) * HD, :] = ref[block(user - held * heads, HD), :].astype(f32)


def adamw(master, moment, second, grad, rate, weighted):
    moment_new = 0.9 * moment + 0.1 * grad
    second_new = 0.999 * second + 0.001 * grad * grad
    mean_hat = moment_new / (1.0 - 0.9**ADAM_STEP)
    var_hat = second_new / (1.0 - 0.999**ADAM_STEP)
    master_new = master - rate * (mean_hat / (jnp.sqrt(var_hat) + 1e-08) + weighted * master)
    return (master_new, moment_new, second_new)


def adam_kernel(names, turned, info, full, a, b, *refs):
    ins, outs = refs[:6], refs[6:12]
    rows = a.shape[0]
    grad = a[...].astype(f32) + b[...].astype(f32)
    grad += full[block(info[4], rows), :].astype(f32)
    cols = ins[0].shape[1]
    if turned:
        grad = grad[:, : cols + ins[3].shape[0]]
    second = grad[:, cols:]
    if turned:
        second = jnp.concatenate([second, jnp.zeros((LANES - rows, second.shape[1]), f32)], 0).T[:, :rows]
    for k, (name, part) in enumerate(zip(names, (grad[:, :cols], second))):
        new = adamw(*[r[...] for r in ins[3 * k : 3 * k + 3]], part, RATES[name], 0.1)
        for ref, value in zip(outs[3 * k : 3 * k + 3], new):
            ref[...] = value


def norm_sum_kernel(info, full, a, b, out, turn):
    rows, width = a.shape
    at = slice(width - LANES, width)
    grad = a[:, at].astype(f32) + b[:, at].astype(f32) + full[block(info[4], rows), at].astype(f32)
    turn[...] = jnp.zeros(turn.shape, f32)
    turn[:rows] = grad
    out[...] = turn[...].T[:8]


def norm_adam_kernel(sums, received, w, m, s, w_out, m_out, s_out):
    rows, cols = w.shape
    grad = (sums[...] + received[...])[:rows, :cols]
    new = adamw(w[...], m[...], s[...], grad, RATES["norm"], 0.0)
    for ref, value in zip((w_out, m_out, s_out), new):
        ref[...] = value


def sum_kernel(a, b, out):
    out[...] = a[...] + b[...]


def swap_core(value):
    return lax.ppermute(value, "mp", [(i, i ^ 1) for i in range(4)])


def swap_x(value):
    return lax.ppermute(value, "mp", [(i, i ^ 2) for i in range(4)])


def both_cores(value):
    return lax.all_gather(value, "mp", axis_index_groups=[[0, 1], [2, 3]], axis=0, tiled=True)


FORWARD = [(RING[i], RING[(i + 1) % 8]) for i in range(8)]
BACKWARD = [(b, a) for a, b in FORWARD]


def ahead(value):
    return lax.ppermute(value, "dp", FORWARD)


def behind(value):
    return lax.ppermute(value, "dp", BACKWARD)


def after(value, *others):
    return lax.optimization_barrier((value,) + others)[0]


class Gather:
    def __init__(self, piece):
        self.ring = lax.axis_size("dp") == len(RING)
        self.start = self.a = self.b = piece
        self.ahead, self.behind = [], []

    def step(self, *gates):
        if not self.ring:
            return
        self.a, self.b = lax.optimization_barrier((self.a, self.b) + gates)[:2]
        self.a = ahead(self.a)
        self.ahead.append(self.a)
        if len(self.behind) < 3:
            self.b = behind(self.b)
            self.behind.append(self.b)

    def pieces(self):
        if not self.ring:
            return [lax.all_gather(self.start, "dp", axis=0, tiled=True)]
        return [self.start] + self.ahead + self.behind


class Scatter:
    def __init__(self, name, info, full, fw, bw):
        self.ring = lax.axis_size("dp") == len(RING)
        self.name, self.info, self.full, self.a, self.b = name, info, full, fw, bw
        self.steps = 0

    def step(self, *gates):
        if not self.ring:
            return
        self.a = after(self.a, *gates)
        k = 4 - self.steps
        shape = (self.a.shape, bf16)
        if k in (3, 2):
            kernel = functools.partial(hop_kernel, k, 1 - k)
            self.a, self.b = call(kernel, f"{self.name}_hop{k}", (self.info,), [self.full, self.a, self.b], [shape] * 2)
        if k == 1:
            (self.a,) = call(hop_last_kernel, f"{self.name}_hop1", (self.info,), [self.full, self.a], [shape])
        self.last = self.a
        self.a = ahead(self.a)
        if k > 1:
            self.b = behind(self.b)
        self.steps += 1

    def ends(self):
        return (self.a, self.b) if self.ring else None


def update(name, info, full, ends, firsts, seconds, turned):
    first, second = name
    outs = [(w.shape, f32) for w in firsts + seconds]
    if ends is not None:
        new = call(
            functools.partial(adam_kernel, name, turned),
            f"adam_{first}",
            (info,),
            [full, *ends, *firsts, *seconds],
            outs,
        )
        return tuple(new[:3]), tuple(new[3:])
    grad = lax.psum_scatter(full.astype(f32), "dp", scatter_dimension=0, tiled=True)
    cols = firsts[0].shape[1]
    other = grad[:, cols : cols + seconds[0].shape[0 if turned else 1]]
    return (
        adamw(*firsts, grad[:, :cols], RATES[first], 0.1),
        adamw(*seconds, other.T if turned else other, RATES[second], 0.1),
    )


def local(
    tokens_in,
    first_values,
    skip_source,
    grad_out,
    qkv_weight,
    proj_weight,
    fc_weight,
    down_weight,
    norm_params,
    qkv_moment,
    proj_moment,
    fc_moment,
    down_moment,
    norm_moment,
    qkv_second,
    proj_second,
    fc_second,
    down_second,
    norm_second,
):
    n = lax.axis_size("dp")
    ring = n == len(RING)
    pieces = n if ring else 1
    count, width = tokens_in.shape
    cols = qkv_weight.shape[1]
    heads = cols // (3 * HD)
    cw = heads * HD
    hid = fc_weight.shape[1]
    wide = -(-(cols + 4) // LANES) * LANES
    half = count // 2
    shard = qkv_weight.shape[0]
    info = HERE
    src = skip_source

    if ring:
        (ring_one,) = call(
            prep_one_kernel,
            "prep_one",
            (),
            [qkv_weight, norm_params],
            [((shard, wide), bf16)],
            scratch=[
                pltpu.VMEM((shard, cols), f32),
                pltpu.VMEM(norm_params.shape, f32),
                pltpu.VMEM((LANES, LANES), f32),
                pltpu.SemaphoreType.DMA((2,)),
            ],
            vmem=60,
            far=True,
        )
        proj_t, fc_low, down_t = call(
            prep_two_kernel,
            "prep_two",
            (),
            [after(proj_weight, ring_one), fc_weight, down_weight.T],
            [((shard, cw), bf16), ((shard, hid), bf16), ((shard, hid), bf16)],
            scratch=[
                pltpu.VMEM((cw, shard), f32),
                pltpu.VMEM((shard, hid), f32),
                pltpu.VMEM((shard, hid), f32),
                pltpu.VMEM((cw, LANES), f32),
                pltpu.SemaphoreType.DMA((3,)),
            ],
            vmem=56,
            far=True,
        )
    else:
        blank = jnp.zeros((shard, wide - cols - 4), bf16)
        ring_one = jnp.concatenate([qkv_weight.astype(bf16), norm_params.T.astype(bf16), blank], 1)
        proj_t, fc_low, down_t = proj_weight.T.astype(bf16), fc_weight.astype(bf16), down_weight.T.astype(bf16)
    fence = lambda *values: lax.optimization_barrier(values)
    fence = lambda *values: lax.optimization_barrier(values)
    one = Gather(ring_one)
    one.step()
    one.a, one.b, proj_t, tokens = fence(one.a, one.b, proj_t, tokens_in)
    one.step()
    proj_x = swap_x(proj_t)
    (unit_one,) = call(unit_kernel, "unit", (), [tokens], [((count, width), f32)])
    one.a, one.b, proj_x, unit_one = fence(one.a, one.b, proj_x, unit_one)
    one.step()
    if ring:
        (ring_two,) = call(
            join_kernel, "join", (), [fc_low, proj_t, proj_x], [((shard, hid + 2 * cw), bf16)]
        )
    else:
        ring_two = jnp.concatenate([fc_low, proj_t, proj_x], 1)
    two, three = Gather(ring_two), Gather(down_t)
    two.step()
    first_t = after(first_values.T, unit_one)
    first_x, first_c = swap_x(first_t), swap_core(first_t)
    one.a, one.b = fence(one.a, one.b)
    one.step()
    one.a, two.a, two.b, unit_one, first_x, three.a = fence(one.a, two.a, two.b, unit_one, first_x, three.a)
    if ring:
        one.ahead[-1] = one.a
    first_xc = swap_core(first_x)
    two.step()
    three.step()

    a1, mixed, fresh, qkv_full, norms = call(
        functools.partial(qkv_kernel, pieces, heads),
        "qkv",
        (info,),
        [unit_one, *one.pieces()],
        [
            ((count, width), bf16),
            ((count, cols), bf16),
            ((cw, count), bf16),
            ((width, wide), bf16),
            ((8, width), f32),
        ],
    )
    (values,) = call(
        functools.partial(values_kernel, heads),
        "values",
        (info, src),
        [fresh, first_t, first_c, first_x, first_xc],
        [((cw, count), bf16)],
    )

    def attend(part, mixed):
        return call(
            functools.partial(attend_kernel, heads, part * half),
            f"attend{part}",
            (),
            [mixed, values],
            [((half, cw), bf16), ((8, half), f32)],
        )

    ctx_a, lse_a = attend(0, mixed)
    two.a, two.b, three.a, three.b, ctx_a = fence(two.a, two.b, three.a, three.b, ctx_a)
    two.step()
    three.step()
    xa = swap_x(ctx_a)
    ctx_b, lse_b = attend(1, after(mixed, ctx_a))
    two.a, two.b, three.a, three.b, xa, ctx_b = fence(two.a, two.b, three.a, three.b, xa, ctx_b)
    two.step()
    three.step()
    xb = swap_x(ctx_b)
    (grad_out,) = call(
        fetch_kernel,
        "fetch",
        (),
        [after(grad_out, ctx_b)],
        [(grad_out.shape, bf16)],
        scratch=[pltpu.SemaphoreType.DMA],
        vmem=4,
        far=True,
    )
    start, xb, two_last, three.a, three.b, grad_out = fence(two.start, xb, two.a, three.a, three.b, grad_out)
    ca, xca, cb, xcb = swap_core(ctx_a), swap_core(xa), swap_core(ctx_b), swap_core(xb)
    three.step()
    context, lse = (ctx_a, ctx_b), (lse_a, lse_b)
    wf, own_w, across_w = call(
        functools.partial(assemble_two_kernel, pieces),
        "assemble_two",
        (info,),
        [start, *two.pieces()[1:]] if ring else two.pieces(),
        [((width, hid), bf16), ((cw, width), bf16), ((cw, width), bf16)],
        scratch=[pltpu.VMEM((width, 2 * cw), bf16)],
    )
    pair = own_w, swap_core(own_w), across_w, swap_core(across_w)

    def mlp(part, norms, contexts):
        return call(
            functools.partial(mlp_kernel, part),
            f"mlp{part}",
            (),
            [tokens, norms, *contexts, *pair, wf],
            [
                ((half, width), f32),
                ((half, width), f32),
                ((half, width), bf16),
                ((half, hid), bf16),
                ((half, hid), f32),
            ],
        )

    def mlp_back(part, grad):
        return call(
            functools.partial(mlp_back_kernel, part),
            f"mlp_back{part}",
            (info,),
            [grad, unit_two[part], slope[part], wf, wd],
            [((half, hid), bf16)] + [((RB // 2, width), bf16)] * 2 + [((RB, width), f32), ((8, width), f32)],
        )

    def mlp_out(part, gate):
        return call(
            mlp_out_kernel,
            f"mlp_out{part}",
            (info,),
            [after(act[part], gate), wd],
            [((RB, width), bf16), ((RB, width), f32)],
        )

    def add(part, keep, *received):
        return call(add_kernel, f"add{part}", (), [keep, *received], [((RB, width), bf16)])[0]

    forward_a = mlp(0, norms, (ctx_a, ca, xa, xca))
    forward_b = mlp(1, after(norms, forward_a[0]), (ctx_b, cb, xb, xcb))
    resid, unit_two, a2, act, slope = zip(forward_a, forward_b)
    start, last = fence(three.start, act[1])
    (wd,) = call(
        functools.partial(assemble_three_kernel, pieces),
        "assemble_three",
        (info,),
        [start, *three.pieces()[1:]] if ring else three.pieces(),
        [((width, hid), bf16)],
    )
    dpre_a, top_a, bottom_a, dkeep_a, nacc_a = mlp_back(0, after(grad_out, act[1]))
    received_a = swap_core(top_a), swap_core(bottom_a)
    dpre_b, top_b, bottom_b, dkeep_b, nacc_b = mlp_back(1, after(grad_out, dpre_a))
    mine_a = add(0, after(dkeep_a, dpre_b), *received_a)
    received_b = swap_core(top_b), swap_core(bottom_b)
    across_a = swap_x(mine_a)

    piece = lambda w: [((width // pieces if ring else 16, w), bf16)] * 2
    mlp_grad, mlp_fw, mlp_bw = call(
        mlp_grad_kernel,
        "mlp_grad",
        (info,),
        [after(a2[0], mine_a), a2[1], dpre_a, dpre_b, grad_out, act[0], act[1]],
        [((width, 2 * hid), bf16 if ring else f32)] + piece(2 * hid),
    )
    mlp_sum = Scatter("mlp", info, mlp_grad, mlp_fw, mlp_bw)
    mlp_sum.step()
    mine_b = add(1, after(dkeep_b, mlp_grad), *received_b)
    across_b = swap_x(mine_b)
    def norm_two(part, mine, across):
        return call(
            functools.partial(norm_two_kernel, part),
            f"norm_two{part}",
            (info,),
            [resid[part], mine, across, grad_out, norms],
            [((RB, width), f32)] + [((RB // 2, width), bf16)] * 2,
        )

    def attend_back(stage, base, blocks, given, part, before, outs):
        return call(
            functools.partial(attend_back_kernel, heads, base, blocks, stage),
            f"attend_back{stage}",
            (info, src),
            [mixed, values, *given, own_w, lse[part], *before],
            outs,
            vmem=24,
        )

    dr_a, *ab_a = norm_two(0, after(mine_a, mine_b), across_a)
    partner = [swap_core(v) for v in ab_a]
    ab_one, dq_a, dk, dv = attend_back(
        0, 0, 2, [*ab_a, *partner], 0, [], [((half, width), bf16)] + [((half, cw), f32)] * 3
    )
    mlp_sum.a, mlp_sum.b, dq_a = fence(mlp_sum.a, mlp_sum.b, dq_a)
    mlp_sum.step()
    ysend_a, ykeep_a = mlp_out(0, dq_a)
    ysend_b, ykeep_b = mlp_out(1, ysend_a)
    yreceived_a, yreceived_b = swap_core(ysend_a), swap_core(ysend_b)
    rows_mine, rows_sent = call(
        output_rows_kernel,
        "output_rows",
        (info,),
        [ykeep_a, ykeep_b, yreceived_a, yreceived_b],
        [((RB, width), f32), ((RB, width), bf16)],
    )
    dr_b, *ab_b = norm_two(1, after(mine_b, ysend_b), across_b)
    partner = [swap_core(v) for v in ab_b]
    rows_received = swap_x(after(rows_sent, dr_b))
    top = half + RB
    ab_two, dq_b, dk, dv = attend_back(
        1, half, 1, [*ab_b, *partner], 1, [dk, dv], [((half, width), bf16), ((RB, cw), f32)] + [((top, cw), f32)] * 2
    )
    mlp_sum.a, mlp_sum.b, dq_b = fence(mlp_sum.a, mlp_sum.b, dq_b)
    mlp_sum.step()
    dmixed, dreused = attend_back(
        2,
        top,
        1,
        [ab_two],
        1,
        [after(dk, mlp_sum.last) if ring else dk, dv, dq_a, dq_b],
        [((count, cols), bf16), ((cw, count), bf16)],
    )

    *isend, ikeep, sums = call(
        input_kernel,
        "input",
        (info,),
        [dmixed, qkv_full, unit_one, nacc_a, nacc_b],
        [((RB, width), bf16)] * 2 + [((half, width), f32), ((8, width), f32)],
    )
    qkv_grad, qkv_fw, qkv_bw = call(
        qkv_grad_kernel,
        "qkv_grad",
        (info,),
        [a1, dmixed, ab_one, ab_two, context[0], context[1], sums],
        [((width, cols + cw + LANES), bf16 if ring else f32)] + piece(cols + cw + LANES),
        scratch=[pltpu.VMEM((LANES, width), f32)],
    )
    qkv_sum = Scatter("qkv", info, qkv_grad, qkv_fw, qkv_bw)
    mlp_sum.a, mlp_sum.b, qkv_sum.a, qkv_sum.b, rows_received = fence(
        mlp_sum.a, mlp_sum.b, qkv_sum.a, qkv_sum.b, rows_received
    )
    mlp_sum.step()
    qkv_sum.step()
    gathered = [swap_core(v) for v in isend]
    mine, sent = call(
        to_rows_kernel, "to_rows", (info,), [ikeep, *gathered], [((RB, width), f32), ((RB, width), bf16)]
    )
    across, dx = swap_x(sent), swap_x(dreused)
    qkv_sum.a, qkv_sum.b, sent = fence(qkv_sum.a, qkv_sum.b, sent)
    qkv_sum.step()
    (block_out,) = call(
        output_kernel,
        "output",
        (info,),
        [resid[0], resid[1], rows_mine, rows_received],
        [((RB, width), bf16)],
    )
    qkv_sum.a, qkv_sum.b, mlp_sum.a, block_out = fence(qkv_sum.a, qkv_sum.b, mlp_sum.a, block_out)
    qkv_sum.step()
    fc_new, down_new = update(
        ("fc", "down"),
        info,
        mlp_grad,
        mlp_sum.ends(),
        [fc_weight, fc_moment, fc_second],
        [down_weight.T, down_moment.T, down_second.T],
        False,
    )
    qkv_sum.a, qkv_sum.b, across, dx, *fc_new = fence(qkv_sum.a, qkv_sum.b, across, dx, *fc_new)
    down_new = tuple(v.T for v in down_new)
    qkv_sum.step()
    (input_grad,) = call(
        norm_one_kernel,
        "norm_one",
        (info,),
        [tokens, mine, across, dr_a, dr_b, norms],
        [((RB, width), f32)],
    )
    dx, dreused = fence(dx, dreused)
    dc, dxc = swap_core(dreused), swap_core(dx)
    (first_grad,) = call(
        functools.partial(first_kernel, heads),
        "first",
        (info, src),
        [dreused, dc, dx, dxc],
        [((cw, count), f32)],
    )
    qkv_sum.a, input_grad, first_grad = fence(qkv_sum.a, input_grad, first_grad)
    if ring:
        (sums,) = call(
            norm_sum_kernel,
            "norm_sum",
            (info,),
            [qkv_grad, *qkv_sum.ends()],
            [((8, LANES), f32)],
            scratch=[pltpu.VMEM((LANES, LANES), f32)],
        )
        (sums,) = call(sum_kernel, "sum", (), [sums, swap_core(sums)], [(sums.shape, f32)])
        received = swap_x(sums)
    qkv_new, proj_new = update(
        ("qkv", "proj"),
        info,
        qkv_grad,
        qkv_sum.ends(),
        [qkv_weight, qkv_moment, qkv_second],
        [proj_weight, proj_moment, proj_second],
        True,
    )
    if ring:
        norm_new = call(
            norm_adam_kernel,
            "adam_norm",
            (),
            [sums, received, norm_params, norm_moment, norm_second],
            [(norm_params.shape, f32)] * 3,
        )
    else:
        own = lax.psum_scatter(lax.psum(sums, "mp"), "dp", scatter_dimension=1, tiled=True)[:4]
        norm_new = adamw(norm_params, norm_moment, norm_second, own, RATES["norm"], 0.0)
    return (block_out, input_grad, first_grad.T, *qkv_new, *proj_new, *fc_new, *down_new, *norm_new)


def solution(mesh):
    both = P("dp", "mp")
    turned = P("mp", "dp")
    rows = P("dp", None)
    every = P(None, "dp")
    state = (both, turned, both, turned, every)
    return jax.shard_map(
        local,
        mesh=mesh,
        in_specs=(rows, both, P(), rows) + state * 3,
        out_specs=(P(("dp", "mp"), None), P(("dp", "mp"), None), both)
        + (both,) * 3
        + (turned,) * 3
        + (both,) * 3
        + (turned,) * 3
        + (every,) * 3,
        check_vma=False,
    )
```

```python
import functools

import jax
import jax.numpy as jnp
import numpy as np
from jax import lax
from jax.experimental import pallas as pl
from jax.experimental.pallas import tpu as pltpu
from jax.sharding import PartitionSpec as P

H = 12
HD = 64
ADAM_STEP = 5
EPS = 1e-05
MASKED = -1e30
RB = 256
LANES = 128
RING = (0, 2, 4, 6, 7, 5, 3, 1)
AHEAD = (0, -1, -2, -3, -4, 1, 2, 3)
BEHIND = (0, 1, 2, 3, 4, -1, -2, -3)
GELU_A = 0.7978845608028654
GELU_B = 0.044715
RATES = {"qkv": 0.06, "proj": 0.15, "fc": 0.04, "down": 0.03, "norm": 0.3}

bf16 = jnp.bfloat16
f32 = jnp.float32


def dot(a, b):
    return jnp.dot(a, b, preferred_element_type=f32)


def dot_nt(a, b):
    return lax.dot_general(a, b, (((1,), (1,)), ((), ())), preferred_element_type=f32)


def dot_tn(a, b):
    return lax.dot_general(a, b, (((0,), (0,)), ((), ())), preferred_element_type=f32)


class Place:
    def __init__(self):
        self.mp, self.dp = lax.axis_index("mp"), lax.axis_index("dp")

    def __getitem__(self, k):
        return (self.mp % 2, self.mp // 2, self.mp, self.dp)[k]

    def ring(self, offset):
        if lax.axis_size("dp") != len(RING):
            return 0
        z, y = self.dp // 2, self.dp % 2
        at = (jnp.where(y == 0, z, 7 - z) + offset + 8) % 8
        return jnp.where(at < 4, 2 * at, 2 * (7 - at) + 1)


HERE = object()


def call(kernel, name, scalars, ins, outs, scratch=(), vmem=16, far=False):
    if HERE in scalars:
        inner = kernel
        kernel = lambda *refs: inner(Place(), *refs)
        scalars = scalars[1:]
    smem = pl.BlockSpec(memory_space=pltpu.SMEM)
    full = pl.BlockSpec(memory_space=pltpu.VMEM)
    given = pl.BlockSpec(memory_space=pltpu.HBM) if far else full
    return pl.pallas_call(
        kernel,
        in_specs=[smem] * len(scalars) + [given] * len(ins),
        out_specs=[full] * len(outs),
        out_shape=[jax.ShapeDtypeStruct(sh, dt) for sh, dt in outs],
        scratch_shapes=list(scratch),
        compiler_params=pltpu.CompilerParams(vmem_limit_bytes=vmem * 1024 * 1024),
        cost_estimate=pl.CostEstimate(flops=1, bytes_accessed=1, transcendentals=0),
        name=name,
    )(*scalars, *ins)


def block(index, size=RB):
    if isinstance(index, int):
        return slice(index * size, (index + 1) * size)
    return pl.ds(pl.multiple_of(index * size, size), size)


def fetch(pairs, sems):
    copies = [pltpu.make_async_copy(src, dst, sems.at[k]) for k, (src, dst) in enumerate(pairs)]
    for copy in copies:
        copy.start()
    for copy in copies:
        copy.wait()


def prep_one_kernel(q_ref, n_ref, p_ref, out, q, norms, p, turn, turn_p, sems):
    rows, cols = q_ref.shape
    turn[...] = jnp.zeros(turn.shape, f32)
    turn_p[...] = jnp.zeros(turn_p.shape, f32)
    fetch([(q_ref, q), (n_ref, norms), (p_ref, p)], sems)
    wide = -(-(cols + norms.shape[0]) // LANES) * LANES
    end = wide + p.shape[0]
    turn[: norms.shape[0], :rows] = norms[...]
    turn_p[:, :rows] = p[...]
    out[:, :cols] = q[...].astype(bf16)
    out[:, cols:wide] = turn[...].T[:rows, : wide - cols].astype(bf16)
    out[:, wide:end] = turn_p[...].T[:rows].astype(bf16)
    out[:, end:] = jnp.zeros((rows, out.shape[1] - end), bf16)


def prep_two_kernel(f_ref, d_ref, out, f, d, sems):
    fetch([(f_ref, f), (d_ref, d)], sems)
    out[:, : f.shape[1]] = f[...].astype(bf16)
    out[:, f.shape[1] :] = d[...].astype(bf16)


def norm_stats(values):
    center = values - jnp.mean(values, axis=-1, keepdims=True)
    scale = lax.rsqrt(jnp.mean(center * center, axis=-1, keepdims=True) + EPS)
    return center * scale, scale


def unit_kernel(x_ref, unit_ref):
    for i in range(x_ref.shape[0] // RB):
        at = slice(i * RB, (i + 1) * RB)
        unit_ref[at] = norm_stats(x_ref[at].astype(f32))[0]


def fetch_kernel(src, out, sem):
    copy = pltpu.make_async_copy(src, out, sem)
    copy.start()
    copy.wait()


def loop(count, body):
    lax.fori_loop(0, count, lambda i, carry: (body(i), carry)[1], 0)


def qkv_kernel(n, heads, info, unit_ref, *refs):
    pieces, (a1_ref, m_ref, v_ref, w_ref, norm_ref, p_ref, turn) = refs[:n], refs[n:]
    cols = m_ref.shape[1]
    base = cols // LANES * LANES
    rows = w_ref.shape[0] // n
    for offset, piece in zip(AHEAD, pieces):
        at = block(info.ring(offset), rows)
        w_ref[at, :] = piece[:, : w_ref.shape[1]]
        turn[at, :] = piece[:, w_ref.shape[1] : w_ref.shape[1] + turn.shape[1]]
    cw = turn.shape[1]
    p_ref[:cw] = turn[...].T
    p_ref[cw:] = jnp.zeros((p_ref.shape[0] - cw, p_ref.shape[1]), bf16)
    turned = w_ref[:, base : base + LANES].astype(f32).T
    norm_ref[...] = turned[cols - base : cols - base + 8]

    def step(i):
        at = block(i)
        a1 = (unit_ref[at, :] * norm_ref[0:1] + norm_ref[1:2]).astype(bf16)
        a1_ref[at, :] = a1
        mixed = dot(a1, w_ref[:, :cols])
        m_ref[at, :] = mixed.astype(bf16)
        for h in range(heads):
            fresh = mixed[:, (3 * h + 2) * HD : (3 * h + 3) * HD]
            v_ref[h * HD : (h + 1) * HD, at] = fresh.T.astype(bf16)

    loop(m_ref.shape[0] // RB, step)


def values_kernel(heads, info, src, fresh, f0, f1, f2, f3, v_ref):
    mp = info[2]
    for h in range(heads):
        source = src[mp * heads + h]
        held = source // heads
        mine = slice(h * HD, (h + 1) * HD)

        @pl.when(source >= H)
        def _():
            v_ref[mine, :] = fresh[mine, :]

        for r, first in enumerate((f0, f1, f2, f3)):

            @pl.when((source < H) & (held == mp ^ r))
            def _():
                v_ref[mine, :] = first[block(source - held * heads, HD), :]


def masked_tile():
    keys = lax.broadcasted_iota(jnp.int32, (RB, RB), 0)
    queries = lax.broadcasted_iota(jnp.int32, (RB, RB), 1)
    return keys <= queries


def attend_kernel(heads, base, m_ref, v_ref, c_ref, lse_ref):
    keep = masked_tile()
    blocks = c_ref.shape[1] // RB
    turned = [[None] * heads for _ in range(blocks)]
    lse_ref[...] = jnp.zeros(lse_ref.shape, f32)
    for h in range(heads):
        top = base + blocks * RB
        keys = m_ref[:top, (3 * h + 1) * HD : (3 * h + 2) * HD]
        values_t = v_ref[h * HD : (h + 1) * HD, :top]
        for i in range(blocks):
            lo = base + i * RB
            hi = lo + RB
            query = m_ref[lo:hi, 3 * h * HD : (3 * h + 1) * HD] * bf16(HD**-0.5)
            diag = jnp.where(keep, dot_nt(keys[lo:hi], query), MASKED)
            peak = jnp.max(diag, 0, keepdims=True)
            if lo:
                left = dot_nt(keys[:lo], query)
                peak = jnp.maximum(peak, jnp.max(left, 0, keepdims=True))
            diag = jnp.exp(diag - peak)
            total = jnp.sum(diag, 0, keepdims=True)
            if lo:
                left = jnp.exp(left - peak)
                total += jnp.sum(left, 0, keepdims=True)
            inverse = 1.0 / total
            context = dot(values_t[:, lo:hi], (diag * inverse).astype(bf16))
            if lo:
                context += dot(values_t[:, :lo], (left * inverse).astype(bf16))
            turned[i][h] = context
            lse_ref[h : h + 1, i * RB : (i + 1) * RB] = peak + jnp.log(total)
    for i in range(blocks):
        c_ref[:, i * RB : (i + 1) * RB] = jnp.concatenate(turned[i], 0).astype(bf16)


def assemble_kernel(n, info, *refs):
    pieces, (wf, wd) = refs[:n], refs[n:]
    rows, hid = wf.shape[0] // n, wf.shape[1]
    for offset, piece in zip(BEHIND, pieces):
        at = block(info.ring(offset), rows)
        wf[at, :] = piece[:, :hid]
        wd[at, :] = piece[:, hid:]


def mlp_kernel(part, info, x_ref, norm_ref, c0, c1, c2, c3, w0, w1, w2, w3, wf, r_ref, unit_ref, a2_ref, g_ref, slope_ref):
    cw = c0.shape[0]
    partner = block(1 - info[0], cw)
    partner_w = pl.ds(pl.multiple_of((1 - info[0]) * w0.shape[0], 16), cw)
    third = partner if c3.shape[0] > cw else slice(None)

    def step(i):
        at = block(i)
        resid = x_ref[block(2 * part + i), :].astype(f32) + (
            (dot_tn(c0[:, at], w0[:cw]) + dot_tn(c1[:, at], w1[partner_w, :]))
            + (dot_tn(c2[:, at], w2[:cw]) + dot_tn(c3[third, at], w3[partner_w, :]))
        )
        r_ref[at, :] = resid
        unit, _ = norm_stats(resid)
        unit_ref[at, :] = unit
        a2 = (unit * norm_ref[2:3] + norm_ref[3:4]).astype(bf16)
        a2_ref[at, :] = a2
        u = dot(a2, wf[...])
        square = u * u
        t = jnp.tanh(GELU_A * u * (1.0 + GELU_B * square))
        g_ref[at, :] = (0.5 * u * (1.0 + t)).astype(bf16)
        slope_ref[at, :] = 0.5 * (1.0 + t) + 0.5 * u * (1.0 - t * t) * (
            GELU_A * (1.0 + 3.0 * GELU_B * square)
        )

    for i in range(2):
        step(i)


def mlp_back_kernel(part, info, e_ref, unit_ref, slope_ref, wf, wd, du_ref, top, bottom, keep, nacc):
    core = info[0]
    nacc[...] = jnp.zeros(nacc.shape, f32)

    def step(i):
        spot = core if i else 1 - core
        at = block(spot)
        du = (dot(e_ref[block(2 * part + spot), :], wd[...]) * slope_ref[at, :]).astype(bf16)
        du_ref[at, :] = du
        grad = dot_nt(du, wf[...])
        nacc[2:3] += jnp.sum(grad * unit_ref[at, :], 0, keepdims=True)
        nacc[3:4] += jnp.sum(grad, 0, keepdims=True)
        keep[...] = grad

        @pl.when(i < 1)
        def _():
            top[...] = grad[: RB // 2].astype(bf16)
            bottom[...] = grad[RB // 2 :].astype(bf16)

    for i in range(2):
        step(i)


def mlp_out_kernel(info, g_ref, wd, ysend, ykeep):
    ykeep[...] = dot_nt(g_ref[block(info[0]), :], wd[...])
    ysend[...] = dot_nt(g_ref[block(1 - info[0]), :], wd[...]).astype(bf16)


def add_kernel(keep, top, bottom, out):
    out[: RB // 2] = (keep[: RB // 2] + top[...].astype(f32)).astype(bf16)
    out[RB // 2 :] = (keep[RB // 2 :] + bottom[...].astype(f32)).astype(bf16)


def starts(info, full, fw, bw):
    rows = fw.shape[0]
    fw[...] = full[block(info.ring(-4), rows), :].astype(bf16)
    bw[...] = full[block(info.ring(-3), rows), :].astype(bf16)


def mlp_grad_kernel(info, a2a, a2b, dua, dub, e_ref, ga, gb, out, fw, bw):
    hid = dua.shape[1]
    half = dua.shape[0]

    def step(j):
        at = block(j)
        out[at, :hid] = (dot_tn(a2a[:, at], dua[...]) + dot_tn(a2b[:, at], dub[...])).astype(out.dtype)
        out[at, hid:] = (dot_tn(e_ref[:half, at], ga[...]) + dot_tn(e_ref[half:, at], gb[...])).astype(out.dtype)

    for j in range(out.shape[0] // RB):
        step(j)
    starts(info, out, fw, bw)


def hop_kernel(ahead, behind, info, full, a, b, a_out, b_out):
    rows = a.shape[0]
    for offset, value, out in ((ahead, a, a_out), (behind, b, b_out)):
        term = full[block(info.ring(offset), rows), :]
        out[...] = (value[...].astype(f32) + term.astype(f32)).astype(bf16)


def hop_last_kernel(info, full, a, a_out):
    term = full[block(info.ring(1), a.shape[0]), :]
    a_out[...] = (a[...].astype(f32) + term.astype(f32)).astype(bf16)


def norm_back(unit, scale, gain, grad):
    dy = grad * gain
    return scale * (
        dy - jnp.mean(dy, -1, keepdims=True) - unit * jnp.mean(dy * unit, -1, keepdims=True)
    )


def norm_two_kernel(part, info, r_ref, own, received, e_ref, norm_ref, dr_ref, top, bottom):
    unit, scale = norm_stats(r_ref[block(info[0]), :])
    grad = own[...].astype(f32) + received[...].astype(f32)
    e = e_ref[block(2 * part + info[0]), :].astype(f32)
    dr = e + norm_back(unit, scale, norm_ref[2:3], grad)
    dr_ref[...] = dr
    top[...] = dr[: RB // 2].astype(bf16)
    bottom[...] = dr[RB // 2 :].astype(bf16)


def attend_back_kernel(heads, base, blocks, stage, info, src, m_ref, v_ref, *refs):
    if stage < 2:
        halves, refs = refs[:4], refs[4:]
    else:
        ab_in, refs = refs[0], refs[1:]
    wp, lse_ref, c_ref, *refs = refs
    if stage:
        dk_in, dv_in, *refs = refs
    if stage == 0:
        ab_ref, dq_ref, dk_ref, dv_ref = refs
    elif stage == 1:
        ab_ref, dq_ref, dk_ref, dv_ref = refs
    else:
        dq_first, dq_second, dm_ref, dvr_ref = refs
    keep = masked_tile()
    core = info[0]
    if stage < 2:
        for k in range(2):
            ab_ref[block(2 * core + k, RB // 2), :] = halves[k][...]
            ab_ref[block(2 * (1 - core) + k, RB // 2), :] = halves[2 + k][...]
        source, skip = ab_ref, 0
    else:
        source, skip = ab_in, ab_in.shape[0] - blocks * RB
    top = base + blocks * RB
    tiles = top // RB
    dctx = [dot_nt(source[skip + i * RB : skip + (i + 1) * RB], wp[: heads * HD]).astype(bf16) for i in range(blocks)]
    dctx_t = [v.astype(f32).T for v in dctx]
    dq_t = [[None] * heads for _ in range(blocks)]
    dks, dvs = [], []
    for h in range(heads):
        lane = slice(h * HD, (h + 1) * HD)
        keys = m_ref[:top, (3 * h + 1) * HD : (3 * h + 2) * HD]
        keys_t = keys.T
        values = v_ref[h * HD : (h + 1) * HD, :top].T
        dk = [None] * tiles
        dv = [None] * tiles
        if stage:
            for t in range(base // RB):
                dk[t] = dk_in[t * RB : (t + 1) * RB, lane]
                dv[t] = dv_in[t * RB : (t + 1) * RB, lane]
        for i in range(blocks):
            lo = base + i * RB
            hi = lo + RB
            query = m_ref[lo:hi, 3 * h * HD : (3 * h + 1) * HD] * bf16(HD**-0.5)
            dc = dctx[i][:, lane]
            first = lse_ref.shape[1] - blocks * RB if stage == 2 else 0
            lse = lse_ref[h : h + 1, first + i * RB : first + (i + 1) * RB]
            prob = jnp.exp(dot_nt(keys[:hi], query) - lse)
            own = jnp.where(keep, prob[lo:], 0.0)
            prob = jnp.concatenate([prob[:lo], own], 0) if lo else own
            dprob = dot_nt(values[:hi], dc)
            spot = slice(first + i * RB, first + (i + 1) * RB)
            inner = jnp.sum(dctx_t[i][lane] * c_ref[lane, spot].astype(f32), 0, keepdims=True)
            more_v = dot(prob.astype(bf16), dc)
            ds = (prob * (dprob - inner)).astype(bf16)
            more_k = dot(ds, query)
            dq_t[i][h] = dot(keys_t[:, :hi], ds) * HD**-0.5
            for t in range(hi // RB):
                spot = slice(t * RB, (t + 1) * RB)
                dv[t] = more_v[spot] if dv[t] is None else dv[t] + more_v[spot]
                dk[t] = more_k[spot] if dk[t] is None else dk[t] + more_k[spot]
        dks.append(dk)
        dvs.append(dv)
    dq = [jnp.concatenate(dq_t[i], 0).T for i in range(blocks)]
    if stage < 2:
        for i in range(blocks):
            dq_ref[i * RB : (i + 1) * RB] = dq[i]
        for t in range(tiles):
            dk_ref[t * RB : (t + 1) * RB] = jnp.concatenate([dks[h][t] for h in range(heads)], 1)
            dv_ref[t * RB : (t + 1) * RB] = jnp.concatenate([dvs[h][t] for h in range(heads)], 1)
        return
    mp = info[2]
    fresh = [jnp.where(src[mp * heads + h] < H, 0.0, 1.0) for h in range(heads)]
    split = dq_first.shape[0]
    for t in range(tiles):
        spot = slice(t * RB, (t + 1) * RB)
        parts = []
        for h in range(heads):
            lane = slice(h * HD, (h + 1) * HD)
            if t * RB < split:
                dqh = dq_first[spot, lane]
            elif t * RB < base:
                dqh = dq_second[t * RB - split : (t + 1) * RB - split, lane]
            else:
                dqh = dq[t - base // RB][:, lane]
            parts += [dqh, dks[h][t], dvs[h][t] * fresh[h]]
            dvr_ref[h * HD : (h + 1) * HD, spot] = dvs[h][t].T.astype(bf16)
        dm_ref[spot, :] = jnp.concatenate(parts, 1).astype(bf16)


def input_kernel(info, dm_ref, w_ref, unit_ref, na, nb, s0, s1, keep, sums):
    core = info[0]
    cols = dm_ref.shape[1]
    gain = jnp.zeros((1, unit_ref.shape[1]), f32)
    shift = gain
    for own in range(2):
        for half, out in enumerate((s0, s1)):
            at = block(2 * half + (core if own else 1 - core))
            grad = dot_nt(dm_ref[at, :], w_ref[:, :cols])
            gain += jnp.sum(grad * unit_ref[at, :], 0, keepdims=True)
            shift += jnp.sum(grad, 0, keepdims=True)
            if own:
                keep[block(half)] = grad
            else:
                out[...] = grad.astype(bf16)
    sums[...] = na[...] + nb[...]
    sums[0:1] = gain
    sums[1:2] = shift


def to_rows_kernel(info, keep, r0, r1, mine, sent):
    low = info[1] == 0
    first = keep[:RB] + r0[...].astype(f32)
    second = keep[RB:] + r1[...].astype(f32)
    mine[...] = jnp.where(low, first, second)
    sent[...] = jnp.where(low, second, first).astype(bf16)


def output_rows_kernel(info, ka, kb, ga, gb, mine, sent):
    low = info[1] == 0
    at = block(1 - info[0])
    first = ka[...] + ga[at, :].astype(f32)
    second = kb[...] + gb[at, :].astype(f32)
    mine[...] = jnp.where(low, first, second)
    sent[...] = jnp.where(low, second, first).astype(bf16)


def output_kernel(info, ra, rb, mine, received, out):
    at = block(info[0])
    resid = jnp.where(info[1] == 0, ra[at, :], rb[at, :])
    out[...] = (resid + mine[...] + received[...].astype(f32)).astype(bf16)


def qkv_grad_kernel(info, a1_ref, dm_ref, aba, abb, ca, cb, sums, out, fw, bw, turn):
    cols, width = dm_ref.shape[1], sums.shape[1]
    turn[...] = jnp.zeros(turn.shape, f32)
    turn[: sums.shape[0]] = sums[...]

    def step(j):
        at = block(j)
        grad = dot_tn(a1_ref[:, at], dm_ref[...])
        proj = (dot(ca[...], aba[:, at]) + dot(cb[...], abb[:, at])).T
        out[at, : out.shape[1] - LANES] = jnp.concatenate([grad, proj], 1).astype(out.dtype)
        out[at, out.shape[1] - LANES :] = turn[:, at].T.astype(out.dtype)

    for j in range(out.shape[0] // RB):
        step(j)
    starts(info, out, fw, bw)


def norm_one_kernel(info, x_ref, own, received, dra, drb, norm_ref, out):
    unit, scale = norm_stats(x_ref[block(info[2]), :].astype(f32))
    grad = own[...] + received[...].astype(f32)
    dr = jnp.where(info[1] == 0, dra[...], drb[...])
    out[...] = dr + norm_back(unit, scale, norm_ref[0:1], grad)


def first_kernel(heads, info, src, d0, d1, d2, d3, out):
    mp = info[2]
    out[...] = jnp.zeros(out.shape, f32)
    for g in range(heads):
        user = jnp.int32(H)
        for h in range(H):
            user = jnp.where(src[h] == mp * heads + g, h, user)
        held = user // heads
        for r, ref in enumerate((d0, d1, d2, d3)):

            @pl.when((user < H) & (held == mp ^ r))
            def _():
                out[g * HD : (g + 1) * HD, :] = ref[block(user - held * heads, HD), :].astype(f32)


def adamw(master, moment, second, grad, rate, weighted):
    moment_new = 0.9 * moment + 0.1 * grad
    second_new = 0.999 * second + 0.001 * grad * grad
    mean_hat = moment_new / (1.0 - 0.9**ADAM_STEP)
    var_hat = second_new / (1.0 - 0.999**ADAM_STEP)
    master_new = master - rate * (mean_hat / (jnp.sqrt(var_hat) + 1e-08) + weighted * master)
    return (master_new, moment_new, second_new)


def adam_kernel(names, turned, info, full, a, b, *refs):
    ins, outs = refs[:6], refs[6:12]
    rows = a.shape[0]
    grad = a[...].astype(f32) + b[...].astype(f32)
    grad += full[block(info.ring(0), rows), :].astype(f32)
    cols = ins[0].shape[1]
    if turned:
        grad = grad[:, : cols + ins[3].shape[0]]
    second = grad[:, cols:]
    if turned:
        second = jnp.concatenate([second, jnp.zeros((LANES - rows, second.shape[1]), f32)], 0).T[:, :rows]
    for k, (name, part) in enumerate(zip(names, (grad[:, :cols], second))):
        new = adamw(*[r[...] for r in ins[3 * k : 3 * k + 3]], part, RATES[name], 0.1)
        for ref, value in zip(outs[3 * k : 3 * k + 3], new):
            ref[...] = value


def norm_sum_kernel(info, full, a, b, out, turn):
    rows, width = a.shape
    at = slice(width - LANES, width)
    grad = a[:, at].astype(f32) + b[:, at].astype(f32) + full[block(info.ring(0), rows), at].astype(f32)
    turn[...] = jnp.zeros(turn.shape, f32)
    turn[:rows] = grad
    out[...] = turn[...].T[:8]


def norm_adam_kernel(sums, received, w, m, s, w_out, m_out, s_out):
    rows, cols = w.shape
    grad = (sums[...] + received[...])[:rows, :cols]
    new = adamw(w[...], m[...], s[...], grad, RATES["norm"], 0.0)
    for ref, value in zip((w_out, m_out, s_out), new):
        ref[...] = value


def sum_kernel(a, b, out):
    out[...] = a[...] + b[...]


def swap_core(value):
    return lax.ppermute(value, "mp", [(i, i ^ 1) for i in range(4)])


def swap_x(value):
    return lax.ppermute(value, "mp", [(i, i ^ 2) for i in range(4)])


def both_cores(value):
    return lax.all_gather(value, "mp", axis_index_groups=[[0, 1], [2, 3]], axis=0, tiled=True)


FORWARD = [(RING[i], RING[(i + 1) % 8]) for i in range(8)]
BACKWARD = [(b, a) for a, b in FORWARD]


def ahead(value):
    return lax.ppermute(value, "dp", FORWARD)


def behind(value):
    return lax.ppermute(value, "dp", BACKWARD)


def after(value, *others):
    return lax.optimization_barrier((value,) + others)[0]


class Gather:
    def __init__(self, piece, way_a, way_b):
        self.ring = lax.axis_size("dp") == len(RING)
        self.start = self.a = self.b = piece
        self.way_a, self.way_b = way_a, way_b
        self.steps_a, self.steps_b = [], []

    def step_a(self):
        if self.ring:
            self.a = self.way_a(self.a)
            self.steps_a.append(self.a)

    def step_b(self):
        if self.ring:
            self.b = self.way_b(self.b)
            self.steps_b.append(self.b)

    def step(self):
        if self.ring:
            self.a, self.b = lax.optimization_barrier((self.a, self.b))
        self.step_a()
        self.step_b()

    def pieces(self):
        if not self.ring:
            return [lax.all_gather(self.start, "dp", axis=0, tiled=True)]
        return [self.start] + self.steps_a + self.steps_b


class Scatter:
    def __init__(self, name, info, full, fw, bw):
        self.ring = lax.axis_size("dp") == len(RING)
        self.name, self.info, self.full, self.a, self.b = name, info, full, fw, bw
        self.steps = 0

    def step(self, *gates):
        if not self.ring:
            return
        self.a = after(self.a, *gates)
        k = 4 - self.steps
        shape = (self.a.shape, bf16)
        if k in (3, 2):
            kernel = functools.partial(hop_kernel, k, 1 - k)
            self.a, self.b = call(kernel, f"{self.name}_hop{k}", (self.info,), [self.full, self.a, self.b], [shape] * 2)
        if k == 1:
            (self.a,) = call(hop_last_kernel, f"{self.name}_hop1", (self.info,), [self.full, self.a], [shape])
        self.last = self.a
        self.a = ahead(self.a)
        if k > 1:
            self.b = behind(self.b)
        self.steps += 1

    def ends(self):
        return (self.a, self.b) if self.ring else None


def update(name, info, full, ends, firsts, seconds, turned):
    first, second = name
    outs = [(w.shape, f32) for w in firsts + seconds]
    if ends is not None:
        new = call(
            functools.partial(adam_kernel, name, turned),
            f"adam_{first}",
            (info,),
            [full, *ends, *firsts, *seconds],
            outs,
        )
        return tuple(new[:3]), tuple(new[3:])
    grad = lax.psum_scatter(full.astype(f32), "dp", scatter_dimension=0, tiled=True)
    cols = firsts[0].shape[1]
    other = grad[:, cols : cols + seconds[0].shape[0 if turned else 1]]
    return (
        adamw(*firsts, grad[:, :cols], RATES[first], 0.1),
        adamw(*seconds, other.T if turned else other, RATES[second], 0.1),
    )


def local(
    tokens_in,
    first_values,
    skip_source,
    grad_out,
    qkv_weight,
    proj_weight,
    fc_weight,
    down_weight,
    norm_params,
    qkv_moment,
    proj_moment,
    fc_moment,
    down_moment,
    norm_moment,
    qkv_second,
    proj_second,
    fc_second,
    down_second,
    norm_second,
):
    n = lax.axis_size("dp")
    ring = n == len(RING)
    pieces = n if ring else 1
    count, width = tokens_in.shape
    cols = qkv_weight.shape[1]
    heads = cols // (3 * HD)
    cw = heads * HD
    hid = fc_weight.shape[1]
    wide = -(-(cols + 4) // LANES) * LANES
    half = count // 2
    shard = qkv_weight.shape[0]
    info = HERE
    src = skip_source

    if ring:
        (ring_one,) = call(
            prep_one_kernel,
            "prep_one",
            (),
            [qkv_weight, norm_params, proj_weight],
            [((shard, wide + cw + LANES // 2), bf16)],
            scratch=[
                pltpu.VMEM((shard, cols), f32),
                pltpu.VMEM(norm_params.shape, f32),
                pltpu.VMEM((cw, shard), f32),
                pltpu.VMEM((LANES, LANES), f32),
                pltpu.VMEM((cw, LANES), f32),
                pltpu.SemaphoreType.DMA((3,)),
            ],
            vmem=60,
            far=True,
        )
        ring_one, fc_late = lax.optimization_barrier((ring_one, fc_weight))
        (ring_two,) = call(
            prep_two_kernel,
            "prep_two",
            (),
            [fc_late, down_weight.T],
            [((shard, 2 * hid), bf16)],
            scratch=[pltpu.VMEM((shard, hid), f32)] * 2 + [pltpu.SemaphoreType.DMA((2,))],
            vmem=56,
            far=True,
        )
    else:
        blank = jnp.zeros((shard, wide - cols - 4), bf16)
        ring_one = jnp.concatenate(
            [qkv_weight.astype(bf16), norm_params.T.astype(bf16), blank, proj_weight.T.astype(bf16)], 1
        )
        ring_two = jnp.concatenate([fc_weight.astype(bf16), down_weight.T.astype(bf16)], 1)
    fence = lambda *values: lax.optimization_barrier(values)
    fence = lambda *values: lax.optimization_barrier(values)
    one, two = Gather(ring_one, ahead, behind), Gather(ring_two, behind, ahead)
    one.step()
    ring_two, first_t = fence(ring_two, first_values.T)
    first_x, first_c = swap_x(first_t), swap_core(first_t)
    one.a, one.b, tokens, ring_two = fence(one.a, one.b, tokens_in, ring_two)
    two.start = two.a = two.b = ring_two
    one.step()
    (unit_one,) = call(unit_kernel, "unit", (), [tokens], [((count, width), f32)])
    one.a, one.b, unit_one = fence(one.a, one.b, unit_one)
    one.step()
    one.a, one.b, two.a, first_x = fence(one.a, one.b, two.a, first_x)
    if ring:
        one.steps_b[-1] = one.b
    one.step_a()
    two.step_a()
    one_last, unit_one, two.a, two.b = fence(one.a, unit_one, two.a, two.b)
    if ring:
        one.steps_a[-1] = one_last
    two.step()
    first_xc = swap_core(first_x)

    a1, mixed, fresh, qkv_full, norms, own_w = call(
        functools.partial(qkv_kernel, pieces, heads),
        "qkv",
        (info,),
        [unit_one, *one.pieces()],
        [
            ((count, width), bf16),
            ((count, cols), bf16),
            ((cw, count), bf16),
            ((width, wide), bf16),
            ((8, width), f32),
            ((cw + 16, width), bf16),
        ],
        scratch=[pltpu.VMEM((width, cw), bf16)],
    )
    (values,) = call(
        functools.partial(values_kernel, heads),
        "values",
        (info, src),
        [fresh, first_t, first_c, first_x, first_xc],
        [((cw, count), bf16)],
    )
    across_w = swap_x(own_w)

    def attend(part, mixed):
        return call(
            functools.partial(attend_kernel, heads, part * half),
            f"attend{part}",
            (),
            [mixed, values],
            [((cw, half), bf16), ((8, half), f32)],
        )

    ctx_a, lse_a = attend(0, mixed)
    two.a, two.b, ctx_a, mixed, own_w = fence(two.a, two.b, ctx_a, mixed, own_w)
    two.step()
    xa = swap_x(ctx_a)
    ctx_b, lse_b = attend(1, mixed)
    cores_w = both_cores(own_w)
    two.a, two.b, across_w, xa, ctx_b, grad_out, cores_w = fence(
        two.a, two.b, across_w, xa, ctx_b, grad_out, cores_w
    )
    two.step()
    xb, ca, cb = swap_x(ctx_b), swap_core(ctx_a), swap_core(ctx_b)
    (grad_out,) = call(
        fetch_kernel,
        "fetch",
        (),
        [grad_out],
        [(grad_out.shape, bf16)],
        scratch=[pltpu.SemaphoreType.DMA],
        vmem=4,
        far=True,
    )
    far_w, xca = both_cores(across_w), both_cores(xa)
    start, far_w, xca, xb, ca, cb, two.a, two.b, grad_out = fence(
        two.start, far_w, xca, xb, ca, cb, two.a, two.b, grad_out
    )
    xcb = swap_core(xb)
    lse = lse_a, lse_b
    wf, wd = call(
        functools.partial(assemble_kernel, pieces),
        "assemble",
        (info,),
        [start, *two.pieces()[1:]] if ring else two.pieces(),
        [((width, hid), bf16)] * 2,
    )
    pair = own_w, cores_w, across_w, far_w

    def mlp(part, norms, contexts):
        return call(
            functools.partial(mlp_kernel, part),
            f"mlp{part}",
            (info,),
            [tokens, norms, *contexts, *pair, wf],
            [
                ((half, width), f32),
                ((half, width), f32),
                ((half, width), bf16),
                ((half, hid), bf16),
                ((half, hid), f32),
            ],
        )

    def mlp_back(part, grad):
        return call(
            functools.partial(mlp_back_kernel, part),
            f"mlp_back{part}",
            (info,),
            [grad, unit_two[part], slope[part], wf, wd],
            [((half, hid), bf16)] + [((RB // 2, width), bf16)] * 2 + [((RB, width), f32), ((8, width), f32)],
        )

    def mlp_out(part, act):
        return call(
            mlp_out_kernel, f"mlp_out{part}", (info,), [act, wd], [((RB, width), bf16), ((RB, width), f32)]
        )

    def add(part, keep, *received):
        return call(add_kernel, f"add{part}", (), [keep, *received], [((RB, width), bf16)])[0]

    first_r, *forward_a = mlp(0, norms, (ctx_a, ca, xa, xca))
    norms, first_r = fence(norms, first_r)
    forward_b = mlp(1, norms, (ctx_b, cb, xb, xcb))
    resid, unit_two, a2, act, slope = zip((first_r, *forward_a), forward_b)
    dpre_a, top_a, bottom_a, dkeep_a, nacc_a = mlp_back(0, after(grad_out, act[1]))
    received_a = swap_core(top_a), swap_core(bottom_a)
    dpre_b, top_b, bottom_b, dkeep_b, nacc_b = mlp_back(1, after(grad_out, dpre_a))
    mine_a = add(0, after(dkeep_a, dpre_b), *received_a)
    received_b = swap_core(top_b), swap_core(bottom_b)
    across_a = swap_x(mine_a)

    piece = lambda w: [((width // pieces if ring else 16, w), bf16)] * 2
    mlp_grad, mlp_fw, mlp_bw = call(
        mlp_grad_kernel,
        "mlp_grad",
        (info,),
        [after(a2[0], mine_a), a2[1], dpre_a, dpre_b, grad_out, act[0], act[1]],
        [((width, 2 * hid), bf16 if ring else f32)] + piece(2 * hid),
    )
    mlp_sum = Scatter("mlp", info, mlp_grad, mlp_fw, mlp_bw)
    mlp_sum.step()
    mine_b = add(1, after(dkeep_b, mlp_grad), *received_b)
    def norm_two(part, mine, across):
        return call(
            functools.partial(norm_two_kernel, part),
            f"norm_two{part}",
            (info,),
            [resid[part], mine, across, grad_out, norms],
            [((RB, width), f32)] + [((RB // 2, width), bf16)] * 2,
        )

    def attend_back(stage, base, blocks, given, part, before, outs):
        return call(
            functools.partial(attend_back_kernel, heads, base, blocks, stage),
            f"attend_back{stage}",
            (info, src),
            [mixed, values, *given, own_w, lse[part], (ctx_a, ctx_b)[part], *before],
            outs,
            vmem=24,
        )

    across_b = swap_x(mine_b)
    dr_a, *ab_a = norm_two(0, mine_a, across_a)
    partner = [swap_core(v) for v in ab_a]
    ab_one, dq_a, dk, dv = attend_back(
        0, 0, 2, [*ab_a, *partner], 0, [], [((half, width), bf16)] + [((half, cw), f32)] * 3
    )
    mlp_sum.a, mlp_sum.b, dq_a = fence(mlp_sum.a, mlp_sum.b, dq_a)
    mlp_sum.step()
    dr_b, *ab_b = norm_two(1, mine_b, across_b)
    partner = [swap_core(v) for v in ab_b]
    top = half + RB
    ab_two, dq_b, dk, dv = attend_back(
        1, half, 1, [*ab_b, *partner], 1, [dk, dv], [((half, width), bf16), ((RB, cw), f32)] + [((top, cw), f32)] * 2
    )
    mlp_sum.a, mlp_sum.b, dq_b = fence(mlp_sum.a, mlp_sum.b, dq_b)
    mlp_sum.step()
    dmixed, dreused = attend_back(
        2,
        top,
        1,
        [ab_two],
        1,
        [after(dk, mlp_sum.last) if ring else dk, dv, dq_a, dq_b],
        [((count, cols), bf16), ((cw, count), bf16)],
    )

    *isend, ikeep, sums = call(
        input_kernel,
        "input",
        (info,),
        [dmixed, qkv_full, unit_one, nacc_a, nacc_b],
        [((RB, width), bf16)] * 2 + [((half, width), f32), ((8, width), f32)],
    )
    qkv_grad, qkv_fw, qkv_bw = call(
        qkv_grad_kernel,
        "qkv_grad",
        (info,),
        [a1, dmixed, ab_one, ab_two, ctx_a, ctx_b, sums],
        [((width, cols + cw + LANES), bf16 if ring else f32)] + piece(cols + cw + LANES),
        scratch=[pltpu.VMEM((LANES, width), f32)],
    )
    qkv_sum = Scatter("qkv", info, qkv_grad, qkv_fw, qkv_bw)
    mlp_sum.a, mlp_sum.b, qkv_sum.a, qkv_sum.b, *act = fence(mlp_sum.a, mlp_sum.b, qkv_sum.a, qkv_sum.b, *act)
    mlp_sum.step()
    qkv_sum.step()
    gathered = [swap_core(v) for v in isend]
    mine, sent = call(
        to_rows_kernel, "to_rows", (info,), [ikeep, *gathered], [((RB, width), f32), ((RB, width), bf16)]
    )
    across, dx = swap_x(sent), swap_x(dreused)
    ysend_a, ykeep_a = mlp_out(0, act[0])
    ysend_b, ykeep_b = mlp_out(1, act[1])
    qkv_sum.a, qkv_sum.b, sent, ysend_a, ysend_b = fence(qkv_sum.a, qkv_sum.b, sent, ysend_a, ysend_b)
    qkv_sum.step()
    rows_mine, rows_sent = call(
        output_rows_kernel,
        "output_rows",
        (info,),
        [ykeep_a, ykeep_b, both_cores(ysend_a), both_cores(ysend_b)],
        [((RB, width), f32), ((RB, width), bf16)],
    )
    qkv_sum.a, qkv_sum.b, mlp_sum.a, rows_sent = fence(qkv_sum.a, qkv_sum.b, mlp_sum.a, rows_sent)
    qkv_sum.step()
    rows_received = swap_x(rows_sent)
    fc_new, down_new = update(
        ("fc", "down"),
        info,
        mlp_grad,
        mlp_sum.ends(),
        [fc_weight, fc_moment, fc_second],
        [down_weight.T, down_moment.T, down_second.T],
        False,
    )
    qkv_sum.a, qkv_sum.b, across, dx, *fc_new = fence(qkv_sum.a, qkv_sum.b, across, dx, *fc_new)
    down_new = tuple(v.T for v in down_new)
    qkv_sum.step()
    (input_grad,) = call(
        norm_one_kernel,
        "norm_one",
        (info,),
        [tokens, mine, across, dr_a, dr_b, norms],
        [((RB, width), f32)],
    )
    dx, dreused = fence(dx, dreused)
    dc, dxc = swap_core(dreused), swap_core(dx)
    (first_grad,) = call(
        functools.partial(first_kernel, heads),
        "first",
        (info, src),
        [dreused, dc, dx, dxc],
        [((cw, count), f32)],
    )
    qkv_sum.a, input_grad, first_grad = fence(qkv_sum.a, input_grad, first_grad)
    if ring:
        (sums,) = call(
            norm_sum_kernel,
            "norm_sum",
            (info,),
            [qkv_grad, *qkv_sum.ends()],
            [((8, LANES), f32)],
            scratch=[pltpu.VMEM((LANES, LANES), f32)],
        )
        (sums,) = call(sum_kernel, "sum", (), [sums, swap_core(sums)], [(sums.shape, f32)])
        received = swap_x(sums)
    qkv_new, proj_new = update(
        ("qkv", "proj"),
        info,
        qkv_grad,
        qkv_sum.ends(),
        [qkv_weight, qkv_moment, qkv_second],
        [proj_weight, proj_moment, proj_second],
        True,
    )
    late, *qkv_new = fence(rows_received, *qkv_new)
    (block_out,) = call(
        output_kernel,
        "output",
        (info,),
        [resid[0], resid[1], rows_mine, late],
        [((RB, width), bf16)],
    )
    if ring:
        received, block_out = fence(received, block_out)
        norm_new = call(
            norm_adam_kernel,
            "adam_norm",
            (),
            [sums, received, norm_params, norm_moment, norm_second],
            [(norm_params.shape, f32)] * 3,
        )
    else:
        own = lax.psum_scatter(lax.psum(sums, "mp"), "dp", scatter_dimension=1, tiled=True)[:4]
        norm_new = adamw(norm_params, norm_moment, norm_second, own, RATES["norm"], 0.0)
    return (block_out, input_grad, first_grad.T, *qkv_new, *proj_new, *fc_new, *down_new, *norm_new)


def solution(mesh):
    both = P("dp", "mp")
    turned = P("mp", "dp")
    rows = P("dp", None)
    every = P(None, "dp")
    state = (both, turned, both, turned, every)
    return jax.shard_map(
        local,
        mesh=mesh,
        in_specs=(rows, both, P(), rows) + state * 3,
        out_specs=(P(("dp", "mp"), None), P(("dp", "mp"), None), both)
        + (both,) * 3
        + (turned,) * 3
        + (both,) * 3
        + (turned,) * 3
        + (every,) * 3,
        check_vma=False,
    )
```

```python
import functools

import jax
import jax.numpy as jnp
import numpy as np
from jax import lax
from jax.experimental import pallas as pl
from jax.experimental.pallas import tpu as pltpu
from jax.sharding import PartitionSpec as P

H = 12
HD = 64
ADAM_STEP = 5
EPS = 1e-05
MASKED = -1e30
RB = 256
LANES = 128
RING = (0, 2, 4, 6, 7, 5, 3, 1)
OFFSETS = (0, -1, -2, -3, -4, 1, 2, 3)
GELU_A = 0.7978845608028654
GELU_B = 0.044715
RATES = {"qkv": 0.06, "proj": 0.15, "fc": 0.04, "down": 0.03, "norm": 0.3}

bf16 = jnp.bfloat16
f32 = jnp.float32


def dot(a, b):
    return jnp.dot(a, b, preferred_element_type=f32)


def dot_nt(a, b):
    return lax.dot_general(a, b, (((1,), (1,)), ((), ())), preferred_element_type=f32)


def dot_tn(a, b):
    return lax.dot_general(a, b, (((0,), (0,)), ((), ())), preferred_element_type=f32)


class Place:
    def __init__(self):
        self.mp, self.dp = lax.axis_index("mp"), lax.axis_index("dp")

    def __getitem__(self, k):
        if k < 4:
            return (self.mp % 2, self.mp // 2, self.mp, self.dp)[k]
        if lax.axis_size("dp") != len(RING):
            return 0
        z, y = self.dp // 2, self.dp % 2
        at = (jnp.where(y == 0, z, 7 - z) + OFFSETS[k - 4] + 8) % 8
        return jnp.where(at < 4, 2 * at, 2 * (7 - at) + 1)


HERE = object()


def call(kernel, name, scalars, ins, outs, scratch=(), vmem=16, far=False):
    if HERE in scalars:
        inner = kernel
        kernel = lambda *refs: inner(Place(), *refs)
        scalars = scalars[1:]
    smem = pl.BlockSpec(memory_space=pltpu.SMEM)
    full = pl.BlockSpec(memory_space=pltpu.VMEM)
    given = pl.BlockSpec(memory_space=pltpu.HBM) if far else full
    return pl.pallas_call(
        kernel,
        in_specs=[smem] * len(scalars) + [given] * len(ins),
        out_specs=[full] * len(outs),
        out_shape=[jax.ShapeDtypeStruct(sh, dt) for sh, dt in outs],
        scratch_shapes=list(scratch),
        compiler_params=pltpu.CompilerParams(vmem_limit_bytes=vmem * 1024 * 1024),
        cost_estimate=pl.CostEstimate(flops=1, bytes_accessed=1, transcendentals=0),
        name=name,
    )(*scalars, *ins)


def block(index, size=RB):
    if isinstance(index, int):
        return slice(index * size, (index + 1) * size)
    return pl.ds(pl.multiple_of(index * size, size), size)


def fetch(pairs, sems):
    copies = [pltpu.make_async_copy(src, dst, sems.at[k]) for k, (src, dst) in enumerate(pairs)]
    for copy in copies:
        copy.start()
    for copy in copies:
        copy.wait()


def prep_one_kernel(q_ref, n_ref, out, q, norms, turn, sems):
    rows, cols = q.shape
    turn[...] = jnp.zeros(turn.shape, f32)
    fetch([(q_ref, q), (n_ref, norms)], sems)
    turn[: norms.shape[0], :rows] = norms[...]
    out[:, :cols] = q[...].astype(bf16)
    out[:, cols:] = turn[...].T[:rows, : out.shape[1] - cols].astype(bf16)


def prep_two_kernel(p_ref, f_ref, d_ref, proj, fc, down, p, f, d, turn, sems):
    rows = proj.shape[0]
    turn[...] = jnp.zeros(turn.shape, f32)
    fetch([(p_ref, p), (f_ref, f), (d_ref, d)], sems)
    turn[:, :rows] = p[...]
    proj[...] = turn[...].T[:rows].astype(bf16)
    fc[...] = f[...].astype(bf16)
    down[...] = d[...].astype(bf16)


def join_kernel(f_ref, own, across, out):
    hid, cw = f_ref.shape[1], own.shape[1]
    out[:, :hid] = f_ref[...]
    out[:, hid:] = jnp.concatenate([own[...], across[...]], 1)


def norm_stats(values):
    center = values - jnp.mean(values, axis=-1, keepdims=True)
    scale = lax.rsqrt(jnp.mean(center * center, axis=-1, keepdims=True) + EPS)
    return center * scale, scale


def unit_kernel(x_ref, unit_ref):
    for i in range(x_ref.shape[0] // RB):
        at = slice(i * RB, (i + 1) * RB)
        unit_ref[at] = norm_stats(x_ref[at].astype(f32))[0]


def fetch_kernel(src, out, sem):
    copy = pltpu.make_async_copy(src, out, sem)
    copy.start()
    copy.wait()


def loop(count, body):
    lax.fori_loop(0, count, lambda i, carry: (body(i), carry)[1], 0)


def qkv_kernel(n, heads, info, unit_ref, *refs):
    pieces, (a1_ref, m_ref, v_ref, w_ref, norm_ref) = refs[:n], refs[n:]
    cols = m_ref.shape[1]
    base = cols // LANES * LANES
    rows = w_ref.shape[0] // n
    for k, piece in enumerate(pieces):
        w_ref[block(info[4 + k], rows), :] = piece[...]
    turned = w_ref[:, base : base + LANES].astype(f32).T
    norm_ref[...] = turned[cols - base : cols - base + 8]

    def step(i):
        at = block(i)
        a1 = (unit_ref[at, :] * norm_ref[0:1] + norm_ref[1:2]).astype(bf16)
        a1_ref[at, :] = a1
        mixed = dot(a1, w_ref[:, :cols])
        m_ref[at, :] = mixed.astype(bf16)
        for h in range(heads):
            fresh = mixed[:, (3 * h + 2) * HD : (3 * h + 3) * HD]
            v_ref[h * HD : (h + 1) * HD, at] = fresh.T.astype(bf16)

    loop(m_ref.shape[0] // RB, step)


def values_kernel(heads, info, src, fresh, f0, f1, f2, f3, v_ref):
    mp = info[2]
    for h in range(heads):
        source = src[mp * heads + h]
        held = source // heads
        mine = slice(h * HD, (h + 1) * HD)

        @pl.when(source >= H)
        def _():
            v_ref[mine, :] = fresh[mine, :]

        for r, first in enumerate((f0, f1, f2, f3)):

            @pl.when((source < H) & (held == mp ^ r))
            def _():
                v_ref[mine, :] = first[block(source - held * heads, HD), :]


def masked_tile():
    keys = lax.broadcasted_iota(jnp.int32, (RB, RB), 0)
    queries = lax.broadcasted_iota(jnp.int32, (RB, RB), 1)
    return keys <= queries


def attend_kernel(heads, base, m_ref, v_ref, c_ref, lse_ref):
    keep = masked_tile()
    blocks = c_ref.shape[0] // RB
    turned = [[None] * heads for _ in range(blocks)]
    lse_ref[...] = jnp.zeros(lse_ref.shape, f32)
    for h in range(heads):
        top = base + blocks * RB
        keys = m_ref[:top, (3 * h + 1) * HD : (3 * h + 2) * HD]
        values_t = v_ref[h * HD : (h + 1) * HD, :top]
        for i in range(blocks):
            lo = base + i * RB
            hi = lo + RB
            query = m_ref[lo:hi, 3 * h * HD : (3 * h + 1) * HD] * bf16(HD**-0.5)
            diag = jnp.where(keep, dot_nt(keys[lo:hi], query), MASKED)
            peak = jnp.max(diag, 0, keepdims=True)
            if lo:
                left = dot_nt(keys[:lo], query)
                peak = jnp.maximum(peak, jnp.max(left, 0, keepdims=True))
            diag = jnp.exp(diag - peak)
            total = jnp.sum(diag, 0, keepdims=True)
            if lo:
                left = jnp.exp(left - peak)
                total += jnp.sum(left, 0, keepdims=True)
            inverse = 1.0 / total
            context = dot(values_t[:, lo:hi], (diag * inverse).astype(bf16))
            if lo:
                context += dot(values_t[:, :lo], (left * inverse).astype(bf16))
            turned[i][h] = context
            lse_ref[h : h + 1, i * RB : (i + 1) * RB] = peak + jnp.log(total)
    for i in range(blocks):
        c_ref[i * RB : (i + 1) * RB] = jnp.concatenate(turned[i], 0).T.astype(bf16)


def assemble_two_kernel(n, info, *refs):
    pieces, (wf, own, across, turn) = refs[:n], refs[n:]
    width, hid = wf.shape
    cw = own.shape[0]
    rows = width // n
    for k, piece in enumerate(pieces):
        at = block(info[4 + k], rows)
        wf[at, :] = piece[:, :hid]
        turn[at, :] = piece[:, hid:]
    pair = turn[...].T
    own[...] = pair[:cw]
    across[...] = pair[cw:]


def assemble_three_kernel(n, info, *refs):
    pieces, (wd,) = refs[:n], refs[n:]
    rows = wd.shape[0] // n
    for k, piece in enumerate(pieces):
        wd[block(info[4 + k], rows), :] = piece[...]


def mlp_kernel(part, x_ref, norm_ref, c0, c1, c2, c3, w0, w1, w2, w3, wf, r_ref, unit_ref, a2_ref, g_ref, slope_ref):
    def step(i):
        at = block(i)
        resid = x_ref[block(2 * part + i), :].astype(f32) + (
            (dot(c0[at, :], w0[...]) + dot(c1[at, :], w1[...]))
            + (dot(c2[at, :], w2[...]) + dot(c3[at, :], w3[...]))
        )
        r_ref[at, :] = resid
        unit, _ = norm_stats(resid)
        unit_ref[at, :] = unit
        a2 = (unit * norm_ref[2:3] + norm_ref[3:4]).astype(bf16)
        a2_ref[at, :] = a2
        u = dot(a2, wf[...])
        square = u * u
        t = jnp.tanh(GELU_A * u * (1.0 + GELU_B * square))
        g_ref[at, :] = (0.5 * u * (1.0 + t)).astype(bf16)
        slope_ref[at, :] = 0.5 * (1.0 + t) + 0.5 * u * (1.0 - t * t) * (
            GELU_A * (1.0 + 3.0 * GELU_B * square)
        )

    loop(2, step)


def mlp_back_kernel(part, info, e_ref, unit_ref, slope_ref, wf, wd, du_ref, top, bottom, keep, nacc):
    core = info[0]
    nacc[...] = jnp.zeros(nacc.shape, f32)

    def step(i):
        spot = core if i else 1 - core
        at = block(spot)
        du = (dot(e_ref[block(2 * part + spot), :], wd[...]) * slope_ref[at, :]).astype(bf16)
        du_ref[at, :] = du
        grad = dot_nt(du, wf[...])
        nacc[2:3] += jnp.sum(grad * unit_ref[at, :], 0, keepdims=True)
        nacc[3:4] += jnp.sum(grad, 0, keepdims=True)
        keep[...] = grad

        @pl.when(i < 1)
        def _():
            top[...] = grad[: RB // 2].astype(bf16)
            bottom[...] = grad[RB // 2 :].astype(bf16)

    for i in range(2):
        step(i)


def mlp_out_kernel(info, g_ref, wd, ysend, ykeep):
    ykeep[...] = dot_nt(g_ref[block(info[0]), :], wd[...])
    ysend[...] = dot_nt(g_ref[block(1 - info[0]), :], wd[...]).astype(bf16)


def add_kernel(keep, top, bottom, out):
    out[: RB // 2] = (keep[: RB // 2] + top[...].astype(f32)).astype(bf16)
    out[RB // 2 :] = (keep[RB // 2 :] + bottom[...].astype(f32)).astype(bf16)


def starts(info, full, fw, bw):
    rows = fw.shape[0]
    fw[...] = full[block(info[4 + OFFSETS.index(-4)], rows), :].astype(bf16)
    bw[...] = full[block(info[4 + OFFSETS.index(-3)], rows), :].astype(bf16)


def mlp_grad_kernel(info, a2a, a2b, dua, dub, e_ref, ga, gb, out, fw, bw):
    hid = dua.shape[1]
    half = dua.shape[0]

    def step(j):
        at = block(j)
        out[at, :hid] = (dot_tn(a2a[:, at], dua[...]) + dot_tn(a2b[:, at], dub[...])).astype(out.dtype)
        out[at, hid:] = (dot_tn(e_ref[:half, at], ga[...]) + dot_tn(e_ref[half:, at], gb[...])).astype(out.dtype)

    for j in range(out.shape[0] // RB):
        step(j)
    starts(info, out, fw, bw)


def hop_kernel(ahead, behind, info, full, a, b, a_out, b_out):
    rows = a.shape[0]
    for offset, value, out in ((ahead, a, a_out), (behind, b, b_out)):
        term = full[block(info[4 + OFFSETS.index(offset)], rows), :]
        out[...] = (value[...].astype(f32) + term.astype(f32)).astype(bf16)


def hop_last_kernel(info, full, a, a_out):
    term = full[block(info[4 + OFFSETS.index(1)], a.shape[0]), :]
    a_out[...] = (a[...].astype(f32) + term.astype(f32)).astype(bf16)


def norm_back(unit, scale, gain, grad):
    dy = grad * gain
    return scale * (
        dy - jnp.mean(dy, -1, keepdims=True) - unit * jnp.mean(dy * unit, -1, keepdims=True)
    )


def norm_two_kernel(part, info, r_ref, own, received, e_ref, norm_ref, dr_ref, top, bottom):
    unit, scale = norm_stats(r_ref[block(info[0]), :])
    grad = own[...].astype(f32) + received[...].astype(f32)
    e = e_ref[block(2 * part + info[0]), :].astype(f32)
    dr = e + norm_back(unit, scale, norm_ref[2:3], grad)
    dr_ref[...] = dr
    top[...] = dr[: RB // 2].astype(bf16)
    bottom[...] = dr[RB // 2 :].astype(bf16)


def attend_back_kernel(heads, base, blocks, stage, info, src, m_ref, v_ref, *refs):
    if stage < 2:
        halves, refs = refs[:4], refs[4:]
    else:
        ab_in, refs = refs[0], refs[1:]
    wp, lse_ref, c_ref, *refs = refs
    if stage:
        dk_in, dv_in, *refs = refs
    if stage == 0:
        ab_ref, dq_ref, dk_ref, dv_ref = refs
    elif stage == 1:
        ab_ref, dq_ref, dk_ref, dv_ref = refs
    else:
        dq_first, dq_second, dm_ref, dvr_ref = refs
    keep = masked_tile()
    core = info[0]
    if stage < 2:
        for k in range(2):
            ab_ref[block(2 * core + k, RB // 2), :] = halves[k][...]
            ab_ref[block(2 * (1 - core) + k, RB // 2), :] = halves[2 + k][...]
        source, skip = ab_ref, 0
    else:
        source, skip = ab_in, ab_in.shape[0] - blocks * RB
    top = base + blocks * RB
    tiles = top // RB
    dctx = [dot_nt(source[skip + i * RB : skip + (i + 1) * RB], wp[...]).astype(bf16) for i in range(blocks)]
    first = c_ref.shape[0] - blocks * RB if stage == 2 else 0
    own_rows = [slice(first + i * RB, first + (i + 1) * RB) for i in range(blocks)]
    terms = [(d.astype(f32) * c_ref[at].astype(f32)).T for d, at in zip(dctx, own_rows)]
    dq_t = [[None] * heads for _ in range(blocks)]
    dks, dvs = [], []
    for h in range(heads):
        lane = slice(h * HD, (h + 1) * HD)
        keys = m_ref[:top, (3 * h + 1) * HD : (3 * h + 2) * HD]
        keys_t = keys.T
        values = v_ref[h * HD : (h + 1) * HD, :top].T
        dk = [None] * tiles
        dv = [None] * tiles
        if stage:
            for t in range(base // RB):
                dk[t] = dk_in[t * RB : (t + 1) * RB, lane]
                dv[t] = dv_in[t * RB : (t + 1) * RB, lane]
        for i in range(blocks):
            lo = base + i * RB
            hi = lo + RB
            query = m_ref[lo:hi, 3 * h * HD : (3 * h + 1) * HD] * bf16(HD**-0.5)
            dc = dctx[i][:, lane]
            lse = lse_ref[h : h + 1, own_rows[i]]
            prob = jnp.exp(dot_nt(keys[:hi], query) - lse)
            own = jnp.where(keep, prob[lo:], 0.0)
            prob = jnp.concatenate([prob[:lo], own], 0) if lo else own
            dprob = dot_nt(values[:hi], dc)
            inner = jnp.sum(terms[i][lane], 0, keepdims=True)
            more_v = dot(prob.astype(bf16), dc)
            ds = (prob * (dprob - inner)).astype(bf16)
            more_k = dot(ds, query)
            dq_t[i][h] = dot(keys_t[:, :hi], ds) * HD**-0.5
            for t in range(hi // RB):
                spot = slice(t * RB, (t + 1) * RB)
                dv[t] = more_v[spot] if dv[t] is None else dv[t] + more_v[spot]
                dk[t] = more_k[spot] if dk[t] is None else dk[t] + more_k[spot]
        dks.append(dk)
        dvs.append(dv)
    dq = [jnp.concatenate(dq_t[i], 0).T for i in range(blocks)]
    if stage < 2:
        for i in range(blocks):
            dq_ref[i * RB : (i + 1) * RB] = dq[i]
        for t in range(tiles):
            dk_ref[t * RB : (t + 1) * RB] = jnp.concatenate([dks[h][t] for h in range(heads)], 1)
            dv_ref[t * RB : (t + 1) * RB] = jnp.concatenate([dvs[h][t] for h in range(heads)], 1)
        return
    mp = info[2]
    fresh = [jnp.where(src[mp * heads + h] < H, 0.0, 1.0) for h in range(heads)]
    split = dq_first.shape[0]
    for t in range(tiles):
        spot = slice(t * RB, (t + 1) * RB)
        parts = []
        for h in range(heads):
            lane = slice(h * HD, (h + 1) * HD)
            if t * RB < split:
                dqh = dq_first[spot, lane]
            elif t * RB < base:
                dqh = dq_second[t * RB - split : (t + 1) * RB - split, lane]
            else:
                dqh = dq[t - base // RB][:, lane]
            parts += [dqh, dks[h][t], dvs[h][t] * fresh[h]]
            dvr_ref[h * HD : (h + 1) * HD, spot] = dvs[h][t].T.astype(bf16)
        dm_ref[spot, :] = jnp.concatenate(parts, 1).astype(bf16)


def input_kernel(info, dm_ref, w_ref, unit_ref, na, nb, s0, s1, keep, sums):
    core = info[0]
    cols = dm_ref.shape[1]
    gain = jnp.zeros((1, unit_ref.shape[1]), f32)
    shift = gain
    for own in range(2):
        for half, out in enumerate((s0, s1)):
            at = block(2 * half + (core if own else 1 - core))
            grad = dot_nt(dm_ref[at, :], w_ref[:, :cols])
            gain += jnp.sum(grad * unit_ref[at, :], 0, keepdims=True)
            shift += jnp.sum(grad, 0, keepdims=True)
            if own:
                keep[block(half)] = grad
            else:
                out[...] = grad.astype(bf16)
    sums[...] = na[...] + nb[...]
    sums[0:1] = gain
    sums[1:2] = shift


def to_rows_kernel(info, keep, r0, r1, mine, sent):
    low = info[1] == 0
    first = keep[:RB] + r0[...].astype(f32)
    second = keep[RB:] + r1[...].astype(f32)
    mine[...] = jnp.where(low, first, second)
    sent[...] = jnp.where(low, second, first).astype(bf16)


def output_rows_kernel(info, ka, kb, ra, rb, mine, sent):
    low = info[1] == 0
    first = ka[...] + ra[...].astype(f32)
    second = kb[...] + rb[...].astype(f32)
    mine[...] = jnp.where(low, first, second)
    sent[...] = jnp.where(low, second, first).astype(bf16)


def output_kernel(info, ra, rb, mine, received, out):
    at = block(info[0])
    resid = jnp.where(info[1] == 0, ra[at, :], rb[at, :])
    out[...] = (resid + mine[...] + received[...].astype(f32)).astype(bf16)


def qkv_grad_kernel(info, a1_ref, dm_ref, aba, abb, ca, cb, sums, out, fw, bw, turn):
    cols, width = dm_ref.shape[1], sums.shape[1]
    turn[...] = jnp.zeros(turn.shape, f32)
    turn[: sums.shape[0]] = sums[...]

    def step(j):
        at = block(j)
        grad = dot_tn(a1_ref[:, at], dm_ref[...])
        proj = dot_tn(aba[:, at], ca[...]) + dot_tn(abb[:, at], cb[...])
        out[at, : out.shape[1] - LANES] = jnp.concatenate([grad, proj], 1).astype(out.dtype)
        out[at, out.shape[1] - LANES :] = turn[:, at].T.astype(out.dtype)

    for j in range(out.shape[0] // RB):
        step(j)
    starts(info, out, fw, bw)


def norm_one_kernel(info, x_ref, own, received, dra, drb, norm_ref, out):
    unit, scale = norm_stats(x_ref[block(info[2]), :].astype(f32))
    grad = own[...] + received[...].astype(f32)
    dr = jnp.where(info[1] == 0, dra[...], drb[...])
    out[...] = dr + norm_back(unit, scale, norm_ref[0:1], grad)


def first_kernel(heads, info, src, d0, d1, d2, d3, out):
    mp = info[2]
    out[...] = jnp.zeros(out.shape, f32)
    for g in range(heads):
        user = jnp.int32(H)
        for h in range(H):
            user = jnp.where(src[h] == mp * heads + g, h, user)
        held = user // heads
        for r, ref in enumerate((d0, d1, d2, d3)):

            @pl.when((user < H) & (held == mp ^ r))
            def _():
                out[g * HD : (g + 1) * HD, :] = ref[block(user - held * heads, HD), :].astype(f32)


def adamw(master, moment, second, grad, rate, weighted):
    moment_new = 0.9 * moment + 0.1 * grad
    second_new = 0.999 * second + 0.001 * grad * grad
    mean_hat = moment_new / (1.0 - 0.9**ADAM_STEP)
    var_hat = second_new / (1.0 - 0.999**ADAM_STEP)
    master_new = master - rate * (mean_hat / (jnp.sqrt(var_hat) + 1e-08) + weighted * master)
    return (master_new, moment_new, second_new)


def adam_kernel(names, turned, info, full, a, b, *refs):
    ins, outs = refs[:6], refs[6:12]
    rows = a.shape[0]
    grad = a[...].astype(f32) + b[...].astype(f32)
    grad += full[block(info[4], rows), :].astype(f32)
    cols = ins[0].shape[1]
    if turned:
        grad = grad[:, : cols + ins[3].shape[0]]
    second = grad[:, cols:]
    if turned:
        second = jnp.concatenate([second, jnp.zeros((LANES - rows, second.shape[1]), f32)], 0).T[:, :rows]
    for k, (name, part) in enumerate(zip(names, (grad[:, :cols], second))):
        new = adamw(*[r[...] for r in ins[3 * k : 3 * k + 3]], part, RATES[name], 0.1)
        for ref, value in zip(outs[3 * k : 3 * k + 3], new):
            ref[...] = value


def norm_sum_kernel(info, full, a, b, out, turn):
    rows, width = a.shape
    at = slice(width - LANES, width)
    grad = a[:, at].astype(f32) + b[:, at].astype(f32) + full[block(info[4], rows), at].astype(f32)
    turn[...] = jnp.zeros(turn.shape, f32)
    turn[:rows] = grad
    out[...] = turn[...].T[:8]


def norm_adam_kernel(sums, received, w, m, s, w_out, m_out, s_out):
    rows, cols = w.shape
    grad = (sums[...] + received[...])[:rows, :cols]
    new = adamw(w[...], m[...], s[...], grad, RATES["norm"], 0.0)
    for ref, value in zip((w_out, m_out, s_out), new):
        ref[...] = value


def sum_kernel(a, b, out):
    out[...] = a[...] + b[...]


def swap_core(value):
    return lax.ppermute(value, "mp", [(i, i ^ 1) for i in range(4)])


def swap_x(value):
    return lax.ppermute(value, "mp", [(i, i ^ 2) for i in range(4)])


FORWARD = [(RING[i], RING[(i + 1) % 8]) for i in range(8)]
BACKWARD = [(b, a) for a, b in FORWARD]


def ahead(value):
    return lax.ppermute(value, "dp", FORWARD)


def behind(value):
    return lax.ppermute(value, "dp", BACKWARD)


def after(value, *others):
    return lax.optimization_barrier((value,) + others)[0]


class Gather:
    def __init__(self, piece):
        self.ring = lax.axis_size("dp") == len(RING)
        self.start = self.a = self.b = piece
        self.ahead, self.behind = [], []

    def step(self, *gates):
        if not self.ring:
            return
        self.a, self.b = lax.optimization_barrier((self.a, self.b) + gates)[:2]
        self.a = ahead(self.a)
        self.ahead.append(self.a)
        if len(self.behind) < 3:
            self.b = behind(self.b)
            self.behind.append(self.b)

    def pieces(self):
        if not self.ring:
            return [lax.all_gather(self.start, "dp", axis=0, tiled=True)]
        return [self.start] + self.ahead + self.behind


class Scatter:
    def __init__(self, name, info, full, fw, bw):
        self.ring = lax.axis_size("dp") == len(RING)
        self.name, self.info, self.full, self.a, self.b = name, info, full, fw, bw
        self.steps = 0

    def step(self, *gates):
        if not self.ring:
            return
        self.a = after(self.a, *gates)
        k = 4 - self.steps
        shape = (self.a.shape, bf16)
        if k in (3, 2):
            kernel = functools.partial(hop_kernel, k, 1 - k)
            self.a, self.b = call(kernel, f"{self.name}_hop{k}", (self.info,), [self.full, self.a, self.b], [shape] * 2)
        if k == 1:
            (self.a,) = call(hop_last_kernel, f"{self.name}_hop1", (self.info,), [self.full, self.a], [shape])
        self.last = self.a
        self.a = ahead(self.a)
        if k > 1:
            self.b = behind(self.b)
        self.steps += 1

    def ends(self):
        return (self.a, self.b) if self.ring else None


def update(name, info, full, ends, firsts, seconds, turned):
    first, second = name
    outs = [(w.shape, f32) for w in firsts + seconds]
    if ends is not None:
        new = call(
            functools.partial(adam_kernel, name, turned),
            f"adam_{first}",
            (info,),
            [full, *ends, *firsts, *seconds],
            outs,
        )
        return tuple(new[:3]), tuple(new[3:])
    grad = lax.psum_scatter(full.astype(f32), "dp", scatter_dimension=0, tiled=True)
    cols = firsts[0].shape[1]
    other = grad[:, cols : cols + seconds[0].shape[0 if turned else 1]]
    return (
        adamw(*firsts, grad[:, :cols], RATES[first], 0.1),
        adamw(*seconds, other.T if turned else other, RATES[second], 0.1),
    )


def local(
    tokens_in,
    first_values,
    skip_source,
    grad_out,
    qkv_weight,
    proj_weight,
    fc_weight,
    down_weight,
    norm_params,
    qkv_moment,
    proj_moment,
    fc_moment,
    down_moment,
    norm_moment,
    qkv_second,
    proj_second,
    fc_second,
    down_second,
    norm_second,
):
    n = lax.axis_size("dp")
    ring = n == len(RING)
    pieces = n if ring else 1
    count, width = tokens_in.shape
    cols = qkv_weight.shape[1]
    heads = cols // (3 * HD)
    cw = heads * HD
    hid = fc_weight.shape[1]
    wide = -(-(cols + 4) // LANES) * LANES
    half = count // 2
    shard = qkv_weight.shape[0]
    info = HERE
    src = skip_source

    if ring:
        (ring_one,) = call(
            prep_one_kernel,
            "prep_one",
            (),
            [qkv_weight, norm_params],
            [((shard, wide), bf16)],
            scratch=[
                pltpu.VMEM((shard, cols), f32),
                pltpu.VMEM(norm_params.shape, f32),
                pltpu.VMEM((LANES, LANES), f32),
                pltpu.SemaphoreType.DMA((2,)),
            ],
            vmem=60,
            far=True,
        )
        proj_t, fc_low, down_t = call(
            prep_two_kernel,
            "prep_two",
            (),
            [after(proj_weight, ring_one), fc_weight, down_weight.T],
            [((shard, cw), bf16), ((shard, hid), bf16), ((shard, hid), bf16)],
            scratch=[
                pltpu.VMEM((cw, shard), f32),
                pltpu.VMEM((shard, hid), f32),
                pltpu.VMEM((shard, hid), f32),
                pltpu.VMEM((cw, LANES), f32),
                pltpu.SemaphoreType.DMA((3,)),
            ],
            vmem=56,
            far=True,
        )
    else:
        blank = jnp.zeros((shard, wide - cols - 4), bf16)
        ring_one = jnp.concatenate([qkv_weight.astype(bf16), norm_params.T.astype(bf16), blank], 1)
        proj_t, fc_low, down_t = proj_weight.T.astype(bf16), fc_weight.astype(bf16), down_weight.T.astype(bf16)
    fence = lambda *values: lax.optimization_barrier(values)
    fence = lambda *values: lax.optimization_barrier(values)
    one = Gather(ring_one)
    one.step()
    one.a, one.b, proj_t, tokens = fence(one.a, one.b, proj_t, tokens_in)
    one.step()
    proj_x = swap_x(proj_t)
    (unit_one,) = call(unit_kernel, "unit", (), [tokens], [((count, width), f32)])
    one.a, one.b, proj_x, unit_one = fence(one.a, one.b, proj_x, unit_one)
    one.step()
    if ring:
        (ring_two,) = call(
            join_kernel, "join", (), [fc_low, proj_t, proj_x], [((shard, hid + 2 * cw), bf16)]
        )
    else:
        ring_two = jnp.concatenate([fc_low, proj_t, proj_x], 1)
    two, three = Gather(ring_two), Gather(down_t)
    two.step()
    first_t = after(first_values.T, unit_one)
    first_x, first_c = swap_x(first_t), swap_core(first_t)
    one.a, one.b = fence(one.a, one.b)
    one.step()
    one.a, two.a, two.b, unit_one, first_x, three.a = fence(one.a, two.a, two.b, unit_one, first_x, three.a)
    if ring:
        one.ahead[-1] = one.a
    first_xc = swap_core(first_x)
    two.step()
    three.step()

    a1, mixed, fresh, qkv_full, norms = call(
        functools.partial(qkv_kernel, pieces, heads),
        "qkv",
        (info,),
        [unit_one, *one.pieces()],
        [
            ((count, width), bf16),
            ((count, cols), bf16),
            ((cw, count), bf16),
            ((width, wide), bf16),
            ((8, width), f32),
        ],
    )
    (values,) = call(
        functools.partial(values_kernel, heads),
        "values",
        (info, src),
        [fresh, first_t, first_c, first_x, first_xc],
        [((cw, count), bf16)],
    )

    def attend(part, mixed):
        return call(
            functools.partial(attend_kernel, heads, part * half),
            f"attend{part}",
            (),
            [mixed, values],
            [((half, cw), bf16), ((8, half), f32)],
        )

    ctx_a, lse_a = attend(0, mixed)
    two.a, two.b, three.a, three.b, ctx_a = fence(two.a, two.b, three.a, three.b, ctx_a)
    two.step()
    three.step()
    xa = swap_x(ctx_a)
    ctx_b, lse_b = attend(1, after(mixed, ctx_a))
    two.a, two.b, three.a, three.b, xa, ctx_b = fence(two.a, two.b, three.a, three.b, xa, ctx_b)
    two.step()
    three.step()
    xb = swap_x(ctx_b)
    (grad_out,) = call(
        fetch_kernel,
        "fetch",
        (),
        [after(grad_out, ctx_b)],
        [(grad_out.shape, bf16)],
        scratch=[pltpu.SemaphoreType.DMA],
        vmem=4,
        far=True,
    )
    start, xb, two_last, three.a, three.b, grad_out = fence(two.start, xb, two.a, three.a, three.b, grad_out)
    ca, xca, cb, xcb = swap_core(ctx_a), swap_core(xa), swap_core(ctx_b), swap_core(xb)
    three.step()
    context, lse = (ctx_a, ctx_b), (lse_a, lse_b)
    wf, own_w, across_w = call(
        functools.partial(assemble_two_kernel, pieces),
        "assemble_two",
        (info,),
        [start, *two.pieces()[1:]] if ring else two.pieces(),
        [((width, hid), bf16), ((cw, width), bf16), ((cw, width), bf16)],
        scratch=[pltpu.VMEM((width, 2 * cw), bf16)],
    )
    pair = own_w, swap_core(own_w), across_w, swap_core(across_w)

    def mlp(part, norms, contexts):
        return call(
            functools.partial(mlp_kernel, part),
            f"mlp{part}",
            (),
            [tokens, norms, *contexts, *pair, wf],
            [
                ((half, width), f32),
                ((half, width), f32),
                ((half, width), bf16),
                ((half, hid), bf16),
                ((half, hid), f32),
            ],
        )

    def mlp_back(part, grad):
        return call(
            functools.partial(mlp_back_kernel, part),
            f"mlp_back{part}",
            (info,),
            [grad, unit_two[part], slope[part], wf, wd],
            [((half, hid), bf16)] + [((RB // 2, width), bf16)] * 2 + [((RB, width), f32), ((8, width), f32)],
        )

    def mlp_out(part, gate):
        return call(
            mlp_out_kernel,
            f"mlp_out{part}",
            (info,),
            [after(act[part], gate), wd],
            [((RB, width), bf16), ((RB, width), f32)],
        )

    def add(part, keep, *received):
        return call(add_kernel, f"add{part}", (), [keep, *received], [((RB, width), bf16)])[0]

    forward_a = mlp(0, norms, (ctx_a, ca, xa, xca))
    forward_b = mlp(1, after(norms, forward_a[0]), (ctx_b, cb, xb, xcb))
    resid, unit_two, a2, act, slope = zip(forward_a, forward_b)
    start, last = fence(three.start, act[1])
    (wd,) = call(
        functools.partial(assemble_three_kernel, pieces),
        "assemble_three",
        (info,),
        [start, *three.pieces()[1:]] if ring else three.pieces(),
        [((width, hid), bf16)],
    )
    dpre_a, top_a, bottom_a, dkeep_a, nacc_a = mlp_back(0, after(grad_out, act[1]))
    received_a = swap_core(top_a), swap_core(bottom_a)
    dpre_b, top_b, bottom_b, dkeep_b, nacc_b = mlp_back(1, after(grad_out, dpre_a))
    mine_a = add(0, after(dkeep_a, dpre_b), *received_a)
    received_b = swap_core(top_b), swap_core(bottom_b)
    across_a = swap_x(mine_a)

    piece = lambda w: [((width // pieces if ring else 16, w), bf16)] * 2
    mlp_grad, mlp_fw, mlp_bw = call(
        mlp_grad_kernel,
        "mlp_grad",
        (info,),
        [after(a2[0], mine_a), a2[1], dpre_a, dpre_b, grad_out, act[0], act[1]],
        [((width, 2 * hid), bf16 if ring else f32)] + piece(2 * hid),
    )
    mlp_sum = Scatter("mlp", info, mlp_grad, mlp_fw, mlp_bw)
    mlp_sum.step()
    mine_b = add(1, after(dkeep_b, mlp_grad), *received_b)
    across_b = swap_x(mine_b)
    def norm_two(part, mine, across):
        return call(
            functools.partial(norm_two_kernel, part),
            f"norm_two{part}",
            (info,),
            [resid[part], mine, across, grad_out, norms],
            [((RB, width), f32)] + [((RB // 2, width), bf16)] * 2,
        )

    def attend_back(stage, base, blocks, given, part, before, outs):
        return call(
            functools.partial(attend_back_kernel, heads, base, blocks, stage),
            f"attend_back{stage}",
            (info, src),
            [mixed, values, *given, own_w, lse[part], context[part], *before],
            outs,
            vmem=24,
        )

    dr_a, *ab_a = norm_two(0, after(mine_a, mine_b), across_a)
    partner = [swap_core(v) for v in ab_a]
    ab_one, dq_a, dk, dv = attend_back(
        0, 0, 2, [*ab_a, *partner], 0, [], [((half, width), bf16)] + [((half, cw), f32)] * 3
    )
    mlp_sum.a, mlp_sum.b, dq_a = fence(mlp_sum.a, mlp_sum.b, dq_a)
    mlp_sum.step()
    ysend_a, ykeep_a = mlp_out(0, dq_a)
    ysend_b, ykeep_b = mlp_out(1, ysend_a)
    yreceived_a, yreceived_b = swap_core(ysend_a), swap_core(ysend_b)
    rows_mine, rows_sent = call(
        output_rows_kernel,
        "output_rows",
        (info,),
        [ykeep_a, ykeep_b, yreceived_a, yreceived_b],
        [((RB, width), f32), ((RB, width), bf16)],
    )
    dr_b, *ab_b = norm_two(1, after(mine_b, ysend_b), across_b)
    partner = [swap_core(v) for v in ab_b]
    rows_received = swap_x(after(rows_sent, dr_b))
    top = half + RB
    ab_two, dq_b, dk, dv = attend_back(
        1, half, 1, [*ab_b, *partner], 1, [dk, dv], [((half, width), bf16), ((RB, cw), f32)] + [((top, cw), f32)] * 2
    )
    mlp_sum.a, mlp_sum.b, dq_b = fence(mlp_sum.a, mlp_sum.b, dq_b)
    mlp_sum.step()
    dmixed, dreused = attend_back(
        2,
        top,
        1,
        [ab_two],
        1,
        [after(dk, mlp_sum.last) if ring else dk, dv, dq_a, dq_b],
        [((count, cols), bf16), ((cw, count), bf16)],
    )

    *isend, ikeep, sums = call(
        input_kernel,
        "input",
        (info,),
        [dmixed, qkv_full, unit_one, nacc_a, nacc_b],
        [((RB, width), bf16)] * 2 + [((half, width), f32), ((8, width), f32)],
    )
    qkv_grad, qkv_fw, qkv_bw = call(
        qkv_grad_kernel,
        "qkv_grad",
        (info,),
        [a1, dmixed, ab_one, ab_two, context[0], context[1], sums],
        [((width, cols + cw + LANES), bf16 if ring else f32)] + piece(cols + cw + LANES),
        scratch=[pltpu.VMEM((LANES, width), f32)],
    )
    qkv_sum = Scatter("qkv", info, qkv_grad, qkv_fw, qkv_bw)
    mlp_sum.a, mlp_sum.b, qkv_sum.a, qkv_sum.b, rows_received = fence(
        mlp_sum.a, mlp_sum.b, qkv_sum.a, qkv_sum.b, rows_received
    )
    mlp_sum.step()
    qkv_sum.step()
    gathered = [swap_core(v) for v in isend]
    mine, sent = call(
        to_rows_kernel, "to_rows", (info,), [ikeep, *gathered], [((RB, width), f32), ((RB, width), bf16)]
    )
    across, dx = swap_x(sent), swap_x(dreused)
    qkv_sum.a, qkv_sum.b, sent = fence(qkv_sum.a, qkv_sum.b, sent)
    qkv_sum.step()
    (block_out,) = call(
        output_kernel,
        "output",
        (info,),
        [resid[0], resid[1], rows_mine, rows_received],
        [((RB, width), bf16)],
    )
    qkv_sum.a, qkv_sum.b, mlp_sum.a, block_out = fence(qkv_sum.a, qkv_sum.b, mlp_sum.a, block_out)
    qkv_sum.step()
    fc_new, down_new = update(
        ("fc", "down"),
        info,
        mlp_grad,
        mlp_sum.ends(),
        [fc_weight, fc_moment, fc_second],
        [down_weight.T, down_moment.T, down_second.T],
        False,
    )
    qkv_sum.a, qkv_sum.b, across, dx, *fc_new = fence(qkv_sum.a, qkv_sum.b, across, dx, *fc_new)
    down_new = tuple(v.T for v in down_new)
    qkv_sum.step()
    (input_grad,) = call(
        norm_one_kernel,
        "norm_one",
        (info,),
        [tokens, mine, across, dr_a, dr_b, norms],
        [((RB, width), f32)],
    )
    dx, dreused = fence(dx, dreused)
    dc, dxc = swap_core(dreused), swap_core(dx)
    (first_grad,) = call(
        functools.partial(first_kernel, heads),
        "first",
        (info, src),
        [dreused, dc, dx, dxc],
        [((cw, count), f32)],
    )
    qkv_sum.a, input_grad, first_grad = fence(qkv_sum.a, input_grad, first_grad)
    if ring:
        (sums,) = call(
            norm_sum_kernel,
            "norm_sum",
            (info,),
            [qkv_grad, *qkv_sum.ends()],
            [((8, LANES), f32)],
            scratch=[pltpu.VMEM((LANES, LANES), f32)],
        )
        (sums,) = call(sum_kernel, "sum", (), [sums, swap_core(sums)], [(sums.shape, f32)])
        received = swap_x(sums)
    qkv_new, proj_new = update(
        ("qkv", "proj"),
        info,
        qkv_grad,
        qkv_sum.ends(),
        [qkv_weight, qkv_moment, qkv_second],
        [proj_weight, proj_moment, proj_second],
        True,
    )
    if ring:
        norm_new = call(
            norm_adam_kernel,
            "adam_norm",
            (),
            [sums, received, norm_params, norm_moment, norm_second],
            [(norm_params.shape, f32)] * 3,
        )
    else:
        own = lax.psum_scatter(lax.psum(sums, "mp"), "dp", scatter_dimension=1, tiled=True)[:4]
        norm_new = adamw(norm_params, norm_moment, norm_second, own, RATES["norm"], 0.0)
    return (block_out, input_grad, first_grad.T, *qkv_new, *proj_new, *fc_new, *down_new, *norm_new)


def solution(mesh):
    both = P("dp", "mp")
    turned = P("mp", "dp")
    rows = P("dp", None)
    every = P(None, "dp")
    state = (both, turned, both, turned, every)
    return jax.shard_map(
        local,
        mesh=mesh,
        in_specs=(rows, both, P(), rows) + state * 3,
        out_specs=(P(("dp", "mp"), None), P(("dp", "mp"), None), both)
        + (both,) * 3
        + (turned,) * 3
        + (both,) * 3
        + (turned,) * 3
        + (every,) * 3,
        check_vma=False,
    )
```

```python
import functools

import jax
import jax.numpy as jnp
import numpy as np
from jax import lax
from jax.experimental import pallas as pl
from jax.experimental.pallas import tpu as pltpu
from jax.sharding import PartitionSpec as P

H = 12
HD = 64
ADAM_STEP = 5
EPS = 1e-05
MASKED = -1e30
RB = 256
LANES = 128
RING = (0, 2, 4, 6, 7, 5, 3, 1)
OFFSETS = (0, -1, -2, -3, -4, 1, 2, 3)
GELU_A = 0.7978845608028654
GELU_B = 0.044715
RATES = {"qkv": 0.06, "proj": 0.15, "fc": 0.04, "down": 0.03, "norm": 0.3}

bf16 = jnp.bfloat16
f32 = jnp.float32


def dot(a, b):
    return jnp.dot(a, b, preferred_element_type=f32)


def dot_nt(a, b):
    return lax.dot_general(a, b, (((1,), (1,)), ((), ())), preferred_element_type=f32)


def dot_tn(a, b):
    return lax.dot_general(a, b, (((0,), (0,)), ((), ())), preferred_element_type=f32)


class Place:
    def __init__(self):
        self.mp, self.dp = lax.axis_index("mp"), lax.axis_index("dp")

    def __getitem__(self, k):
        if k < 4:
            return (self.mp % 2, self.mp // 2, self.mp, self.dp)[k]
        if lax.axis_size("dp") != len(RING):
            return 0
        z, y = self.dp // 2, self.dp % 2
        at = (jnp.where(y == 0, z, 7 - z) + OFFSETS[k - 4] + 8) % 8
        return jnp.where(at < 4, 2 * at, 2 * (7 - at) + 1)


HERE = object()


def call(kernel, name, scalars, ins, outs, scratch=(), vmem=16, far=False):
    if HERE in scalars:
        inner = kernel
        kernel = lambda *refs: inner(Place(), *refs)
        scalars = scalars[1:]
    smem = pl.BlockSpec(memory_space=pltpu.SMEM)
    full = pl.BlockSpec(memory_space=pltpu.VMEM)
    given = pl.BlockSpec(memory_space=pltpu.HBM) if far else full
    return pl.pallas_call(
        kernel,
        in_specs=[smem] * len(scalars) + [given] * len(ins),
        out_specs=[full] * len(outs),
        out_shape=[jax.ShapeDtypeStruct(sh, dt) for sh, dt in outs],
        scratch_shapes=list(scratch),
        compiler_params=pltpu.CompilerParams(vmem_limit_bytes=vmem * 1024 * 1024),
        cost_estimate=pl.CostEstimate(flops=1, bytes_accessed=1, transcendentals=0),
        name=name,
    )(*scalars, *ins)


def block(index, size=RB):
    if isinstance(index, int):
        return slice(index * size, (index + 1) * size)
    return pl.ds(pl.multiple_of(index * size, size), size)


def fetch(pairs, sems):
    copies = [pltpu.make_async_copy(src, dst, sems.at[k]) for k, (src, dst) in enumerate(pairs)]
    for copy in copies:
        copy.start()
    for copy in copies:
        copy.wait()


def prep_one_kernel(q_ref, n_ref, out, q, norms, turn, sems):
    rows, cols = q.shape
    turn[...] = jnp.zeros(turn.shape, f32)
    fetch([(q_ref, q), (n_ref, norms)], sems)
    turn[: norms.shape[0], :rows] = norms[...]
    out[:, :cols] = q[...].astype(bf16)
    out[:, cols:] = turn[...].T[:rows, : out.shape[1] - cols].astype(bf16)


def prep_two_kernel(p_ref, f_ref, d_ref, proj, fc, down, p, f, d, turn, sems):
    rows = proj.shape[0]
    turn[...] = jnp.zeros(turn.shape, f32)
    fetch([(p_ref, p), (f_ref, f), (d_ref, d)], sems)
    turn[:, :rows] = p[...]
    proj[...] = turn[...].T[:rows].astype(bf16)
    fc[...] = f[...].astype(bf16)
    down[...] = d[...].astype(bf16)


def join_kernel(f_ref, own, across, out):
    hid, cw = f_ref.shape[1], own.shape[1]
    out[:, :hid] = f_ref[...]
    out[:, hid:] = jnp.concatenate([own[...], across[...]], 1)


def norm_stats(values):
    center = values - jnp.mean(values, axis=-1, keepdims=True)
    scale = lax.rsqrt(jnp.mean(center * center, axis=-1, keepdims=True) + EPS)
    return center * scale, scale


def unit_kernel(x_ref, unit_ref):
    for i in range(x_ref.shape[0] // RB):
        at = slice(i * RB, (i + 1) * RB)
        unit_ref[at] = norm_stats(x_ref[at].astype(f32))[0]


def fetch_kernel(src, out, sem):
    copy = pltpu.make_async_copy(src, out, sem)
    copy.start()
    copy.wait()


def loop(count, body):
    lax.fori_loop(0, count, lambda i, carry: (body(i), carry)[1], 0)


def qkv_kernel(n, heads, info, unit_ref, *refs):
    pieces, (a1_ref, m_ref, v_ref, w_ref, norm_ref) = refs[:n], refs[n:]
    cols = m_ref.shape[1]
    base = cols // LANES * LANES
    rows = w_ref.shape[0] // n
    for k, piece in enumerate(pieces):
        w_ref[block(info[4 + k], rows), :] = piece[...]
    turned = w_ref[:, base : base + LANES].astype(f32).T
    norm_ref[...] = turned[cols - base : cols - base + 8]

    def step(i):
        at = block(i)
        a1 = (unit_ref[at, :] * norm_ref[0:1] + norm_ref[1:2]).astype(bf16)
        a1_ref[at, :] = a1
        mixed = dot(a1, w_ref[:, :cols])
        m_ref[at, :] = mixed.astype(bf16)
        for h in range(heads):
            fresh = mixed[:, (3 * h + 2) * HD : (3 * h + 3) * HD]
            v_ref[h * HD : (h + 1) * HD, at] = fresh.T.astype(bf16)

    loop(m_ref.shape[0] // RB, step)


def values_kernel(heads, info, src, fresh, f0, f1, f2, f3, v_ref):
    mp = info[2]
    for h in range(heads):
        source = src[mp * heads + h]
        held = source // heads
        mine = slice(h * HD, (h + 1) * HD)

        @pl.when(source >= H)
        def _():
            v_ref[mine, :] = fresh[mine, :]

        for r, first in enumerate((f0, f1, f2, f3)):

            @pl.when((source < H) & (held == mp ^ r))
            def _():
                v_ref[mine, :] = first[block(source - held * heads, HD), :]


def masked_tile():
    keys = lax.broadcasted_iota(jnp.int32, (RB, RB), 0)
    queries = lax.broadcasted_iota(jnp.int32, (RB, RB), 1)
    return keys <= queries


def attend_kernel(heads, base, m_ref, v_ref, c_ref, lse_ref, keys_ref, query_ref, turned):
    keep = masked_tile()
    blocks = c_ref.shape[0] // RB
    top = base + blocks * RB
    lse_ref[...] = jnp.zeros(lse_ref.shape, f32)
    for h in range(heads):
        keys_ref[h] = m_ref[:top, (3 * h + 1) * HD : (3 * h + 2) * HD]
        query_ref[h] = m_ref[base:top, 3 * h * HD : (3 * h + 1) * HD] * bf16(HD**-0.5)

    def step(h):
        mine = block(h, HD)
        for i in range(blocks):
            lo = base + i * RB
            hi = lo + RB
            at = slice(i * RB, (i + 1) * RB)
            query = query_ref[h, at]
            diag = jnp.where(keep, dot_nt(keys_ref[h, lo:hi], query), MASKED)
            peak = jnp.max(diag, 0, keepdims=True)
            if lo:
                left = dot_nt(keys_ref[h, :lo], query)
                peak = jnp.maximum(peak, jnp.max(left, 0, keepdims=True))
            diag = jnp.exp(diag - peak)
            total = jnp.sum(diag, 0, keepdims=True)
            if lo:
                left = jnp.exp(left - peak)
                total += jnp.sum(left, 0, keepdims=True)
            inverse = 1.0 / total
            context = dot(v_ref[mine, lo:hi], (diag * inverse).astype(bf16))
            if lo:
                context += dot(v_ref[mine, :lo], (left * inverse).astype(bf16))
            turned[mine, at] = context
            lse_ref[pl.ds(h, 1), at] = peak + jnp.log(total)

    loop(heads, step)
    c_ref[...] = turned[...].T.astype(bf16)


def assemble_two_kernel(n, info, *refs):
    pieces, (wf, own, across, turn) = refs[:n], refs[n:]
    width, hid = wf.shape
    cw = own.shape[0]
    rows = width // n
    for k, piece in enumerate(pieces):
        at = block(info[4 + k], rows)
        wf[at, :] = piece[:, :hid]
        turn[at, :] = piece[:, hid:]
    pair = turn[...].T
    own[...] = pair[:cw]
    across[...] = pair[cw:]


def assemble_three_kernel(n, info, *refs):
    pieces, (wd,) = refs[:n], refs[n:]
    rows = wd.shape[0] // n
    for k, piece in enumerate(pieces):
        wd[block(info[4 + k], rows), :] = piece[...]


def mlp_kernel(part, x_ref, norm_ref, c0, c1, c2, c3, w0, w1, w2, w3, wf, r_ref, unit_ref, a2_ref, g_ref, slope_ref):
    def step(i):
        at = block(i)
        resid = x_ref[block(2 * part + i), :].astype(f32) + (
            (dot(c0[at, :], w0[...]) + dot(c1[at, :], w1[...]))
            + (dot(c2[at, :], w2[...]) + dot(c3[at, :], w3[...]))
        )
        r_ref[at, :] = resid
        unit, _ = norm_stats(resid)
        unit_ref[at, :] = unit
        a2 = (unit * norm_ref[2:3] + norm_ref[3:4]).astype(bf16)
        a2_ref[at, :] = a2
        u = dot(a2, wf[...])
        square = u * u
        t = jnp.tanh(GELU_A * u * (1.0 + GELU_B * square))
        g_ref[at, :] = (0.5 * u * (1.0 + t)).astype(bf16)
        slope_ref[at, :] = 0.5 * (1.0 + t) + 0.5 * u * (1.0 - t * t) * (
            GELU_A * (1.0 + 3.0 * GELU_B * square)
        )

    loop(2, step)


def mlp_back_kernel(part, info, e_ref, unit_ref, slope_ref, wf, wd, du_ref, top, bottom, keep, nacc):
    core = info[0]
    nacc[...] = jnp.zeros(nacc.shape, f32)

    def step(i):
        spot = core if i else 1 - core
        at = block(spot)
        du = (dot(e_ref[block(2 * part + spot), :], wd[...]) * slope_ref[at, :]).astype(bf16)
        du_ref[at, :] = du
        grad = dot_nt(du, wf[...])
        nacc[2:3] += jnp.sum(grad * unit_ref[at, :], 0, keepdims=True)
        nacc[3:4] += jnp.sum(grad, 0, keepdims=True)
        keep[...] = grad

        @pl.when(i < 1)
        def _():
            top[...] = grad[: RB // 2].astype(bf16)
            bottom[...] = grad[RB // 2 :].astype(bf16)

    for i in range(2):
        step(i)


def mlp_out_kernel(info, g_ref, wd, ysend, ykeep):
    ykeep[...] = dot_nt(g_ref[block(info[0]), :], wd[...])
    ysend[...] = dot_nt(g_ref[block(1 - info[0]), :], wd[...]).astype(bf16)


def add_kernel(keep, top, bottom, out):
    out[: RB // 2] = (keep[: RB // 2] + top[...].astype(f32)).astype(bf16)
    out[RB // 2 :] = (keep[RB // 2 :] + bottom[...].astype(f32)).astype(bf16)


def starts(info, full, fw, bw):
    rows = fw.shape[0]
    fw[...] = full[block(info[4 + OFFSETS.index(-4)], rows), :].astype(bf16)
    bw[...] = full[block(info[4 + OFFSETS.index(-3)], rows), :].astype(bf16)


def mlp_grad_kernel(info, a2a, a2b, dua, dub, e_ref, ga, gb, out, fw, bw):
    hid = dua.shape[1]
    half = dua.shape[0]

    def step(j):
        at = block(j)
        out[at, :hid] = (dot_tn(a2a[:, at], dua[...]) + dot_tn(a2b[:, at], dub[...])).astype(out.dtype)
        out[at, hid:] = (dot_tn(e_ref[:half, at], ga[...]) + dot_tn(e_ref[half:, at], gb[...])).astype(out.dtype)

    for j in range(out.shape[0] // RB):
        step(j)
    starts(info, out, fw, bw)


def hop_kernel(ahead, behind, info, full, a, b, a_out, b_out):
    rows = a.shape[0]
    for offset, value, out in ((ahead, a, a_out), (behind, b, b_out)):
        term = full[block(info[4 + OFFSETS.index(offset)], rows), :]
        out[...] = (value[...].astype(f32) + term.astype(f32)).astype(bf16)


def hop_last_kernel(info, full, a, a_out):
    term = full[block(info[4 + OFFSETS.index(1)], a.shape[0]), :]
    a_out[...] = (a[...].astype(f32) + term.astype(f32)).astype(bf16)


def norm_back(unit, scale, gain, grad):
    dy = grad * gain
    return scale * (
        dy - jnp.mean(dy, -1, keepdims=True) - unit * jnp.mean(dy * unit, -1, keepdims=True)
    )


def norm_two_kernel(part, info, r_ref, own, received, e_ref, norm_ref, dr_ref, top, bottom):
    unit, scale = norm_stats(r_ref[block(info[0]), :])
    grad = own[...].astype(f32) + received[...].astype(f32)
    e = e_ref[block(2 * part + info[0]), :].astype(f32)
    dr = e + norm_back(unit, scale, norm_ref[2:3], grad)
    dr_ref[...] = dr
    top[...] = dr[: RB // 2].astype(bf16)
    bottom[...] = dr[RB // 2 :].astype(bf16)


def attend_back_kernel(heads, base, blocks, stage, info, src, m_ref, v_ref, *refs):
    if stage < 2:
        halves, refs = refs[:4], refs[4:]
    else:
        ab_in, refs = refs[0], refs[1:]
    wp, lse_ref, c_ref, *refs = refs
    if stage:
        dk_in, dv_in, *refs = refs
    if stage == 0:
        ab_ref, dq_ref, dk_ref, dv_ref = refs
    elif stage == 1:
        ab_ref, dq_ref, dk_ref, dv_ref = refs
    else:
        dq_first, dq_second, dm_ref, dvr_ref = refs
    keep = masked_tile()
    core = info[0]
    if stage < 2:
        for k in range(2):
            ab_ref[block(2 * core + k, RB // 2), :] = halves[k][...]
            ab_ref[block(2 * (1 - core) + k, RB // 2), :] = halves[2 + k][...]
        source, skip = ab_ref, 0
    else:
        source, skip = ab_in, ab_in.shape[0] - blocks * RB
    top = base + blocks * RB
    tiles = top // RB
    dctx = [dot_nt(source[skip + i * RB : skip + (i + 1) * RB], wp[...]).astype(bf16) for i in range(blocks)]
    first = c_ref.shape[0] - blocks * RB if stage == 2 else 0
    own_rows = [slice(first + i * RB, first + (i + 1) * RB) for i in range(blocks)]
    terms = [(d.astype(f32) * c_ref[at].astype(f32)).T for d, at in zip(dctx, own_rows)]
    dq_t = [[None] * heads for _ in range(blocks)]
    dks, dvs = [], []
    for h in range(heads):
        lane = slice(h * HD, (h + 1) * HD)
        keys = m_ref[:top, (3 * h + 1) * HD : (3 * h + 2) * HD]
        keys_t = keys.T
        values = v_ref[h * HD : (h + 1) * HD, :top].T
        dk = [None] * tiles
        dv = [None] * tiles
        if stage:
            for t in range(base // RB):
                dk[t] = dk_in[t * RB : (t + 1) * RB, lane]
                dv[t] = dv_in[t * RB : (t + 1) * RB, lane]
        for i in range(blocks):
            lo = base + i * RB
            hi = lo + RB
            query = m_ref[lo:hi, 3 * h * HD : (3 * h + 1) * HD] * bf16(HD**-0.5)
            dc = dctx[i][:, lane]
            lse = lse_ref[h : h + 1, own_rows[i]]
            prob = jnp.exp(dot_nt(keys[:hi], query) - lse)
            own = jnp.where(keep, prob[lo:], 0.0)
            prob = jnp.concatenate([prob[:lo], own], 0) if lo else own
            dprob = dot_nt(values[:hi], dc)
            inner = jnp.sum(terms[i][lane], 0, keepdims=True)
            more_v = dot(prob.astype(bf16), dc)
            ds = (prob * (dprob - inner)).astype(bf16)
            more_k = dot(ds, query)
            dq_t[i][h] = dot(keys_t[:, :hi], ds) * HD**-0.5
            for t in range(hi // RB):
                spot = slice(t * RB, (t + 1) * RB)
                dv[t] = more_v[spot] if dv[t] is None else dv[t] + more_v[spot]
                dk[t] = more_k[spot] if dk[t] is None else dk[t] + more_k[spot]
        dks.append(dk)
        dvs.append(dv)
    dq = [jnp.concatenate(dq_t[i], 0).T for i in range(blocks)]
    if stage < 2:
        for i in range(blocks):
            dq_ref[i * RB : (i + 1) * RB] = dq[i]
        for t in range(tiles):
            dk_ref[t * RB : (t + 1) * RB] = jnp.concatenate([dks[h][t] for h in range(heads)], 1)
            dv_ref[t * RB : (t + 1) * RB] = jnp.concatenate([dvs[h][t] for h in range(heads)], 1)
        return
    mp = info[2]
    fresh = [jnp.where(src[mp * heads + h] < H, 0.0, 1.0) for h in range(heads)]
    split = dq_first.shape[0]
    for t in range(tiles):
        spot = slice(t * RB, (t + 1) * RB)
        parts = []
        for h in range(heads):
            lane = slice(h * HD, (h + 1) * HD)
            if t * RB < split:
                dqh = dq_first[spot, lane]
            elif t * RB < base:
                dqh = dq_second[t * RB - split : (t + 1) * RB - split, lane]
            else:
                dqh = dq[t - base // RB][:, lane]
            parts += [dqh, dks[h][t], dvs[h][t] * fresh[h]]
            dvr_ref[h * HD : (h + 1) * HD, spot] = dvs[h][t].T.astype(bf16)
        dm_ref[spot, :] = jnp.concatenate(parts, 1).astype(bf16)


def input_kernel(info, dm_ref, w_ref, unit_ref, na, nb, s0, s1, keep, sums):
    core = info[0]
    cols = dm_ref.shape[1]
    gain = jnp.zeros((1, unit_ref.shape[1]), f32)
    shift = gain
    for own in range(2):
        for half, out in enumerate((s0, s1)):
            at = block(2 * half + (core if own else 1 - core))
            grad = dot_nt(dm_ref[at, :], w_ref[:, :cols])
            gain += jnp.sum(grad * unit_ref[at, :], 0, keepdims=True)
            shift += jnp.sum(grad, 0, keepdims=True)
            if own:
                keep[block(half)] = grad
            else:
                out[...] = grad.astype(bf16)
    sums[...] = na[...] + nb[...]
    sums[0:1] = gain
    sums[1:2] = shift


def to_rows_kernel(info, keep, r0, r1, mine, sent):
    low = info[1] == 0
    first = keep[:RB] + r0[...].astype(f32)
    second = keep[RB:] + r1[...].astype(f32)
    mine[...] = jnp.where(low, first, second)
    sent[...] = jnp.where(low, second, first).astype(bf16)


def output_rows_kernel(info, ka, kb, ra, rb, mine, sent):
    low = info[1] == 0
    first = ka[...] + ra[...].astype(f32)
    second = kb[...] + rb[...].astype(f32)
    mine[...] = jnp.where(low, first, second)
    sent[...] = jnp.where(low, second, first).astype(bf16)


def output_kernel(info, ra, rb, mine, received, out):
    at = block(info[0])
    resid = jnp.where(info[1] == 0, ra[at, :], rb[at, :])
    out[...] = (resid + mine[...] + received[...].astype(f32)).astype(bf16)


def qkv_grad_kernel(info, a1_ref, dm_ref, aba, abb, ca, cb, sums, out, fw, bw, turn):
    cols, width = dm_ref.shape[1], sums.shape[1]
    turn[...] = jnp.zeros(turn.shape, f32)
    turn[: sums.shape[0]] = sums[...]

    def step(j):
        at = block(j)
        grad = dot_tn(a1_ref[:, at], dm_ref[...])
        proj = dot_tn(aba[:, at], ca[...]) + dot_tn(abb[:, at], cb[...])
        out[at, : out.shape[1] - LANES] = jnp.concatenate([grad, proj], 1).astype(out.dtype)
        out[at, out.shape[1] - LANES :] = turn[:, at].T.astype(out.dtype)

    for j in range(out.shape[0] // RB):
        step(j)
    starts(info, out, fw, bw)


def norm_one_kernel(info, x_ref, own, received, dra, drb, norm_ref, out):
    unit, scale = norm_stats(x_ref[block(info[2]), :].astype(f32))
    grad = own[...] + received[...].astype(f32)
    dr = jnp.where(info[1] == 0, dra[...], drb[...])
    out[...] = dr + norm_back(unit, scale, norm_ref[0:1], grad)


def first_kernel(heads, info, src, d0, d1, d2, d3, out):
    mp = info[2]
    out[...] = jnp.zeros(out.shape, f32)
    for g in range(heads):
        user = jnp.int32(H)
        for h in range(H):
            user = jnp.where(src[h] == mp * heads + g, h, user)
        held = user // heads
        for r, ref in enumerate((d0, d1, d2, d3)):

            @pl.when((user < H) & (held == mp ^ r))
            def _():
                out[g * HD : (g + 1) * HD, :] = ref[block(user - held * heads, HD), :].astype(f32)


def adamw(master, moment, second, grad, rate, weighted):
    moment_new = 0.9 * moment + 0.1 * grad
    second_new = 0.999 * second + 0.001 * grad * grad
    mean_hat = moment_new / (1.0 - 0.9**ADAM_STEP)
    var_hat = second_new / (1.0 - 0.999**ADAM_STEP)
    master_new = master - rate * (mean_hat / (jnp.sqrt(var_hat) + 1e-08) + weighted * master)
    return (master_new, moment_new, second_new)


def adam_kernel(names, turned, info, full, a, b, *refs):
    ins, outs = refs[:6], refs[6:12]
    rows = a.shape[0]
    grad = a[...].astype(f32) + b[...].astype(f32)
    grad += full[block(info[4], rows), :].astype(f32)
    cols = ins[0].shape[1]
    if turned:
        grad = grad[:, : cols + ins[3].shape[0]]
    second = grad[:, cols:]
    if turned:
        second = jnp.concatenate([second, jnp.zeros((LANES - rows, second.shape[1]), f32)], 0).T[:, :rows]
    for k, (name, part) in enumerate(zip(names, (grad[:, :cols], second))):
        new = adamw(*[r[...] for r in ins[3 * k : 3 * k + 3]], part, RATES[name], 0.1)
        for ref, value in zip(outs[3 * k : 3 * k + 3], new):
            ref[...] = value


def norm_sum_kernel(info, full, a, b, out, turn):
    rows, width = a.shape
    at = slice(width - LANES, width)
    grad = a[:, at].astype(f32) + b[:, at].astype(f32) + full[block(info[4], rows), at].astype(f32)
    turn[...] = jnp.zeros(turn.shape, f32)
    turn[:rows] = grad
    out[...] = turn[...].T[:8]


def norm_adam_kernel(sums, received, w, m, s, w_out, m_out, s_out):
    rows, cols = w.shape
    grad = (sums[...] + received[...])[:rows, :cols]
    new = adamw(w[...], m[...], s[...], grad, RATES["norm"], 0.0)
    for ref, value in zip((w_out, m_out, s_out), new):
        ref[...] = value


def sum_kernel(a, b, out):
    out[...] = a[...] + b[...]


def swap_core(value):
    return lax.ppermute(value, "mp", [(i, i ^ 1) for i in range(4)])


def swap_x(value):
    return lax.ppermute(value, "mp", [(i, i ^ 2) for i in range(4)])


FORWARD = [(RING[i], RING[(i + 1) % 8]) for i in range(8)]
BACKWARD = [(b, a) for a, b in FORWARD]


def ahead(value):
    return lax.ppermute(value, "dp", FORWARD)


def behind(value):
    return lax.ppermute(value, "dp", BACKWARD)


def after(value, *others):
    return lax.optimization_barrier((value,) + others)[0]


class Gather:
    def __init__(self, piece):
        self.ring = lax.axis_size("dp") == len(RING)
        self.start = self.a = self.b = piece
        self.ahead, self.behind = [], []

    def step(self, *gates):
        if not self.ring:
            return
        self.a, self.b = lax.optimization_barrier((self.a, self.b) + gates)[:2]
        self.a = ahead(self.a)
        self.ahead.append(self.a)
        if len(self.behind) < 3:
            self.b = behind(self.b)
            self.behind.append(self.b)

    def pieces(self):
        if not self.ring:
            return [lax.all_gather(self.start, "dp", axis=0, tiled=True)]
        return [self.start] + self.ahead + self.behind


class Scatter:
    def __init__(self, name, info, full, fw, bw):
        self.ring = lax.axis_size("dp") == len(RING)
        self.name, self.info, self.full, self.a, self.b = name, info, full, fw, bw
        self.steps = 0

    def step(self, *gates):
        if not self.ring:
            return
        self.a = after(self.a, *gates)
        k = 4 - self.steps
        shape = (self.a.shape, bf16)
        if k in (3, 2):
            kernel = functools.partial(hop_kernel, k, 1 - k)
            self.a, self.b = call(kernel, f"{self.name}_hop{k}", (self.info,), [self.full, self.a, self.b], [shape] * 2)
        if k == 1:
            (self.a,) = call(hop_last_kernel, f"{self.name}_hop1", (self.info,), [self.full, self.a], [shape])
        self.last = self.a
        self.a = ahead(self.a)
        if k > 1:
            self.b = behind(self.b)
        self.steps += 1

    def ends(self):
        return (self.a, self.b) if self.ring else None


def update(name, info, full, ends, firsts, seconds, turned):
    first, second = name
    outs = [(w.shape, f32) for w in firsts + seconds]
    if ends is not None:
        new = call(
            functools.partial(adam_kernel, name, turned),
            f"adam_{first}",
            (info,),
            [full, *ends, *firsts, *seconds],
            outs,
        )
        return tuple(new[:3]), tuple(new[3:])
    grad = lax.psum_scatter(full.astype(f32), "dp", scatter_dimension=0, tiled=True)
    cols = firsts[0].shape[1]
    other = grad[:, cols : cols + seconds[0].shape[0 if turned else 1]]
    return (
        adamw(*firsts, grad[:, :cols], RATES[first], 0.1),
        adamw(*seconds, other.T if turned else other, RATES[second], 0.1),
    )


def local(
    tokens_in,
    first_values,
    skip_source,
    grad_out,
    qkv_weight,
    proj_weight,
    fc_weight,
    down_weight,
    norm_params,
    qkv_moment,
    proj_moment,
    fc_moment,
    down_moment,
    norm_moment,
    qkv_second,
    proj_second,
    fc_second,
    down_second,
    norm_second,
):
    n = lax.axis_size("dp")
    ring = n == len(RING)
    pieces = n if ring else 1
    count, width = tokens_in.shape
    cols = qkv_weight.shape[1]
    heads = cols // (3 * HD)
    cw = heads * HD
    hid = fc_weight.shape[1]
    wide = -(-(cols + 4) // LANES) * LANES
    half = count // 2
    shard = qkv_weight.shape[0]
    info = HERE
    src = skip_source

    if ring:
        (ring_one,) = call(
            prep_one_kernel,
            "prep_one",
            (),
            [qkv_weight, norm_params],
            [((shard, wide), bf16)],
            scratch=[
                pltpu.VMEM((shard, cols), f32),
                pltpu.VMEM(norm_params.shape, f32),
                pltpu.VMEM((LANES, LANES), f32),
                pltpu.SemaphoreType.DMA((2,)),
            ],
            vmem=60,
            far=True,
        )
        proj_t, fc_low, down_t = call(
            prep_two_kernel,
            "prep_two",
            (),
            [after(proj_weight, ring_one), fc_weight, down_weight.T],
            [((shard, cw), bf16), ((shard, hid), bf16), ((shard, hid), bf16)],
            scratch=[
                pltpu.VMEM((cw, shard), f32),
                pltpu.VMEM((shard, hid), f32),
                pltpu.VMEM((shard, hid), f32),
                pltpu.VMEM((cw, LANES), f32),
                pltpu.SemaphoreType.DMA((3,)),
            ],
            vmem=56,
            far=True,
        )
    else:
        blank = jnp.zeros((shard, wide - cols - 4), bf16)
        ring_one = jnp.concatenate([qkv_weight.astype(bf16), norm_params.T.astype(bf16), blank], 1)
        proj_t, fc_low, down_t = proj_weight.T.astype(bf16), fc_weight.astype(bf16), down_weight.T.astype(bf16)
    fence = lambda *values: lax.optimization_barrier(values)
    fence = lambda *values: lax.optimization_barrier(values)
    one = Gather(ring_one)
    one.step()
    one.a, one.b, proj_t, tokens = fence(one.a, one.b, proj_t, tokens_in)
    one.step()
    proj_x = swap_x(proj_t)
    (unit_one,) = call(unit_kernel, "unit", (), [tokens], [((count, width), f32)])
    one.a, one.b, proj_x, unit_one = fence(one.a, one.b, proj_x, unit_one)
    one.step()
    if ring:
        (ring_two,) = call(
            join_kernel, "join", (), [fc_low, proj_t, proj_x], [((shard, hid + 2 * cw), bf16)]
        )
    else:
        ring_two = jnp.concatenate([fc_low, proj_t, proj_x], 1)
    two, three = Gather(ring_two), Gather(down_t)
    two.step()
    first_t = after(first_values.T, unit_one)
    first_x, first_c = swap_x(first_t), swap_core(first_t)
    one.a, one.b = fence(one.a, one.b)
    one.step()
    one.a, two.a, two.b, unit_one, first_x, three.a = fence(one.a, two.a, two.b, unit_one, first_x, three.a)
    if ring:
        one.ahead[-1] = one.a
    first_xc = swap_core(first_x)
    two.step()
    three.step()

    a1, mixed, fresh, qkv_full, norms = call(
        functools.partial(qkv_kernel, pieces, heads),
        "qkv",
        (info,),
        [unit_one, *one.pieces()],
        [
            ((count, width), bf16),
            ((count, cols), bf16),
            ((cw, count), bf16),
            ((width, wide), bf16),
            ((8, width), f32),
        ],
    )
    (values,) = call(
        functools.partial(values_kernel, heads),
        "values",
        (info, src),
        [fresh, first_t, first_c, first_x, first_xc],
        [((cw, count), bf16)],
    )

    def attend(part, mixed):
        return call(
            functools.partial(attend_kernel, heads, part * half),
            f"attend{part}",
            (),
            [mixed, values],
            [((half, cw), bf16), ((8, half), f32)],
            scratch=[
                pltpu.VMEM((heads, (part + 1) * half, HD), bf16),
                pltpu.VMEM((heads, half, HD), bf16),
                pltpu.VMEM((cw, half), f32),
            ],
        )

    ctx_a, lse_a = attend(0, mixed)
    two.a, two.b, three.a, three.b, ctx_a = fence(two.a, two.b, three.a, three.b, ctx_a)
    two.step()
    three.step()
    xa = swap_x(ctx_a)
    ctx_b, lse_b = attend(1, after(mixed, ctx_a))
    two.a, two.b, three.a, three.b, xa, ctx_b = fence(two.a, two.b, three.a, three.b, xa, ctx_b)
    two.step()
    three.step()
    xb = swap_x(ctx_b)
    (grad_out,) = call(
        fetch_kernel,
        "fetch",
        (),
        [after(grad_out, ctx_b)],
        [(grad_out.shape, bf16)],
        scratch=[pltpu.SemaphoreType.DMA],
        vmem=4,
        far=True,
    )
    start, xb, two_last, three.a, three.b, grad_out = fence(two.start, xb, two.a, three.a, three.b, grad_out)
    ca, xca, cb, xcb = swap_core(ctx_a), swap_core(xa), swap_core(ctx_b), swap_core(xb)
    three.step()
    context, lse = (ctx_a, ctx_b), (lse_a, lse_b)
    wf, own_w, across_w = call(
        functools.partial(assemble_two_kernel, pieces),
        "assemble_two",
        (info,),
        [start, *two.pieces()[1:]] if ring else two.pieces(),
        [((width, hid), bf16), ((cw, width), bf16), ((cw, width), bf16)],
        scratch=[pltpu.VMEM((width, 2 * cw), bf16)],
    )
    pair = own_w, swap_core(own_w), across_w, swap_core(across_w)

    def mlp(part, norms, contexts):
        return call(
            functools.partial(mlp_kernel, part),
            f"mlp{part}",
            (),
            [tokens, norms, *contexts, *pair, wf],
            [
                ((half, width), f32),
                ((half, width), f32),
                ((half, width), bf16),
                ((half, hid), bf16),
                ((half, hid), f32),
            ],
        )

    def mlp_back(part, grad):
        return call(
            functools.partial(mlp_back_kernel, part),
            f"mlp_back{part}",
            (info,),
            [grad, unit_two[part], slope[part], wf, wd],
            [((half, hid), bf16)] + [((RB // 2, width), bf16)] * 2 + [((RB, width), f32), ((8, width), f32)],
        )

    def mlp_out(part, gate):
        return call(
            mlp_out_kernel,
            f"mlp_out{part}",
            (info,),
            [after(act[part], gate), wd],
            [((RB, width), bf16), ((RB, width), f32)],
        )

    def add(part, keep, *received):
        return call(add_kernel, f"add{part}", (), [keep, *received], [((RB, width), bf16)])[0]

    forward_a = mlp(0, norms, (ctx_a, ca, xa, xca))
    forward_b = mlp(1, after(norms, forward_a[0]), (ctx_b, cb, xb, xcb))
    resid, unit_two, a2, act, slope = zip(forward_a, forward_b)
    start, last = fence(three.start, act[1])
    (wd,) = call(
        functools.partial(assemble_three_kernel, pieces),
        "assemble_three",
        (info,),
        [start, *three.pieces()[1:]] if ring else three.pieces(),
        [((width, hid), bf16)],
    )
    dpre_a, top_a, bottom_a, dkeep_a, nacc_a = mlp_back(0, after(grad_out, act[1]))
    received_a = swap_core(top_a), swap_core(bottom_a)
    dpre_b, top_b, bottom_b, dkeep_b, nacc_b = mlp_back(1, after(grad_out, dpre_a))
    mine_a = add(0, after(dkeep_a, dpre_b), *received_a)
    received_b = swap_core(top_b), swap_core(bottom_b)
    across_a = swap_x(mine_a)

    piece = lambda w: [((width // pieces if ring else 16, w), bf16)] * 2
    mlp_grad, mlp_fw, mlp_bw = call(
        mlp_grad_kernel,
        "mlp_grad",
        (info,),
        [after(a2[0], mine_a), a2[1], dpre_a, dpre_b, grad_out, act[0], act[1]],
        [((width, 2 * hid), bf16 if ring else f32)] + piece(2 * hid),
    )
    mlp_sum = Scatter("mlp", info, mlp_grad, mlp_fw, mlp_bw)
    mlp_sum.step()
    mine_b = add(1, after(dkeep_b, mlp_grad), *received_b)
    across_b = swap_x(mine_b)
    def norm_two(part, mine, across):
        return call(
            functools.partial(norm_two_kernel, part),
            f"norm_two{part}",
            (info,),
            [resid[part], mine, across, grad_out, norms],
            [((RB, width), f32)] + [((RB // 2, width), bf16)] * 2,
        )

    def attend_back(stage, base, blocks, given, part, before, outs):
        return call(
            functools.partial(attend_back_kernel, heads, base, blocks, stage),
            f"attend_back{stage}",
            (info, src),
            [mixed, values, *given, own_w, lse[part], context[part], *before],
            outs,
            vmem=24,
        )

    dr_a, *ab_a = norm_two(0, after(mine_a, mine_b), across_a)
    partner = [swap_core(v) for v in ab_a]
    ab_one, dq_a, dk, dv = attend_back(
        0, 0, 2, [*ab_a, *partner], 0, [], [((half, width), bf16)] + [((half, cw), f32)] * 3
    )
    mlp_sum.a, mlp_sum.b, dq_a = fence(mlp_sum.a, mlp_sum.b, dq_a)
    mlp_sum.step()
    ysend_a, ykeep_a = mlp_out(0, dq_a)
    ysend_b, ykeep_b = mlp_out(1, ysend_a)
    yreceived_a, yreceived_b = swap_core(ysend_a), swap_core(ysend_b)
    rows_mine, rows_sent = call(
        output_rows_kernel,
        "output_rows",
        (info,),
        [ykeep_a, ykeep_b, yreceived_a, yreceived_b],
        [((RB, width), f32), ((RB, width), bf16)],
    )
    dr_b, *ab_b = norm_two(1, after(mine_b, ysend_b), across_b)
    partner = [swap_core(v) for v in ab_b]
    rows_received = swap_x(after(rows_sent, dr_b))
    top = half + RB
    ab_two, dq_b, dk, dv = attend_back(
        1, half, 1, [*ab_b, *partner], 1, [dk, dv], [((half, width), bf16), ((RB, cw), f32)] + [((top, cw), f32)] * 2
    )
    mlp_sum.a, mlp_sum.b, dq_b = fence(mlp_sum.a, mlp_sum.b, dq_b)
    mlp_sum.step()
    dmixed, dreused = attend_back(
        2,
        top,
        1,
        [ab_two],
        1,
        [after(dk, mlp_sum.last) if ring else dk, dv, dq_a, dq_b],
        [((count, cols), bf16), ((cw, count), bf16)],
    )

    *isend, ikeep, sums = call(
        input_kernel,
        "input",
        (info,),
        [dmixed, qkv_full, unit_one, nacc_a, nacc_b],
        [((RB, width), bf16)] * 2 + [((half, width), f32), ((8, width), f32)],
    )
    qkv_grad, qkv_fw, qkv_bw = call(
        qkv_grad_kernel,
        "qkv_grad",
        (info,),
        [a1, dmixed, ab_one, ab_two, context[0], context[1], sums],
        [((width, cols + cw + LANES), bf16 if ring else f32)] + piece(cols + cw + LANES),
        scratch=[pltpu.VMEM((LANES, width), f32)],
    )
    qkv_sum = Scatter("qkv", info, qkv_grad, qkv_fw, qkv_bw)
    mlp_sum.a, mlp_sum.b, qkv_sum.a, qkv_sum.b, rows_received = fence(
        mlp_sum.a, mlp_sum.b, qkv_sum.a, qkv_sum.b, rows_received
    )
    mlp_sum.step()
    qkv_sum.step()
    gathered = [swap_core(v) for v in isend]
    mine, sent = call(
        to_rows_kernel, "to_rows", (info,), [ikeep, *gathered], [((RB, width), f32), ((RB, width), bf16)]
    )
    across, dx = swap_x(sent), swap_x(dreused)
    qkv_sum.a, qkv_sum.b, sent = fence(qkv_sum.a, qkv_sum.b, sent)
    qkv_sum.step()
    (block_out,) = call(
        output_kernel,
        "output",
        (info,),
        [resid[0], resid[1], rows_mine, rows_received],
        [((RB, width), bf16)],
    )
    qkv_sum.a, qkv_sum.b, mlp_sum.a, block_out = fence(qkv_sum.a, qkv_sum.b, mlp_sum.a, block_out)
    qkv_sum.step()
    fc_new, down_new = update(
        ("fc", "down"),
        info,
        mlp_grad,
        mlp_sum.ends(),
        [fc_weight, fc_moment, fc_second],
        [down_weight.T, down_moment.T, down_second.T],
        False,
    )
    qkv_sum.a, qkv_sum.b, across, dx, *fc_new = fence(qkv_sum.a, qkv_sum.b, across, dx, *fc_new)
    down_new = tuple(v.T for v in down_new)
    qkv_sum.step()
    (input_grad,) = call(
        norm_one_kernel,
        "norm_one",
        (info,),
        [tokens, mine, across, dr_a, dr_b, norms],
        [((RB, width), f32)],
    )
    dx, dreused = fence(dx, dreused)
    dc, dxc = swap_core(dreused), swap_core(dx)
    (first_grad,) = call(
        functools.partial(first_kernel, heads),
        "first",
        (info, src),
        [dreused, dc, dx, dxc],
        [((cw, count), f32)],
    )
    qkv_sum.a, input_grad, first_grad = fence(qkv_sum.a, input_grad, first_grad)
    if ring:
        (sums,) = call(
            norm_sum_kernel,
            "norm_sum",
            (info,),
            [qkv_grad, *qkv_sum.ends()],
            [((8, LANES), f32)],
            scratch=[pltpu.VMEM((LANES, LANES), f32)],
        )
        (sums,) = call(sum_kernel, "sum", (), [sums, swap_core(sums)], [(sums.shape, f32)])
        received = swap_x(sums)
    qkv_new, proj_new = update(
        ("qkv", "proj"),
        info,
        qkv_grad,
        qkv_sum.ends(),
        [qkv_weight, qkv_moment, qkv_second],
        [proj_weight, proj_moment, proj_second],
        True,
    )
    if ring:
        norm_new = call(
            norm_adam_kernel,
            "adam_norm",
            (),
            [sums, received, norm_params, norm_moment, norm_second],
            [(norm_params.shape, f32)] * 3,
        )
    else:
        own = lax.psum_scatter(lax.psum(sums, "mp"), "dp", scatter_dimension=1, tiled=True)[:4]
        norm_new = adamw(norm_params, norm_moment, norm_second, own, RATES["norm"], 0.0)
    return (block_out, input_grad, first_grad.T, *qkv_new, *proj_new, *fc_new, *down_new, *norm_new)


def solution(mesh):
    both = P("dp", "mp")
    turned = P("mp", "dp")
    rows = P("dp", None)
    every = P(None, "dp")
    state = (both, turned, both, turned, every)
    return jax.shard_map(
        local,
        mesh=mesh,
        in_specs=(rows, both, P(), rows) + state * 3,
        out_specs=(P(("dp", "mp"), None), P(("dp", "mp"), None), both)
        + (both,) * 3
        + (turned,) * 3
        + (both,) * 3
        + (turned,) * 3
        + (every,) * 3,
        check_vma=False,
    )
```

```python
import functools

import jax
import jax.numpy as jnp
import numpy as np
from jax import lax
from jax.experimental import pallas as pl
from jax.experimental.pallas import tpu as pltpu
from jax.sharding import PartitionSpec as P

H = 12
HD = 64
ADAM_STEP = 5
EPS = 1e-05
MASKED = -1e30
RB = 256
LANES = 128
RING = (0, 2, 4, 6, 7, 5, 3, 1)
OFFSETS = (0, -1, -2, -3, -4, 1, 2, 3)
GELU_A = 0.7978845608028654
GELU_B = 0.044715
RATES = {"qkv": 0.06, "proj": 0.15, "fc": 0.04, "down": 0.03, "norm": 0.3}

bf16 = jnp.bfloat16
f32 = jnp.float32


def dot(a, b):
    return jnp.dot(a, b, preferred_element_type=f32)


def dot_nt(a, b):
    return lax.dot_general(a, b, (((1,), (1,)), ((), ())), preferred_element_type=f32)


def dot_tn(a, b):
    return lax.dot_general(a, b, (((0,), (0,)), ((), ())), preferred_element_type=f32)


class Place:
    def __init__(self):
        self.mp, self.dp = lax.axis_index("mp"), lax.axis_index("dp")

    def __getitem__(self, k):
        if k < 4:
            return (self.mp % 2, self.mp // 2, self.mp, self.dp)[k]
        if lax.axis_size("dp") != len(RING):
            return 0
        z, y = self.dp // 2, self.dp % 2
        at = (jnp.where(y == 0, z, 7 - z) + OFFSETS[k - 4] + 8) % 8
        return jnp.where(at < 4, 2 * at, 2 * (7 - at) + 1)


HERE = object()


def call(kernel, name, scalars, ins, outs, scratch=(), vmem=16, far=False):
    if HERE in scalars:
        inner = kernel
        kernel = lambda *refs: inner(Place(), *refs)
        scalars = scalars[1:]
    smem = pl.BlockSpec(memory_space=pltpu.SMEM)
    full = pl.BlockSpec(memory_space=pltpu.VMEM)
    given = pl.BlockSpec(memory_space=pltpu.HBM) if far else full
    return pl.pallas_call(
        kernel,
        in_specs=[smem] * len(scalars) + [given] * len(ins),
        out_specs=[full] * len(outs),
        out_shape=[jax.ShapeDtypeStruct(sh, dt) for sh, dt in outs],
        scratch_shapes=list(scratch),
        compiler_params=pltpu.CompilerParams(vmem_limit_bytes=vmem * 1024 * 1024),
        cost_estimate=pl.CostEstimate(flops=1, bytes_accessed=1, transcendentals=0),
        name=name,
    )(*scalars, *ins)


def block(index, size=RB):
    if isinstance(index, int):
        return slice(index * size, (index + 1) * size)
    return pl.ds(pl.multiple_of(index * size, size), size)


def fetch(pairs, sems):
    copies = [pltpu.make_async_copy(src, dst, sems.at[k]) for k, (src, dst) in enumerate(pairs)]
    for copy in copies:
        copy.start()
    for copy in copies:
        copy.wait()


def prep_one_kernel(q_ref, n_ref, out, q, norms, turn, sems):
    rows, cols = q.shape
    turn[...] = jnp.zeros(turn.shape, f32)
    fetch([(q_ref, q), (n_ref, norms)], sems)
    turn[: norms.shape[0], :rows] = norms[...]
    out[:, :cols] = q[...].astype(bf16)
    out[:, cols:] = turn[...].T[:rows, : out.shape[1] - cols].astype(bf16)


def prep_two_kernel(p_ref, f_ref, d_ref, proj, fc, down, p, f, d, turn, sems):
    rows = proj.shape[0]
    turn[...] = jnp.zeros(turn.shape, f32)
    fetch([(p_ref, p), (f_ref, f), (d_ref, d)], sems)
    turn[:, :rows] = p[...]
    proj[...] = turn[...].T[:rows].astype(bf16)
    fc[...] = f[...].astype(bf16)
    down[...] = d[...].astype(bf16)


def join_kernel(f_ref, own, across, out):
    hid, cw = f_ref.shape[1], own.shape[1]
    out[:, :hid] = f_ref[...]
    out[:, hid:] = jnp.concatenate([own[...], across[...]], 1)


def norm_stats(values):
    center = values - jnp.mean(values, axis=-1, keepdims=True)
    scale = lax.rsqrt(jnp.mean(center * center, axis=-1, keepdims=True) + EPS)
    return center * scale, scale


def unit_kernel(x_ref, unit_ref):
    for i in range(x_ref.shape[0] // RB):
        at = slice(i * RB, (i + 1) * RB)
        unit_ref[at] = norm_stats(x_ref[at].astype(f32))[0]


def fetch_kernel(src, out, sem):
    copy = pltpu.make_async_copy(src, out, sem)
    copy.start()
    copy.wait()


def loop(count, body):
    lax.fori_loop(0, count, lambda i, carry: (body(i), carry)[1], 0)


def qkv_kernel(n, heads, info, unit_ref, *refs):
    pieces, (a1_ref, m_ref, v_ref, w_ref, norm_ref) = refs[:n], refs[n:]
    cols = m_ref.shape[1]
    base = cols // LANES * LANES
    rows = w_ref.shape[0] // n
    for k, piece in enumerate(pieces):
        w_ref[block(info[4 + k], rows), :] = piece[...]
    turned = w_ref[:, base : base + LANES].astype(f32).T
    norm_ref[...] = turned[cols - base : cols - base + 8]

    def step(i):
        at = block(i)
        a1 = (unit_ref[at, :] * norm_ref[0:1] + norm_ref[1:2]).astype(bf16)
        a1_ref[at, :] = a1
        mixed = dot(a1, w_ref[:, :cols])
        m_ref[at, :] = mixed.astype(bf16)
        for h in range(heads):
            fresh = mixed[:, (3 * h + 2) * HD : (3 * h + 3) * HD]
            v_ref[h * HD : (h + 1) * HD, at] = fresh.T.astype(bf16)

    loop(m_ref.shape[0] // RB, step)


def values_kernel(heads, info, src, fresh, f0, f1, f2, f3, v_ref):
    mp = info[2]
    for h in range(heads):
        source = src[mp * heads + h]
        held = source // heads
        mine = slice(h * HD, (h + 1) * HD)

        @pl.when(source >= H)
        def _():
            v_ref[mine, :] = fresh[mine, :]

        for r, first in enumerate((f0, f1, f2, f3)):

            @pl.when((source < H) & (held == mp ^ r))
            def _():
                v_ref[mine, :] = first[block(source - held * heads, HD), :]


def masked_tile():
    keys = lax.broadcasted_iota(jnp.int32, (RB, RB), 0)
    queries = lax.broadcasted_iota(jnp.int32, (RB, RB), 1)
    return keys <= queries


def attend_kernel(heads, base, m_ref, v_ref, c_ref, lse_ref, keys_ref, query_ref, turned):
    keep = masked_tile()
    blocks = c_ref.shape[0] // RB
    top = base + blocks * RB
    lse_ref[...] = jnp.zeros(lse_ref.shape, f32)
    for h in range(heads):
        keys_ref[h] = m_ref[:top, (3 * h + 1) * HD : (3 * h + 2) * HD]
        query_ref[h] = m_ref[base:top, 3 * h * HD : (3 * h + 1) * HD] * bf16(HD**-0.5)

    def step(h):
        mine = block(h, HD)
        for i in range(blocks):
            lo = base + i * RB
            hi = lo + RB
            at = slice(i * RB, (i + 1) * RB)
            query = query_ref[h, at]
            diag = jnp.where(keep, dot_nt(keys_ref[h, lo:hi], query), MASKED)
            peak = jnp.max(diag, 0, keepdims=True)
            if lo:
                left = dot_nt(keys_ref[h, :lo], query)
                peak = jnp.maximum(peak, jnp.max(left, 0, keepdims=True))
            diag = jnp.exp(diag - peak)
            total = jnp.sum(diag, 0, keepdims=True)
            if lo:
                left = jnp.exp(left - peak)
                total += jnp.sum(left, 0, keepdims=True)
            inverse = 1.0 / total
            context = dot(v_ref[mine, lo:hi], (diag * inverse).astype(bf16))
            if lo:
                context += dot(v_ref[mine, :lo], (left * inverse).astype(bf16))
            turned[mine, at] = context
            lse_ref[pl.ds(h, 1), at] = peak + jnp.log(total)

    loop(heads, step)
    c_ref[...] = turned[...].T.astype(bf16)


def assemble_two_kernel(n, info, *refs):
    pieces, (wf, own, across, turn) = refs[:n], refs[n:]
    width, hid = wf.shape
    cw = own.shape[0]
    rows = width // n
    for k, piece in enumerate(pieces):
        at = block(info[4 + k], rows)
        wf[at, :] = piece[:, :hid]
        turn[at, :] = piece[:, hid:]
    pair = turn[...].T
    own[...] = pair[:cw]
    across[...] = pair[cw:]


def assemble_three_kernel(n, info, *refs):
    pieces, (wd,) = refs[:n], refs[n:]
    rows = wd.shape[0] // n
    for k, piece in enumerate(pieces):
        wd[block(info[4 + k], rows), :] = piece[...]


def mlp_kernel(part, x_ref, norm_ref, c0, c1, c2, c3, w0, w1, w2, w3, wf, r_ref, unit_ref, a2_ref, g_ref, slope_ref):
    def step(i):
        at = block(i)
        resid = x_ref[block(2 * part + i), :].astype(f32) + (
            (dot(c0[at, :], w0[...]) + dot(c1[at, :], w1[...]))
            + (dot(c2[at, :], w2[...]) + dot(c3[at, :], w3[...]))
        )
        r_ref[at, :] = resid
        unit, _ = norm_stats(resid)
        unit_ref[at, :] = unit
        a2 = (unit * norm_ref[2:3] + norm_ref[3:4]).astype(bf16)
        a2_ref[at, :] = a2
        u = dot(a2, wf[...])
        square = u * u
        t = jnp.tanh(GELU_A * u * (1.0 + GELU_B * square))
        g_ref[at, :] = (0.5 * u * (1.0 + t)).astype(bf16)
        slope_ref[at, :] = 0.5 * (1.0 + t) + 0.5 * u * (1.0 - t * t) * (
            GELU_A * (1.0 + 3.0 * GELU_B * square)
        )

    loop(2, step)


def mlp_back_kernel(part, info, e_ref, unit_ref, slope_ref, wf, wd, du_ref, top, bottom, keep, nacc):
    core = info[0]
    nacc[...] = jnp.zeros(nacc.shape, f32)

    def step(i):
        spot = core if i else 1 - core
        at = block(spot)
        du = (dot(e_ref[block(2 * part + spot), :], wd[...]) * slope_ref[at, :]).astype(bf16)
        du_ref[at, :] = du
        grad = dot_nt(du, wf[...])
        nacc[2:3] += jnp.sum(grad * unit_ref[at, :], 0, keepdims=True)
        nacc[3:4] += jnp.sum(grad, 0, keepdims=True)
        keep[...] = grad

        @pl.when(i < 1)
        def _():
            top[...] = grad[: RB // 2].astype(bf16)
            bottom[...] = grad[RB // 2 :].astype(bf16)

    for i in range(2):
        step(i)


def mlp_out_kernel(info, g_ref, wd, ysend, ykeep):
    ykeep[...] = dot_nt(g_ref[block(info[0]), :], wd[...])
    ysend[...] = dot_nt(g_ref[block(1 - info[0]), :], wd[...]).astype(bf16)


def add_kernel(keep, top, bottom, out):
    out[: RB // 2] = (keep[: RB // 2] + top[...].astype(f32)).astype(bf16)
    out[RB // 2 :] = (keep[RB // 2 :] + bottom[...].astype(f32)).astype(bf16)


def starts(info, full, fw, bw):
    rows = fw.shape[0]
    fw[...] = full[block(info[4 + OFFSETS.index(-4)], rows), :].astype(bf16)
    bw[...] = full[block(info[4 + OFFSETS.index(-3)], rows), :].astype(bf16)


def mlp_grad_kernel(info, a2a, a2b, dua, dub, e_ref, ga, gb, out, fw, bw):
    hid = dua.shape[1]
    half = dua.shape[0]

    def step(j):
        at = block(j)
        out[at, :hid] = (dot_tn(a2a[:, at], dua[...]) + dot_tn(a2b[:, at], dub[...])).astype(out.dtype)
        out[at, hid:] = (dot_tn(e_ref[:half, at], ga[...]) + dot_tn(e_ref[half:, at], gb[...])).astype(out.dtype)

    for j in range(out.shape[0] // RB):
        step(j)
    starts(info, out, fw, bw)


def hop_kernel(ahead, behind, info, full, a, b, a_out, b_out):
    rows = a.shape[0]
    for offset, value, out in ((ahead, a, a_out), (behind, b, b_out)):
        term = full[block(info[4 + OFFSETS.index(offset)], rows), :]
        out[...] = (value[...].astype(f32) + term.astype(f32)).astype(bf16)


def hop_last_kernel(info, full, a, a_out):
    term = full[block(info[4 + OFFSETS.index(1)], a.shape[0]), :]
    a_out[...] = (a[...].astype(f32) + term.astype(f32)).astype(bf16)


def norm_back(unit, scale, gain, grad):
    dy = grad * gain
    return scale * (
        dy - jnp.mean(dy, -1, keepdims=True) - unit * jnp.mean(dy * unit, -1, keepdims=True)
    )


def norm_two_kernel(part, info, r_ref, own, received, e_ref, norm_ref, dr_ref, top, bottom):
    unit, scale = norm_stats(r_ref[block(info[0]), :])
    grad = own[...].astype(f32) + received[...].astype(f32)
    e = e_ref[block(2 * part + info[0]), :].astype(f32)
    dr = e + norm_back(unit, scale, norm_ref[2:3], grad)
    dr_ref[...] = dr
    top[...] = dr[: RB // 2].astype(bf16)
    bottom[...] = dr[RB // 2 :].astype(bf16)


def attend_back_kernel(heads, base, blocks, stage, info, src, m_ref, v_ref, *refs):
    if stage < 2:
        halves, refs = refs[:4], refs[4:]
    else:
        ab_in, refs = refs[0], refs[1:]
    wp, lse_ref, c_ref, *refs = refs
    if stage:
        dk_in, dv_in, *refs = refs
    if stage == 0:
        ab_ref, dq_ref, dk_ref, dv_ref = refs
    elif stage == 1:
        ab_ref, dq_ref, dk_ref, dv_ref = refs
    else:
        dq_first, dq_second, dm_ref, dvr_ref = refs
    keep = masked_tile()
    core = info[0]
    if stage < 2:
        for k in range(2):
            ab_ref[block(2 * core + k, RB // 2), :] = halves[k][...]
            ab_ref[block(2 * (1 - core) + k, RB // 2), :] = halves[2 + k][...]
        source, skip = ab_ref, 0
    else:
        source, skip = ab_in, ab_in.shape[0] - blocks * RB
    top = base + blocks * RB
    tiles = top // RB
    dctx = [dot_nt(source[skip + i * RB : skip + (i + 1) * RB], wp[...]).astype(bf16) for i in range(blocks)]
    first = c_ref.shape[0] - blocks * RB if stage == 2 else 0
    own_rows = [slice(first + i * RB, first + (i + 1) * RB) for i in range(blocks)]
    terms = [(d.astype(f32) * c_ref[at].astype(f32)).T for d, at in zip(dctx, own_rows)]
    dq_t = [[None] * heads for _ in range(blocks)]
    dks, dvs = [], []
    for h in range(heads):
        lane = slice(h * HD, (h + 1) * HD)
        keys = m_ref[:top, (3 * h + 1) * HD : (3 * h + 2) * HD]
        keys_t = keys.T
        values = v_ref[h * HD : (h + 1) * HD, :top].T
        dk = [None] * tiles
        dv = [None] * tiles
        if stage:
            for t in range(base // RB):
                dk[t] = dk_in[t * RB : (t + 1) * RB, lane]
                dv[t] = dv_in[t * RB : (t + 1) * RB, lane]
        for i in range(blocks):
            lo = base + i * RB
            hi = lo + RB
            query = m_ref[lo:hi, 3 * h * HD : (3 * h + 1) * HD] * bf16(HD**-0.5)
            dc = dctx[i][:, lane]
            lse = lse_ref[h : h + 1, own_rows[i]]
            prob = jnp.exp(dot_nt(keys[:hi], query) - lse)
            own = jnp.where(keep, prob[lo:], 0.0)
            prob = jnp.concatenate([prob[:lo], own], 0) if lo else own
            dprob = dot_nt(values[:hi], dc)
            inner = jnp.sum(terms[i][lane], 0, keepdims=True)
            more_v = dot(prob.astype(bf16), dc)
            ds = (prob * (dprob - inner)).astype(bf16)
            more_k = dot(ds, query)
            dq_t[i][h] = dot(keys_t[:, :hi], ds) * HD**-0.5
            for t in range(hi // RB):
                spot = slice(t * RB, (t + 1) * RB)
                dv[t] = more_v[spot] if dv[t] is None else dv[t] + more_v[spot]
                dk[t] = more_k[spot] if dk[t] is None else dk[t] + more_k[spot]
        dks.append(dk)
        dvs.append(dv)
    dq = [jnp.concatenate(dq_t[i], 0).T for i in range(blocks)]
    if stage < 2:
        for i in range(blocks):
            dq_ref[i * RB : (i + 1) * RB] = dq[i]
        for t in range(tiles):
            dk_ref[t * RB : (t + 1) * RB] = jnp.concatenate([dks[h][t] for h in range(heads)], 1)
            dv_ref[t * RB : (t + 1) * RB] = jnp.concatenate([dvs[h][t] for h in range(heads)], 1)
        return
    mp = info[2]
    fresh = [jnp.where(src[mp * heads + h] < H, 0.0, 1.0) for h in range(heads)]
    split = dq_first.shape[0]
    for t in range(tiles):
        spot = slice(t * RB, (t + 1) * RB)
        parts = []
        for h in range(heads):
            lane = slice(h * HD, (h + 1) * HD)
            if t * RB < split:
                dqh = dq_first[spot, lane]
            elif t * RB < base:
                dqh = dq_second[t * RB - split : (t + 1) * RB - split, lane]
            else:
                dqh = dq[t - base // RB][:, lane]
            parts += [dqh, dks[h][t], dvs[h][t] * fresh[h]]
            dvr_ref[h * HD : (h + 1) * HD, spot] = dvs[h][t].T.astype(bf16)
        dm_ref[spot, :] = jnp.concatenate(parts, 1).astype(bf16)


def input_kernel(info, dm_ref, w_ref, unit_ref, na, nb, s0, s1, keep, sums):
    core = info[0]
    cols = dm_ref.shape[1]
    gain = jnp.zeros((1, unit_ref.shape[1]), f32)
    shift = gain
    for own in range(2):
        for half, out in enumerate((s0, s1)):
            at = block(2 * half + (core if own else 1 - core))
            grad = dot_nt(dm_ref[at, :], w_ref[:, :cols])
            gain += jnp.sum(grad * unit_ref[at, :], 0, keepdims=True)
            shift += jnp.sum(grad, 0, keepdims=True)
            if own:
                keep[block(half)] = grad
            else:
                out[...] = grad.astype(bf16)
    sums[...] = na[...] + nb[...]
    sums[0:1] = gain
    sums[1:2] = shift


def to_rows_kernel(info, keep, r0, r1, mine, sent):
    low = info[1] == 0
    first = keep[:RB] + r0[...].astype(f32)
    second = keep[RB:] + r1[...].astype(f32)
    mine[...] = jnp.where(low, first, second)
    sent[...] = jnp.where(low, second, first).astype(bf16)


def output_rows_kernel(info, ka, kb, ra, rb, mine, sent):
    low = info[1] == 0
    first = ka[...] + ra[...].astype(f32)
    second = kb[...] + rb[...].astype(f32)
    mine[...] = jnp.where(low, first, second)
    sent[...] = jnp.where(low, second, first).astype(bf16)


def output_kernel(info, ra, rb, mine, received, out):
    at = block(info[0])
    resid = jnp.where(info[1] == 0, ra[at, :], rb[at, :])
    out[...] = (resid + mine[...] + received[...].astype(f32)).astype(bf16)


def qkv_grad_kernel(info, a1_ref, dm_ref, aba, abb, ca, cb, sums, out, fw, bw, turn):
    cols, width = dm_ref.shape[1], sums.shape[1]
    turn[...] = jnp.zeros(turn.shape, f32)
    turn[: sums.shape[0]] = sums[...]

    def step(j):
        at = block(j)
        grad = dot_tn(a1_ref[:, at], dm_ref[...])
        proj = dot_tn(aba[:, at], ca[...]) + dot_tn(abb[:, at], cb[...])
        out[at, : out.shape[1] - LANES] = jnp.concatenate([grad, proj], 1).astype(out.dtype)
        out[at, out.shape[1] - LANES :] = turn[:, at].T.astype(out.dtype)

    for j in range(out.shape[0] // RB):
        step(j)
    starts(info, out, fw, bw)


def norm_one_kernel(info, x_ref, own, received, dra, drb, norm_ref, out):
    unit, scale = norm_stats(x_ref[block(info[2]), :].astype(f32))
    grad = own[...] + received[...].astype(f32)
    dr = jnp.where(info[1] == 0, dra[...], drb[...])
    out[...] = dr + norm_back(unit, scale, norm_ref[0:1], grad)


def first_kernel(heads, info, src, d0, d1, d2, d3, out):
    mp = info[2]
    out[...] = jnp.zeros(out.shape, f32)
    for g in range(heads):
        user = jnp.int32(H)
        for h in range(H):
            user = jnp.where(src[h] == mp * heads + g, h, user)
        held = user // heads
        for r, ref in enumerate((d0, d1, d2, d3)):

            @pl.when((user < H) & (held == mp ^ r))
            def _():
                out[g * HD : (g + 1) * HD, :] = ref[block(user - held * heads, HD), :].astype(f32)


def adamw(master, moment, second, grad, rate, weighted):
    moment_new = 0.9 * moment + 0.1 * grad
    second_new = 0.999 * second + 0.001 * grad * grad
    mean_hat = moment_new / (1.0 - 0.9**ADAM_STEP)
    var_hat = second_new / (1.0 - 0.999**ADAM_STEP)
    master_new = master - rate * (mean_hat / (jnp.sqrt(var_hat) + 1e-08) + weighted * master)
    return (master_new, moment_new, second_new)


def adam_kernel(names, turned, info, full, a, b, *refs):
    ins, outs = refs[:6], refs[6:12]
    rows = a.shape[0]
    grad = a[...].astype(f32) + b[...].astype(f32)
    grad += full[block(info[4], rows), :].astype(f32)
    cols = ins[0].shape[1]
    if turned:
        grad = grad[:, : cols + ins[3].shape[0]]
    second = grad[:, cols:]
    if turned:
        second = jnp.concatenate([second, jnp.zeros((LANES - rows, second.shape[1]), f32)], 0).T[:, :rows]
    for k, (name, part) in enumerate(zip(names, (grad[:, :cols], second))):
        new = adamw(*[r[...] for r in ins[3 * k : 3 * k + 3]], part, RATES[name], 0.1)
        for ref, value in zip(outs[3 * k : 3 * k + 3], new):
            ref[...] = value


def norm_sum_kernel(info, full, a, b, out, turn):
    rows, width = a.shape
    at = slice(width - LANES, width)
    grad = a[:, at].astype(f32) + b[:, at].astype(f32) + full[block(info[4], rows), at].astype(f32)
    turn[...] = jnp.zeros(turn.shape, f32)
    turn[:rows] = grad
    out[...] = turn[...].T[:8]


def norm_adam_kernel(sums, received, w, m, s, w_out, m_out, s_out):
    rows, cols = w.shape
    grad = (sums[...] + received[...])[:rows, :cols]
    new = adamw(w[...], m[...], s[...], grad, RATES["norm"], 0.0)
    for ref, value in zip((w_out, m_out, s_out), new):
        ref[...] = value


def sum_kernel(a, b, out):
    out[...] = a[...] + b[...]


def swap_core(value):
    return lax.ppermute(value, "mp", [(i, i ^ 1) for i in range(4)])


def swap_x(value):
    return lax.ppermute(value, "mp", [(i, i ^ 2) for i in range(4)])


FORWARD = [(RING[i], RING[(i + 1) % 8]) for i in range(8)]
BACKWARD = [(b, a) for a, b in FORWARD]


def ahead(value):
    return lax.ppermute(value, "dp", FORWARD)


def behind(value):
    return lax.ppermute(value, "dp", BACKWARD)


def after(value, *others):
    return lax.optimization_barrier((value,) + others)[0]


class Gather:
    def __init__(self, piece):
        self.ring = lax.axis_size("dp") == len(RING)
        self.start = self.a = self.b = piece
        self.ahead, self.behind = [], []

    def step(self, *gates):
        if not self.ring:
            return
        self.a, self.b = lax.optimization_barrier((self.a, self.b) + gates)[:2]
        self.a = ahead(self.a)
        self.ahead.append(self.a)
        if len(self.behind) < 3:
            self.b = behind(self.b)
            self.behind.append(self.b)

    def pieces(self):
        if not self.ring:
            return [lax.all_gather(self.start, "dp", axis=0, tiled=True)]
        return [self.start] + self.ahead + self.behind


class Scatter:
    def __init__(self, name, info, full, fw, bw):
        self.ring = lax.axis_size("dp") == len(RING)
        self.name, self.info, self.full, self.a, self.b = name, info, full, fw, bw
        self.steps = 0

    def step(self, *gates):
        if not self.ring:
            return
        self.a = after(self.a, *gates)
        k = 4 - self.steps
        shape = (self.a.shape, bf16)
        if k in (3, 2):
            kernel = functools.partial(hop_kernel, k, 1 - k)
            self.a, self.b = call(kernel, f"{self.name}_hop{k}", (self.info,), [self.full, self.a, self.b], [shape] * 2)
        if k == 1:
            (self.a,) = call(hop_last_kernel, f"{self.name}_hop1", (self.info,), [self.full, self.a], [shape])
        self.last = self.a
        self.a = ahead(self.a)
        if k > 1:
            self.b = behind(self.b)
        self.steps += 1

    def ends(self):
        return (self.a, self.b) if self.ring else None


def update(name, info, full, ends, firsts, seconds, turned):
    first, second = name
    outs = [(w.shape, f32) for w in firsts + seconds]
    if ends is not None:
        new = call(
            functools.partial(adam_kernel, name, turned),
            f"adam_{first}",
            (info,),
            [full, *ends, *firsts, *seconds],
            outs,
        )
        return tuple(new[:3]), tuple(new[3:])
    grad = lax.psum_scatter(full.astype(f32), "dp", scatter_dimension=0, tiled=True)
    cols = firsts[0].shape[1]
    other = grad[:, cols : cols + seconds[0].shape[0 if turned else 1]]
    return (
        adamw(*firsts, grad[:, :cols], RATES[first], 0.1),
        adamw(*seconds, other.T if turned else other, RATES[second], 0.1),
    )


def local(
    tokens_in,
    first_values,
    skip_source,
    grad_out,
    qkv_weight,
    proj_weight,
    fc_weight,
    down_weight,
    norm_params,
    qkv_moment,
    proj_moment,
    fc_moment,
    down_moment,
    norm_moment,
    qkv_second,
    proj_second,
    fc_second,
    down_second,
    norm_second,
):
    n = lax.axis_size("dp")
    ring = n == len(RING)
    pieces = n if ring else 1
    count, width = tokens_in.shape
    cols = qkv_weight.shape[1]
    heads = cols // (3 * HD)
    cw = heads * HD
    hid = fc_weight.shape[1]
    wide = -(-(cols + 4) // LANES) * LANES
    half = count // 2
    shard = qkv_weight.shape[0]
    info = HERE
    src = skip_source

    if ring:
        (ring_one,) = call(
            prep_one_kernel,
            "prep_one",
            (),
            [qkv_weight, norm_params],
            [((shard, wide), bf16)],
            scratch=[
                pltpu.VMEM((shard, cols), f32),
                pltpu.VMEM(norm_params.shape, f32),
                pltpu.VMEM((LANES, LANES), f32),
                pltpu.SemaphoreType.DMA((2,)),
            ],
            vmem=60,
            far=True,
        )
        proj_t, fc_low, down_t = call(
            prep_two_kernel,
            "prep_two",
            (),
            [after(proj_weight, ring_one), fc_weight, down_weight.T],
            [((shard, cw), bf16), ((shard, hid), bf16), ((shard, hid), bf16)],
            scratch=[
                pltpu.VMEM((cw, shard), f32),
                pltpu.VMEM((shard, hid), f32),
                pltpu.VMEM((shard, hid), f32),
                pltpu.VMEM((cw, LANES), f32),
                pltpu.SemaphoreType.DMA((3,)),
            ],
            vmem=56,
            far=True,
        )
    else:
        blank = jnp.zeros((shard, wide - cols - 4), bf16)
        ring_one = jnp.concatenate([qkv_weight.astype(bf16), norm_params.T.astype(bf16), blank], 1)
        proj_t, fc_low, down_t = proj_weight.T.astype(bf16), fc_weight.astype(bf16), down_weight.T.astype(bf16)
    fence = lambda *values: lax.optimization_barrier(values)
    fence = lambda *values: lax.optimization_barrier(values)
    one = Gather(ring_one)
    one.step()
    one.a, one.b, proj_t, tokens = fence(one.a, one.b, proj_t, tokens_in)
    one.step()
    proj_x = swap_x(proj_t)
    (unit_one,) = call(unit_kernel, "unit", (), [tokens], [((count, width), f32)])
    one.a, one.b, proj_x, unit_one = fence(one.a, one.b, proj_x, unit_one)
    one.step()
    if ring:
        (ring_two,) = call(
            join_kernel, "join", (), [fc_low, proj_t, proj_x], [((shard, hid + 2 * cw), bf16)]
        )
    else:
        ring_two = jnp.concatenate([fc_low, proj_t, proj_x], 1)
    two, three = Gather(ring_two), Gather(down_t)
    two.step()
    first_t = after(first_values.T, unit_one)
    first_x, first_c = swap_x(first_t), swap_core(first_t)
    one.a, one.b = fence(one.a, one.b)
    one.step()
    one.a, two.a, two.b, unit_one, first_x, three.a = fence(one.a, two.a, two.b, unit_one, first_x, three.a)
    if ring:
        one.ahead[-1] = one.a
    first_xc = swap_core(first_x)
    two.step()
    three.step()

    a1, mixed, fresh, qkv_full, norms = call(
        functools.partial(qkv_kernel, pieces, heads),
        "qkv",
        (info,),
        [unit_one, *one.pieces()],
        [
            ((count, width), bf16),
            ((count, cols), bf16),
            ((cw, count), bf16),
            ((width, wide), bf16),
            ((8, width), f32),
        ],
    )
    (values,) = call(
        functools.partial(values_kernel, heads),
        "values",
        (info, src),
        [fresh, first_t, first_c, first_x, first_xc],
        [((cw, count), bf16)],
    )

    def attend(part, mixed):
        return call(
            functools.partial(attend_kernel, heads, part * half),
            f"attend{part}",
            (),
            [mixed, values],
            [((half, cw), bf16), ((8, half), f32)],
            scratch=[
                pltpu.VMEM((heads, (part + 1) * half, HD), bf16),
                pltpu.VMEM((heads, half, HD), bf16),
                pltpu.VMEM((cw, half), f32),
            ],
        )

    ctx_a, lse_a = attend(0, mixed)
    two.a, two.b, three.a, three.b, ctx_a = fence(two.a, two.b, three.a, three.b, ctx_a)
    two.step()
    three.step()
    xa = swap_x(ctx_a)
    ctx_b, lse_b = attend(1, after(mixed, ctx_a))
    two.a, two.b, three.a, three.b, xa, ctx_b = fence(two.a, two.b, three.a, three.b, xa, ctx_b)
    two.step()
    three.step()
    xb = swap_x(ctx_b)
    (grad_out,) = call(
        fetch_kernel,
        "fetch",
        (),
        [after(grad_out, ctx_b)],
        [(grad_out.shape, bf16)],
        scratch=[pltpu.SemaphoreType.DMA],
        vmem=4,
        far=True,
    )
    start, xb, two_last, three.a, three.b, grad_out = fence(two.start, xb, two.a, three.a, three.b, grad_out)
    ca, xca, cb, xcb = swap_core(ctx_a), swap_core(xa), swap_core(ctx_b), swap_core(xb)
    three.step()
    context, lse = (ctx_a, ctx_b), (lse_a, lse_b)
    wf, own_w, across_w = call(
        functools.partial(assemble_two_kernel, pieces),
        "assemble_two",
        (info,),
        [start, *two.pieces()[1:]] if ring else two.pieces(),
        [((width, hid), bf16), ((cw, width), bf16), ((cw, width), bf16)],
        scratch=[pltpu.VMEM((width, 2 * cw), bf16)],
    )
    pair = own_w, swap_core(own_w), across_w, swap_core(across_w)

    def mlp(part, norms, contexts):
        return call(
            functools.partial(mlp_kernel, part),
            f"mlp{part}",
            (),
            [tokens, norms, *contexts, *pair, wf],
            [
                ((half, width), f32),
                ((half, width), f32),
                ((half, width), bf16),
                ((half, hid), bf16),
                ((half, hid), f32),
            ],
        )

    def mlp_back(part, grad):
        return call(
            functools.partial(mlp_back_kernel, part),
            f"mlp_back{part}",
            (info,),
            [grad, unit_two[part], slope[part], wf, wd],
            [((half, hid), bf16)] + [((RB // 2, width), bf16)] * 2 + [((RB, width), f32), ((8, width), f32)],
        )

    def mlp_out(part, gate):
        return call(
            mlp_out_kernel,
            f"mlp_out{part}",
            (info,),
            [after(act[part], gate), wd],
            [((RB, width), bf16), ((RB, width), f32)],
        )

    def add(part, keep, *received):
        return call(add_kernel, f"add{part}", (), [keep, *received], [((RB, width), bf16)])[0]

    forward_a = mlp(0, norms, (ctx_a, ca, xa, xca))
    forward_b = mlp(1, after(norms, forward_a[0]), (ctx_b, cb, xb, xcb))
    resid, unit_two, a2, act, slope = zip(forward_a, forward_b)
    start, last = fence(three.start, act[1])
    (wd,) = call(
        functools.partial(assemble_three_kernel, pieces),
        "assemble_three",
        (info,),
        [start, *three.pieces()[1:]] if ring else three.pieces(),
        [((width, hid), bf16)],
    )
    dpre_a, top_a, bottom_a, dkeep_a, nacc_a = mlp_back(0, after(grad_out, act[1]))
    received_a = swap_core(top_a), swap_core(bottom_a)
    dpre_b, top_b, bottom_b, dkeep_b, nacc_b = mlp_back(1, after(grad_out, dpre_a))
    mine_a = add(0, after(dkeep_a, dpre_b), *received_a)
    received_b = swap_core(top_b), swap_core(bottom_b)
    across_a = swap_x(mine_a)

    piece = lambda w: [((width // pieces if ring else 16, w), bf16)] * 2
    mlp_grad, mlp_fw, mlp_bw = call(
        mlp_grad_kernel,
        "mlp_grad",
        (info,),
        [after(a2[0], mine_a), a2[1], dpre_a, dpre_b, grad_out, act[0], act[1]],
        [((width, 2 * hid), bf16 if ring else f32)] + piece(2 * hid),
    )
    mlp_sum = Scatter("mlp", info, mlp_grad, mlp_fw, mlp_bw)
    mlp_sum.step()
    mine_b = add(1, after(dkeep_b, mlp_grad), *received_b)
    across_b = swap_x(mine_b)
    def norm_two(part, mine, across):
        return call(
            functools.partial(norm_two_kernel, part),
            f"norm_two{part}",
            (info,),
            [resid[part], mine, across, grad_out, norms],
            [((RB, width), f32)] + [((RB // 2, width), bf16)] * 2,
        )

    def attend_back(stage, base, blocks, given, part, before, outs):
        return call(
            functools.partial(attend_back_kernel, heads, base, blocks, stage),
            f"attend_back{stage}",
            (info, src),
            [mixed, values, *given, own_w, lse[part], context[part], *before],
            outs,
            vmem=24,
        )

    ysend_a, ykeep_a = mlp_out(0, mine_b)
    ysend_b, ykeep_b = mlp_out(1, mine_b)
    across_a, ysend_a, ysend_b = fence(across_a, ysend_a, ysend_b)
    dr_a, *ab_a = norm_two(0, after(mine_a, mine_b), across_a)
    partner = [swap_core(v) for v in ab_a]
    ab_one, dq_a, dk, dv = attend_back(
        0, 0, 2, [*ab_a, *partner], 0, [], [((half, width), bf16)] + [((half, cw), f32)] * 3
    )
    mlp_sum.a, mlp_sum.b, dq_a = fence(mlp_sum.a, mlp_sum.b, dq_a)
    mlp_sum.step()
    dq_a, ysend_a, ysend_b = fence(dq_a, ysend_a, ysend_b)
    yreceived_a, yreceived_b = swap_core(ysend_a), swap_core(ysend_b)
    rows_mine, rows_sent = call(
        output_rows_kernel,
        "output_rows",
        (info,),
        [ykeep_a, ykeep_b, yreceived_a, yreceived_b],
        [((RB, width), f32), ((RB, width), bf16)],
    )
    dr_b, *ab_b = norm_two(1, after(mine_b, ysend_b), across_b)
    partner = [swap_core(v) for v in ab_b]
    rows_received = swap_x(after(rows_sent, dr_b))
    top = half + RB
    ab_two, dq_b, dk, dv = attend_back(
        1, half, 1, [*ab_b, *partner], 1, [dk, dv], [((half, width), bf16), ((RB, cw), f32)] + [((top, cw), f32)] * 2
    )
    mlp_sum.a, mlp_sum.b, dq_b = fence(mlp_sum.a, mlp_sum.b, dq_b)
    mlp_sum.step()
    dmixed, dreused = attend_back(
        2,
        top,
        1,
        [ab_two],
        1,
        [after(dk, mlp_sum.last) if ring else dk, dv, dq_a, dq_b],
        [((count, cols), bf16), ((cw, count), bf16)],
    )

    *isend, ikeep, sums = call(
        input_kernel,
        "input",
        (info,),
        [dmixed, qkv_full, unit_one, nacc_a, nacc_b],
        [((RB, width), bf16)] * 2 + [((half, width), f32), ((8, width), f32)],
    )
    qkv_grad, qkv_fw, qkv_bw = call(
        qkv_grad_kernel,
        "qkv_grad",
        (info,),
        [a1, dmixed, ab_one, ab_two, context[0], context[1], sums],
        [((width, cols + cw + LANES), bf16 if ring else f32)] + piece(cols + cw + LANES),
        scratch=[pltpu.VMEM((LANES, width), f32)],
    )
    qkv_sum = Scatter("qkv", info, qkv_grad, qkv_fw, qkv_bw)
    mlp_sum.a, mlp_sum.b, qkv_sum.a, qkv_sum.b, rows_received = fence(
        mlp_sum.a, mlp_sum.b, qkv_sum.a, qkv_sum.b, rows_received
    )
    mlp_sum.step()
    qkv_sum.step()
    gathered = [swap_core(v) for v in isend]
    mine, sent = call(
        to_rows_kernel, "to_rows", (info,), [ikeep, *gathered], [((RB, width), f32), ((RB, width), bf16)]
    )
    across, dx = swap_x(sent), swap_x(dreused)
    qkv_sum.a, qkv_sum.b, sent = fence(qkv_sum.a, qkv_sum.b, sent)
    qkv_sum.step()
    (block_out,) = call(
        output_kernel,
        "output",
        (info,),
        [resid[0], resid[1], rows_mine, rows_received],
        [((RB, width), bf16)],
    )
    qkv_sum.a, qkv_sum.b, mlp_sum.a, block_out = fence(qkv_sum.a, qkv_sum.b, mlp_sum.a, block_out)
    qkv_sum.step()
    fc_new, down_new = update(
        ("fc", "down"),
        info,
        mlp_grad,
        mlp_sum.ends(),
        [fc_weight, fc_moment, fc_second],
        [down_weight.T, down_moment.T, down_second.T],
        False,
    )
    qkv_sum.a, qkv_sum.b, across, dx, *fc_new = fence(qkv_sum.a, qkv_sum.b, across, dx, *fc_new)
    down_new = tuple(v.T for v in down_new)
    qkv_sum.step()
    (input_grad,) = call(
        norm_one_kernel,
        "norm_one",
        (info,),
        [tokens, mine, across, dr_a, dr_b, norms],
        [((RB, width), f32)],
    )
    dx, dreused = fence(dx, dreused)
    dc, dxc = swap_core(dreused), swap_core(dx)
    (first_grad,) = call(
        functools.partial(first_kernel, heads),
        "first",
        (info, src),
        [dreused, dc, dx, dxc],
        [((cw, count), f32)],
    )
    qkv_sum.a, input_grad, first_grad = fence(qkv_sum.a, input_grad, first_grad)
    if ring:
        (sums,) = call(
            norm_sum_kernel,
            "norm_sum",
            (info,),
            [qkv_grad, *qkv_sum.ends()],
            [((8, LANES), f32)],
            scratch=[pltpu.VMEM((LANES, LANES), f32)],
        )
        (sums,) = call(sum_kernel, "sum", (), [sums, swap_core(sums)], [(sums.shape, f32)])
        received = swap_x(sums)
    qkv_new, proj_new = update(
        ("qkv", "proj"),
        info,
        qkv_grad,
        qkv_sum.ends(),
        [qkv_weight, qkv_moment, qkv_second],
        [proj_weight, proj_moment, proj_second],
        True,
    )
    if ring:
        norm_new = call(
            norm_adam_kernel,
            "adam_norm",
            (),
            [sums, received, norm_params, norm_moment, norm_second],
            [(norm_params.shape, f32)] * 3,
        )
    else:
        own = lax.psum_scatter(lax.psum(sums, "mp"), "dp", scatter_dimension=1, tiled=True)[:4]
        norm_new = adamw(norm_params, norm_moment, norm_second, own, RATES["norm"], 0.0)
    return (block_out, input_grad, first_grad.T, *qkv_new, *proj_new, *fc_new, *down_new, *norm_new)


def solution(mesh):
    both = P("dp", "mp")
    turned = P("mp", "dp")
    rows = P("dp", None)
    every = P(None, "dp")
    state = (both, turned, both, turned, every)
    return jax.shard_map(
        local,
        mesh=mesh,
        in_specs=(rows, both, P(), rows) + state * 3,
        out_specs=(P(("dp", "mp"), None), P(("dp", "mp"), None), both)
        + (both,) * 3
        + (turned,) * 3
        + (both,) * 3
        + (turned,) * 3
        + (every,) * 3,
        check_vma=False,
    )
```

```python
import functools

import jax
import jax.numpy as jnp
import numpy as np
from jax import lax
from jax.experimental import pallas as pl
from jax.experimental.pallas import tpu as pltpu
from jax.sharding import PartitionSpec as P

H = 12
HD = 64
ADAM_STEP = 5
EPS = 1e-05
MASKED = -1e30
RB = 256
LANES = 128
RING = (0, 2, 4, 6, 7, 5, 3, 1)
OFFSETS = (0, -1, -2, -3, -4, 1, 2, 3)
GELU_A = 0.7978845608028654
GELU_B = 0.044715
RATES = {"qkv": 0.06, "proj": 0.15, "fc": 0.04, "down": 0.03, "norm": 0.3}

bf16 = jnp.bfloat16
f32 = jnp.float32


def dot(a, b):
    return jnp.dot(a, b, preferred_element_type=f32)


def dot_nt(a, b):
    return lax.dot_general(a, b, (((1,), (1,)), ((), ())), preferred_element_type=f32)


def dot_tn(a, b):
    return lax.dot_general(a, b, (((0,), (0,)), ((), ())), preferred_element_type=f32)


class Place:
    def __init__(self):
        self.mp, self.dp = lax.axis_index("mp"), lax.axis_index("dp")

    def __getitem__(self, k):
        if k < 4:
            return (self.mp % 2, self.mp // 2, self.mp, self.dp)[k]
        if lax.axis_size("dp") != len(RING):
            return 0
        z, y = self.dp // 2, self.dp % 2
        at = (jnp.where(y == 0, z, 7 - z) + OFFSETS[k - 4] + 8) % 8
        return jnp.where(at < 4, 2 * at, 2 * (7 - at) + 1)


HERE = object()


def call(kernel, name, scalars, ins, outs, scratch=(), vmem=16, far=False):
    if HERE in scalars:
        inner = kernel
        kernel = lambda *refs: inner(Place(), *refs)
        scalars = scalars[1:]
    smem = pl.BlockSpec(memory_space=pltpu.SMEM)
    full = pl.BlockSpec(memory_space=pltpu.VMEM)
    given = pl.BlockSpec(memory_space=pltpu.HBM) if far else full
    return pl.pallas_call(
        kernel,
        in_specs=[smem] * len(scalars) + [given] * len(ins),
        out_specs=[full] * len(outs),
        out_shape=[jax.ShapeDtypeStruct(sh, dt) for sh, dt in outs],
        scratch_shapes=list(scratch),
        compiler_params=pltpu.CompilerParams(vmem_limit_bytes=vmem * 1024 * 1024),
        cost_estimate=pl.CostEstimate(flops=1, bytes_accessed=1, transcendentals=0),
        name=name,
    )(*scalars, *ins)


def block(index, size=RB):
    if isinstance(index, int):
        return slice(index * size, (index + 1) * size)
    return pl.ds(pl.multiple_of(index * size, size), size)


def fetch(pairs, sems):
    copies = [pltpu.make_async_copy(src, dst, sems.at[k]) for k, (src, dst) in enumerate(pairs)]
    for copy in copies:
        copy.start()
    for copy in copies:
        copy.wait()


def prep_one_kernel(q_ref, n_ref, out, q, norms, turn, sems):
    rows, cols = q.shape
    turn[...] = jnp.zeros(turn.shape, f32)
    fetch([(q_ref, q), (n_ref, norms)], sems)
    turn[: norms.shape[0], :rows] = norms[...]
    out[:, :cols] = q[...].astype(bf16)
    out[:, cols:] = turn[...].T[:rows, : out.shape[1] - cols].astype(bf16)


def prep_two_kernel(p_ref, f_ref, d_ref, proj, fc, down, p, f, d, turn, sems):
    rows = proj.shape[0]
    turn[...] = jnp.zeros(turn.shape, f32)
    fetch([(p_ref, p), (f_ref, f), (d_ref, d)], sems)
    turn[:, :rows] = p[...]
    proj[...] = turn[...].T[:rows].astype(bf16)
    fc[...] = f[...].astype(bf16)
    down[...] = d[...].astype(bf16)


def join_kernel(f_ref, own, across, out):
    hid, cw = f_ref.shape[1], own.shape[1]
    out[:, :hid] = f_ref[...]
    out[:, hid:] = jnp.concatenate([own[...], across[...]], 1)


def norm_stats(values):
    center = values - jnp.mean(values, axis=-1, keepdims=True)
    scale = lax.rsqrt(jnp.mean(center * center, axis=-1, keepdims=True) + EPS)
    return center * scale, scale


def unit_kernel(x_ref, unit_ref):
    for i in range(x_ref.shape[0] // RB):
        at = slice(i * RB, (i + 1) * RB)
        unit_ref[at] = norm_stats(x_ref[at].astype(f32))[0]


def fetch_kernel(src, out, sem):
    copy = pltpu.make_async_copy(src, out, sem)
    copy.start()
    copy.wait()


def loop(count, body):
    lax.fori_loop(0, count, lambda i, carry: (body(i), carry)[1], 0)


def qkv_kernel(n, heads, info, unit_ref, *refs):
    pieces, (a1_ref, m_ref, v_ref, w_ref, norm_ref) = refs[:n], refs[n:]
    cols = m_ref.shape[1]
    base = cols // LANES * LANES
    rows = w_ref.shape[0] // n
    for k, piece in enumerate(pieces):
        w_ref[block(info[4 + k], rows), :] = piece[...]
    turned = w_ref[:, base : base + LANES].astype(f32).T
    norm_ref[...] = turned[cols - base : cols - base + 8]

    def step(i):
        at = block(i)
        a1 = (unit_ref[at, :] * norm_ref[0:1] + norm_ref[1:2]).astype(bf16)
        a1_ref[at, :] = a1
        mixed = dot(a1, w_ref[:, :cols])
        m_ref[at, :] = mixed.astype(bf16)
        for h in range(heads):
            fresh = mixed[:, (3 * h + 2) * HD : (3 * h + 3) * HD]
            v_ref[h * HD : (h + 1) * HD, at] = fresh.T.astype(bf16)

    loop(m_ref.shape[0] // RB, step)


def values_kernel(heads, info, src, fresh, f0, f1, f2, f3, v_ref):
    mp = info[2]
    for h in range(heads):
        source = src[mp * heads + h]
        held = source // heads
        mine = slice(h * HD, (h + 1) * HD)

        @pl.when(source >= H)
        def _():
            v_ref[mine, :] = fresh[mine, :]

        for r, first in enumerate((f0, f1, f2, f3)):

            @pl.when((source < H) & (held == mp ^ r))
            def _():
                v_ref[mine, :] = first[block(source - held * heads, HD), :]


def masked_tile():
    keys = lax.broadcasted_iota(jnp.int32, (RB, RB), 0)
    queries = lax.broadcasted_iota(jnp.int32, (RB, RB), 1)
    return keys <= queries


def attend_kernel(heads, base, m_ref, v_ref, c_ref, lse_ref, keys_ref, query_ref, turned):
    keep = masked_tile()
    blocks = c_ref.shape[0] // RB
    top = base + blocks * RB
    lse_ref[...] = jnp.zeros(lse_ref.shape, f32)
    for h in range(heads):
        keys_ref[h] = m_ref[:top, (3 * h + 1) * HD : (3 * h + 2) * HD]
        query_ref[h] = m_ref[base:top, 3 * h * HD : (3 * h + 1) * HD] * bf16(HD**-0.5)

    def step(h):
        mine = block(h, HD)
        for i in range(blocks):
            lo = base + i * RB
            hi = lo + RB
            at = slice(i * RB, (i + 1) * RB)
            query = query_ref[h, at]
            diag = jnp.where(keep, dot_nt(keys_ref[h, lo:hi], query), MASKED)
            peak = jnp.max(diag, 0, keepdims=True)
            if lo:
                left = dot_nt(keys_ref[h, :lo], query)
                peak = jnp.maximum(peak, jnp.max(left, 0, keepdims=True))
            diag = jnp.exp(diag - peak)
            total = jnp.sum(diag, 0, keepdims=True)
            if lo:
                left = jnp.exp(left - peak)
                total += jnp.sum(left, 0, keepdims=True)
            inverse = 1.0 / total
            context = dot(v_ref[mine, lo:hi], (diag * inverse).astype(bf16))
            if lo:
                context += dot(v_ref[mine, :lo], (left * inverse).astype(bf16))
            turned[mine, at] = context
            lse_ref[pl.ds(h, 1), at] = peak + jnp.log(total)

    loop(heads, step)
    c_ref[...] = turned[...].T.astype(bf16)


def assemble_two_kernel(n, info, *refs):
    pieces, (wf, own, across, turn) = refs[:n], refs[n:]
    width, hid = wf.shape
    cw = own.shape[0]
    rows = width // n
    for k, piece in enumerate(pieces):
        at = block(info[4 + k], rows)
        wf[at, :] = piece[:, :hid]
        turn[at, :] = piece[:, hid:]
    pair = turn[...].T
    own[...] = pair[:cw]
    across[...] = pair[cw:]


def assemble_three_kernel(n, info, *refs):
    pieces, (wd,) = refs[:n], refs[n:]
    rows = wd.shape[0] // n
    for k, piece in enumerate(pieces):
        wd[block(info[4 + k], rows), :] = piece[...]


def mlp_kernel(part, x_ref, norm_ref, c0, c1, c2, c3, w0, w1, w2, w3, wf, r_ref, unit_ref, a2_ref, g_ref, slope_ref):
    def step(i):
        at = block(i)
        resid = x_ref[block(2 * part + i), :].astype(f32) + (
            (dot(c0[at, :], w0[...]) + dot(c1[at, :], w1[...]))
            + (dot(c2[at, :], w2[...]) + dot(c3[at, :], w3[...]))
        )
        r_ref[at, :] = resid
        unit, _ = norm_stats(resid)
        unit_ref[at, :] = unit
        a2 = (unit * norm_ref[2:3] + norm_ref[3:4]).astype(bf16)
        a2_ref[at, :] = a2
        u = dot(a2, wf[...])
        square = u * u
        t = jnp.tanh(GELU_A * u * (1.0 + GELU_B * square))
        g_ref[at, :] = (0.5 * u * (1.0 + t)).astype(bf16)
        slope_ref[at, :] = 0.5 * (1.0 + t) + 0.5 * u * (1.0 - t * t) * (
            GELU_A * (1.0 + 3.0 * GELU_B * square)
        )

    loop(2, step)


def mlp_back_kernel(part, info, e_ref, unit_ref, slope_ref, wf, wd, du_ref, top, bottom, keep, nacc):
    core = info[0]
    nacc[...] = jnp.zeros(nacc.shape, f32)

    def step(i):
        spot = core if i else 1 - core
        at = block(spot)
        du = (dot(e_ref[block(2 * part + spot), :], wd[...]) * slope_ref[at, :]).astype(bf16)
        du_ref[at, :] = du
        grad = dot_nt(du, wf[...])
        nacc[2:3] += jnp.sum(grad * unit_ref[at, :], 0, keepdims=True)
        nacc[3:4] += jnp.sum(grad, 0, keepdims=True)
        keep[...] = grad

        @pl.when(i < 1)
        def _():
            top[...] = grad[: RB // 2].astype(bf16)
            bottom[...] = grad[RB // 2 :].astype(bf16)

    for i in range(2):
        step(i)


def mlp_out_kernel(info, g_ref, wd, ysend, ykeep):
    ykeep[...] = dot_nt(g_ref[block(info[0]), :], wd[...])
    ysend[...] = dot_nt(g_ref[block(1 - info[0]), :], wd[...]).astype(bf16)


def add_kernel(keep, top, bottom, out):
    out[: RB // 2] = (keep[: RB // 2] + top[...].astype(f32)).astype(bf16)
    out[RB // 2 :] = (keep[RB // 2 :] + bottom[...].astype(f32)).astype(bf16)


def starts(info, full, fw, bw):
    rows = fw.shape[0]
    fw[...] = full[block(info[4 + OFFSETS.index(-4)], rows), :].astype(bf16)
    bw[...] = full[block(info[4 + OFFSETS.index(-3)], rows), :].astype(bf16)


def mlp_grad_kernel(info, a2a, a2b, dua, dub, e_ref, ga, gb, out, fw, bw):
    hid = dua.shape[1]
    half = dua.shape[0]

    def step(j):
        at = block(j)
        out[at, :hid] = (dot_tn(a2a[:, at], dua[...]) + dot_tn(a2b[:, at], dub[...])).astype(out.dtype)
        out[at, hid:] = (dot_tn(e_ref[:half, at], ga[...]) + dot_tn(e_ref[half:, at], gb[...])).astype(out.dtype)

    for j in range(out.shape[0] // RB):
        step(j)
    starts(info, out, fw, bw)


def hop_kernel(ahead, behind, info, full, a, b, a_out, b_out):
    rows = a.shape[0]
    for offset, value, out in ((ahead, a, a_out), (behind, b, b_out)):
        term = full[block(info[4 + OFFSETS.index(offset)], rows), :]
        out[...] = (value[...].astype(f32) + term.astype(f32)).astype(bf16)


def hop_last_kernel(info, full, a, a_out):
    term = full[block(info[4 + OFFSETS.index(1)], a.shape[0]), :]
    a_out[...] = (a[...].astype(f32) + term.astype(f32)).astype(bf16)


def norm_back(unit, scale, gain, grad):
    dy = grad * gain
    return scale * (
        dy - jnp.mean(dy, -1, keepdims=True) - unit * jnp.mean(dy * unit, -1, keepdims=True)
    )


def norm_two_kernel(part, info, r_ref, own, received, e_ref, norm_ref, dr_ref, ab_ref):
    unit, scale = norm_stats(r_ref[block(info[0]), :])
    grad = own[...].astype(f32) + received[...].astype(f32)
    e = e_ref[block(2 * part + info[0]), :].astype(f32)
    dr = e + norm_back(unit, scale, norm_ref[2:3], grad)
    dr_ref[...] = dr
    ab_ref[...] = dr.astype(bf16)


def attend_back_kernel(heads, base, blocks, stage, info, src, m_ref, v_ref, *refs):
    if stage < 2:
        ab_in, refs = refs[0], refs[1:]
    else:
        ab_in, refs = refs[0], refs[1:]
    wp, lse_ref, c_ref, *refs = refs
    if stage:
        dk_in, dv_in, *refs = refs
    if stage == 0:
        dq_ref, dk_ref, dv_ref = refs
    elif stage == 1:
        dq_ref, dk_ref, dv_ref = refs
    else:
        dq_first, dq_second, dm_ref, dvr_ref = refs
    keep = masked_tile()
    core = info[0]
    if stage < 2:
        source, skip = ab_in, 0
    else:
        source, skip = ab_in, ab_in.shape[0] - blocks * RB
    top = base + blocks * RB
    tiles = top // RB
    dctx = [dot_nt(source[skip + i * RB : skip + (i + 1) * RB], wp[...]).astype(bf16) for i in range(blocks)]
    first = c_ref.shape[0] - blocks * RB if stage == 2 else 0
    own_rows = [slice(first + i * RB, first + (i + 1) * RB) for i in range(blocks)]
    terms = [(d.astype(f32) * c_ref[at].astype(f32)).T for d, at in zip(dctx, own_rows)]
    dq_t = [[None] * heads for _ in range(blocks)]
    dks, dvs = [], []
    for h in range(heads):
        lane = slice(h * HD, (h + 1) * HD)
        keys = m_ref[:top, (3 * h + 1) * HD : (3 * h + 2) * HD]
        keys_t = keys.T
        values = v_ref[h * HD : (h + 1) * HD, :top].T
        dk = [None] * tiles
        dv = [None] * tiles
        if stage:
            for t in range(base // RB):
                dk[t] = dk_in[t * RB : (t + 1) * RB, lane]
                dv[t] = dv_in[t * RB : (t + 1) * RB, lane]
        for i in range(blocks):
            lo = base + i * RB
            hi = lo + RB
            query = m_ref[lo:hi, 3 * h * HD : (3 * h + 1) * HD] * bf16(HD**-0.5)
            dc = dctx[i][:, lane]
            lse = lse_ref[h : h + 1, own_rows[i]]
            prob = jnp.exp(dot_nt(keys[:hi], query) - lse)
            own = jnp.where(keep, prob[lo:], 0.0)
            prob = jnp.concatenate([prob[:lo], own], 0) if lo else own
            dprob = dot_nt(values[:hi], dc)
            inner = jnp.sum(terms[i][lane], 0, keepdims=True)
            more_v = dot(prob.astype(bf16), dc)
            ds = (prob * (dprob - inner)).astype(bf16)
            more_k = dot(ds, query)
            dq_t[i][h] = dot(keys_t[:, :hi], ds) * HD**-0.5
            for t in range(hi // RB):
                spot = slice(t * RB, (t + 1) * RB)
                dv[t] = more_v[spot] if dv[t] is None else dv[t] + more_v[spot]
                dk[t] = more_k[spot] if dk[t] is None else dk[t] + more_k[spot]
        dks.append(dk)
        dvs.append(dv)
    dq = [jnp.concatenate(dq_t[i], 0).T for i in range(blocks)]
    if stage < 2:
        for i in range(blocks):
            dq_ref[i * RB : (i + 1) * RB] = dq[i]
        for t in range(tiles):
            dk_ref[t * RB : (t + 1) * RB] = jnp.concatenate([dks[h][t] for h in range(heads)], 1)
            dv_ref[t * RB : (t + 1) * RB] = jnp.concatenate([dvs[h][t] for h in range(heads)], 1)
        return
    mp = info[2]
    fresh = [jnp.where(src[mp * heads + h] < H, 0.0, 1.0) for h in range(heads)]
    split = dq_first.shape[0]
    for t in range(tiles):
        spot = slice(t * RB, (t + 1) * RB)
        parts = []
        for h in range(heads):
            lane = slice(h * HD, (h + 1) * HD)
            if t * RB < split:
                dqh = dq_first[spot, lane]
            elif t * RB < base:
                dqh = dq_second[t * RB - split : (t + 1) * RB - split, lane]
            else:
                dqh = dq[t - base // RB][:, lane]
            parts += [dqh, dks[h][t], dvs[h][t] * fresh[h]]
            dvr_ref[h * HD : (h + 1) * HD, spot] = dvs[h][t].T.astype(bf16)
        dm_ref[spot, :] = jnp.concatenate(parts, 1).astype(bf16)


def input_kernel(info, dm_ref, w_ref, unit_ref, na, nb, s0, s1, keep, sums):
    core = info[0]
    cols = dm_ref.shape[1]
    gain = jnp.zeros((1, unit_ref.shape[1]), f32)
    shift = gain
    for own in range(2):
        for half, out in enumerate((s0, s1)):
            at = block(2 * half + (core if own else 1 - core))
            grad = dot_nt(dm_ref[at, :], w_ref[:, :cols])
            gain += jnp.sum(grad * unit_ref[at, :], 0, keepdims=True)
            shift += jnp.sum(grad, 0, keepdims=True)
            if own:
                keep[block(half)] = grad
            else:
                out[...] = grad.astype(bf16)
    sums[...] = na[...] + nb[...]
    sums[0:1] = gain
    sums[1:2] = shift


def to_rows_kernel(info, keep, r0, r1, mine, sent):
    low = info[1] == 0
    first = keep[:RB] + r0[...].astype(f32)
    second = keep[RB:] + r1[...].astype(f32)
    mine[...] = jnp.where(low, first, second)
    sent[...] = jnp.where(low, second, first).astype(bf16)


def output_rows_kernel(info, ka, kb, ra, rb, mine, sent):
    low = info[1] == 0
    first = ka[...] + ra[...].astype(f32)
    second = kb[...] + rb[...].astype(f32)
    mine[...] = jnp.where(low, first, second)
    sent[...] = jnp.where(low, second, first).astype(bf16)


def output_kernel(info, ra, rb, mine, received, out):
    at = block(info[0])
    resid = jnp.where(info[1] == 0, ra[at, :], rb[at, :])
    out[...] = (resid + mine[...] + received[...].astype(f32)).astype(bf16)


def qkv_grad_kernel(info, a1_ref, dm_ref, aba, abb, ca, cb, sums, out, fw, bw, turn):
    cols, width = dm_ref.shape[1], sums.shape[1]
    turn[...] = jnp.zeros(turn.shape, f32)
    turn[: sums.shape[0]] = sums[...]

    def step(j):
        at = block(j)
        grad = dot_tn(a1_ref[:, at], dm_ref[...])
        proj = dot_tn(aba[:, at], ca[...]) + dot_tn(abb[:, at], cb[...])
        out[at, : out.shape[1] - LANES] = jnp.concatenate([grad, proj], 1).astype(out.dtype)
        out[at, out.shape[1] - LANES :] = turn[:, at].T.astype(out.dtype)

    for j in range(out.shape[0] // RB):
        step(j)
    starts(info, out, fw, bw)


def norm_one_kernel(info, x_ref, own, received, dra, drb, norm_ref, out):
    unit, scale = norm_stats(x_ref[block(info[2]), :].astype(f32))
    grad = own[...] + received[...].astype(f32)
    dr = jnp.where(info[1] == 0, dra[...], drb[...])
    out[...] = dr + norm_back(unit, scale, norm_ref[0:1], grad)


def first_kernel(heads, info, src, d0, d1, d2, d3, out):
    mp = info[2]
    out[...] = jnp.zeros(out.shape, f32)
    for g in range(heads):
        user = jnp.int32(H)
        for h in range(H):
            user = jnp.where(src[h] == mp * heads + g, h, user)
        held = user // heads
        for r, ref in enumerate((d0, d1, d2, d3)):

            @pl.when((user < H) & (held == mp ^ r))
            def _():
                out[g * HD : (g + 1) * HD, :] = ref[block(user - held * heads, HD), :].astype(f32)


def adamw(master, moment, second, grad, rate, weighted):
    moment_new = 0.9 * moment + 0.1 * grad
    second_new = 0.999 * second + 0.001 * grad * grad
    mean_hat = moment_new / (1.0 - 0.9**ADAM_STEP)
    var_hat = second_new / (1.0 - 0.999**ADAM_STEP)
    master_new = master - rate * (mean_hat / (jnp.sqrt(var_hat) + 1e-08) + weighted * master)
    return (master_new, moment_new, second_new)


def adam_kernel(names, turned, info, full, a, b, *refs):
    ins, outs = refs[:6], refs[6:12]
    rows = a.shape[0]
    grad = a[...].astype(f32) + b[...].astype(f32)
    grad += full[block(info[4], rows), :].astype(f32)
    cols = ins[0].shape[1]
    if turned:
        grad = grad[:, : cols + ins[3].shape[0]]
    second = grad[:, cols:]
    if turned:
        second = jnp.concatenate([second, jnp.zeros((LANES - rows, second.shape[1]), f32)], 0).T[:, :rows]
    for k, (name, part) in enumerate(zip(names, (grad[:, :cols], second))):
        new = adamw(*[r[...] for r in ins[3 * k : 3 * k + 3]], part, RATES[name], 0.1)
        for ref, value in zip(outs[3 * k : 3 * k + 3], new):
            ref[...] = value


def norm_sum_kernel(info, full, a, b, out, turn):
    rows, width = a.shape
    at = slice(width - LANES, width)
    grad = a[:, at].astype(f32) + b[:, at].astype(f32) + full[block(info[4], rows), at].astype(f32)
    turn[...] = jnp.zeros(turn.shape, f32)
    turn[:rows] = grad
    out[...] = turn[...].T[:8]


def norm_adam_kernel(sums, received, w, m, s, w_out, m_out, s_out):
    rows, cols = w.shape
    grad = (sums[...] + received[...])[:rows, :cols]
    new = adamw(w[...], m[...], s[...], grad, RATES["norm"], 0.0)
    for ref, value in zip((w_out, m_out, s_out), new):
        ref[...] = value


def sum_kernel(a, b, out):
    out[...] = a[...] + b[...]


def swap_core(value):
    return lax.ppermute(value, "mp", [(i, i ^ 1) for i in range(4)])


def swap_x(value):
    return lax.ppermute(value, "mp", [(i, i ^ 2) for i in range(4)])


def both_cores(value):
    return lax.all_gather(value, "mp", axis_index_groups=[[0, 1], [2, 3]], axis=0, tiled=True)


FORWARD = [(RING[i], RING[(i + 1) % 8]) for i in range(8)]
BACKWARD = [(b, a) for a, b in FORWARD]


def ahead(value):
    return lax.ppermute(value, "dp", FORWARD)


def behind(value):
    return lax.ppermute(value, "dp", BACKWARD)


def after(value, *others):
    return lax.optimization_barrier((value,) + others)[0]


class Gather:
    def __init__(self, piece):
        self.ring = lax.axis_size("dp") == len(RING)
        self.start = self.a = self.b = piece
        self.ahead, self.behind = [], []

    def step(self, *gates):
        if not self.ring:
            return
        self.a, self.b = lax.optimization_barrier((self.a, self.b) + gates)[:2]
        self.a = ahead(self.a)
        self.ahead.append(self.a)
        if len(self.behind) < 3:
            self.b = behind(self.b)
            self.behind.append(self.b)

    def pieces(self):
        if not self.ring:
            return [lax.all_gather(self.start, "dp", axis=0, tiled=True)]
        return [self.start] + self.ahead + self.behind


class Scatter:
    def __init__(self, name, info, full, fw, bw):
        self.ring = lax.axis_size("dp") == len(RING)
        self.name, self.info, self.full, self.a, self.b = name, info, full, fw, bw
        self.steps = 0

    def step(self, *gates):
        if not self.ring:
            return
        self.a = after(self.a, *gates)
        k = 4 - self.steps
        shape = (self.a.shape, bf16)
        if k in (3, 2):
            kernel = functools.partial(hop_kernel, k, 1 - k)
            self.a, self.b = call(kernel, f"{self.name}_hop{k}", (self.info,), [self.full, self.a, self.b], [shape] * 2)
        if k == 1:
            (self.a,) = call(hop_last_kernel, f"{self.name}_hop1", (self.info,), [self.full, self.a], [shape])
        self.last = self.a
        self.a = ahead(self.a)
        if k > 1:
            self.b = behind(self.b)
        self.steps += 1

    def ends(self):
        return (self.a, self.b) if self.ring else None


def update(name, info, full, ends, firsts, seconds, turned):
    first, second = name
    outs = [(w.shape, f32) for w in firsts + seconds]
    if ends is not None:
        new = call(
            functools.partial(adam_kernel, name, turned),
            f"adam_{first}",
            (info,),
            [full, *ends, *firsts, *seconds],
            outs,
        )
        return tuple(new[:3]), tuple(new[3:])
    grad = lax.psum_scatter(full.astype(f32), "dp", scatter_dimension=0, tiled=True)
    cols = firsts[0].shape[1]
    other = grad[:, cols : cols + seconds[0].shape[0 if turned else 1]]
    return (
        adamw(*firsts, grad[:, :cols], RATES[first], 0.1),
        adamw(*seconds, other.T if turned else other, RATES[second], 0.1),
    )


def local(
    tokens_in,
    first_values,
    skip_source,
    grad_out,
    qkv_weight,
    proj_weight,
    fc_weight,
    down_weight,
    norm_params,
    qkv_moment,
    proj_moment,
    fc_moment,
    down_moment,
    norm_moment,
    qkv_second,
    proj_second,
    fc_second,
    down_second,
    norm_second,
):
    n = lax.axis_size("dp")
    ring = n == len(RING)
    pieces = n if ring else 1
    count, width = tokens_in.shape
    cols = qkv_weight.shape[1]
    heads = cols // (3 * HD)
    cw = heads * HD
    hid = fc_weight.shape[1]
    wide = -(-(cols + 4) // LANES) * LANES
    half = count // 2
    shard = qkv_weight.shape[0]
    info = HERE
    src = skip_source

    if ring:
        (ring_one,) = call(
            prep_one_kernel,
            "prep_one",
            (),
            [qkv_weight, norm_params],
            [((shard, wide), bf16)],
            scratch=[
                pltpu.VMEM((shard, cols), f32),
                pltpu.VMEM(norm_params.shape, f32),
                pltpu.VMEM((LANES, LANES), f32),
                pltpu.SemaphoreType.DMA((2,)),
            ],
            vmem=60,
            far=True,
        )
        proj_t, fc_low, down_t = call(
            prep_two_kernel,
            "prep_two",
            (),
            [after(proj_weight, ring_one), fc_weight, down_weight.T],
            [((shard, cw), bf16), ((shard, hid), bf16), ((shard, hid), bf16)],
            scratch=[
                pltpu.VMEM((cw, shard), f32),
                pltpu.VMEM((shard, hid), f32),
                pltpu.VMEM((shard, hid), f32),
                pltpu.VMEM((cw, LANES), f32),
                pltpu.SemaphoreType.DMA((3,)),
            ],
            vmem=56,
            far=True,
        )
    else:
        blank = jnp.zeros((shard, wide - cols - 4), bf16)
        ring_one = jnp.concatenate([qkv_weight.astype(bf16), norm_params.T.astype(bf16), blank], 1)
        proj_t, fc_low, down_t = proj_weight.T.astype(bf16), fc_weight.astype(bf16), down_weight.T.astype(bf16)
    fence = lambda *values: lax.optimization_barrier(values)
    fence = lambda *values: lax.optimization_barrier(values)
    one = Gather(ring_one)
    one.step()
    one.a, one.b, proj_t, tokens = fence(one.a, one.b, proj_t, tokens_in)
    one.step()
    proj_x = swap_x(proj_t)
    (unit_one,) = call(unit_kernel, "unit", (), [tokens], [((count, width), f32)])
    one.a, one.b, proj_x, unit_one = fence(one.a, one.b, proj_x, unit_one)
    one.step()
    if ring:
        (ring_two,) = call(
            join_kernel, "join", (), [fc_low, proj_t, proj_x], [((shard, hid + 2 * cw), bf16)]
        )
    else:
        ring_two = jnp.concatenate([fc_low, proj_t, proj_x], 1)
    two, three = Gather(ring_two), Gather(down_t)
    two.step()
    first_t = after(first_values.T, unit_one)
    first_x, first_c = swap_x(first_t), swap_core(first_t)
    one.a, one.b = fence(one.a, one.b)
    one.step()
    one.a, two.a, two.b, unit_one, first_x, three.a = fence(one.a, two.a, two.b, unit_one, first_x, three.a)
    if ring:
        one.ahead[-1] = one.a
    first_xc = swap_core(first_x)
    two.step()
    three.step()

    a1, mixed, fresh, qkv_full, norms = call(
        functools.partial(qkv_kernel, pieces, heads),
        "qkv",
        (info,),
        [unit_one, *one.pieces()],
        [
            ((count, width), bf16),
            ((count, cols), bf16),
            ((cw, count), bf16),
            ((width, wide), bf16),
            ((8, width), f32),
        ],
    )
    (values,) = call(
        functools.partial(values_kernel, heads),
        "values",
        (info, src),
        [fresh, first_t, first_c, first_x, first_xc],
        [((cw, count), bf16)],
    )

    def attend(part, mixed):
        return call(
            functools.partial(attend_kernel, heads, part * half),
            f"attend{part}",
            (),
            [mixed, values],
            [((half, cw), bf16), ((8, half), f32)],
            scratch=[
                pltpu.VMEM((heads, (part + 1) * half, HD), bf16),
                pltpu.VMEM((heads, half, HD), bf16),
                pltpu.VMEM((cw, half), f32),
            ],
        )

    ctx_a, lse_a = attend(0, mixed)
    two.a, two.b, three.a, three.b, ctx_a = fence(two.a, two.b, three.a, three.b, ctx_a)
    two.step()
    three.step()
    xa = swap_x(ctx_a)
    ctx_b, lse_b = attend(1, after(mixed, ctx_a))
    two.a, two.b, three.a, three.b, xa, ctx_b = fence(two.a, two.b, three.a, three.b, xa, ctx_b)
    two.step()
    three.step()
    xb = swap_x(ctx_b)
    (grad_out,) = call(
        fetch_kernel,
        "fetch",
        (),
        [after(grad_out, ctx_b)],
        [(grad_out.shape, bf16)],
        scratch=[pltpu.SemaphoreType.DMA],
        vmem=4,
        far=True,
    )
    start, xb, two_last, three.a, three.b, grad_out = fence(two.start, xb, two.a, three.a, three.b, grad_out)
    ca, xca, cb, xcb = swap_core(ctx_a), swap_core(xa), swap_core(ctx_b), swap_core(xb)
    three.step()
    context, lse = (ctx_a, ctx_b), (lse_a, lse_b)
    wf, own_w, across_w = call(
        functools.partial(assemble_two_kernel, pieces),
        "assemble_two",
        (info,),
        [start, *two.pieces()[1:]] if ring else two.pieces(),
        [((width, hid), bf16), ((cw, width), bf16), ((cw, width), bf16)],
        scratch=[pltpu.VMEM((width, 2 * cw), bf16)],
    )
    pair = own_w, swap_core(own_w), across_w, swap_core(across_w)

    def mlp(part, norms, contexts):
        return call(
            functools.partial(mlp_kernel, part),
            f"mlp{part}",
            (),
            [tokens, norms, *contexts, *pair, wf],
            [
                ((half, width), f32),
                ((half, width), f32),
                ((half, width), bf16),
                ((half, hid), bf16),
                ((half, hid), f32),
            ],
        )

    def mlp_back(part, grad):
        return call(
            functools.partial(mlp_back_kernel, part),
            f"mlp_back{part}",
            (info,),
            [grad, unit_two[part], slope[part], wf, wd],
            [((half, hid), bf16)] + [((RB // 2, width), bf16)] * 2 + [((RB, width), f32), ((8, width), f32)],
        )

    def mlp_out(part, gate):
        return call(
            mlp_out_kernel,
            f"mlp_out{part}",
            (info,),
            [after(act[part], gate), wd],
            [((RB, width), bf16), ((RB, width), f32)],
        )

    def add(part, keep, *received):
        return call(add_kernel, f"add{part}", (), [keep, *received], [((RB, width), bf16)])[0]

    forward_a = mlp(0, norms, (ctx_a, ca, xa, xca))
    forward_b = mlp(1, after(norms, forward_a[0]), (ctx_b, cb, xb, xcb))
    resid, unit_two, a2, act, slope = zip(forward_a, forward_b)
    start, last = fence(three.start, act[1])
    (wd,) = call(
        functools.partial(assemble_three_kernel, pieces),
        "assemble_three",
        (info,),
        [start, *three.pieces()[1:]] if ring else three.pieces(),
        [((width, hid), bf16)],
    )
    dpre_a, top_a, bottom_a, dkeep_a, nacc_a = mlp_back(0, after(grad_out, act[1]))
    received_a = swap_core(top_a), swap_core(bottom_a)
    dpre_b, top_b, bottom_b, dkeep_b, nacc_b = mlp_back(1, after(grad_out, dpre_a))
    mine_a = add(0, after(dkeep_a, dpre_b), *received_a)
    received_b = swap_core(top_b), swap_core(bottom_b)
    across_a = swap_x(mine_a)

    piece = lambda w: [((width // pieces if ring else 16, w), bf16)] * 2
    mlp_grad, mlp_fw, mlp_bw = call(
        mlp_grad_kernel,
        "mlp_grad",
        (info,),
        [after(a2[0], mine_a), a2[1], dpre_a, dpre_b, grad_out, act[0], act[1]],
        [((width, 2 * hid), bf16 if ring else f32)] + piece(2 * hid),
    )
    mlp_sum = Scatter("mlp", info, mlp_grad, mlp_fw, mlp_bw)
    mlp_sum.step()
    mine_b = add(1, after(dkeep_b, mlp_grad), *received_b)
    across_b = swap_x(mine_b)
    def norm_two(part, mine, across):
        return call(
            functools.partial(norm_two_kernel, part),
            f"norm_two{part}",
            (info,),
            [resid[part], mine, across, grad_out, norms],
            [((RB, width), f32), ((RB, width), bf16)],
        )

    def attend_back(stage, base, blocks, given, part, before, outs):
        return call(
            functools.partial(attend_back_kernel, heads, base, blocks, stage),
            f"attend_back{stage}",
            (info, src),
            [mixed, values, *given, own_w, lse[part], context[part], *before],
            outs,
            vmem=24,
        )

    ysend_a, ykeep_a = mlp_out(0, mine_b)
    ysend_b, ykeep_b = mlp_out(1, mine_b)
    across_a, ysend_a, ysend_b = fence(across_a, ysend_a, ysend_b)
    dr_a, ab_a = norm_two(0, after(mine_a, mine_b), across_a)
    ab_one = both_cores(ab_a)
    dq_a, dk, dv = attend_back(
        0, 0, 2, [ab_one], 0, [], [((half, cw), f32)] * 3
    )
    mlp_sum.a, mlp_sum.b, dq_a = fence(mlp_sum.a, mlp_sum.b, dq_a)
    mlp_sum.step()
    dq_a, ysend_a, ysend_b = fence(dq_a, ysend_a, ysend_b)
    yreceived_a, yreceived_b = swap_core(ysend_a), swap_core(ysend_b)
    rows_mine, rows_sent = call(
        output_rows_kernel,
        "output_rows",
        (info,),
        [ykeep_a, ykeep_b, yreceived_a, yreceived_b],
        [((RB, width), f32), ((RB, width), bf16)],
    )
    dr_b, ab_b = norm_two(1, after(mine_b, ysend_b), across_b)
    ab_two = both_cores(ab_b)
    rows_received = swap_x(after(rows_sent, dr_b))
    top = half + RB
    dq_b, dk, dv = attend_back(
        1, half, 1, [ab_two], 1, [dk, dv], [((RB, cw), f32)] + [((top, cw), f32)] * 2
    )
    mlp_sum.a, mlp_sum.b, dq_b = fence(mlp_sum.a, mlp_sum.b, dq_b)
    mlp_sum.step()
    dmixed, dreused = attend_back(
        2,
        top,
        1,
        [ab_two],
        1,
        [after(dk, mlp_sum.last) if ring else dk, dv, dq_a, dq_b],
        [((count, cols), bf16), ((cw, count), bf16)],
    )

    *isend, ikeep, sums = call(
        input_kernel,
        "input",
        (info,),
        [dmixed, qkv_full, unit_one, nacc_a, nacc_b],
        [((RB, width), bf16)] * 2 + [((half, width), f32), ((8, width), f32)],
    )
    qkv_grad, qkv_fw, qkv_bw = call(
        qkv_grad_kernel,
        "qkv_grad",
        (info,),
        [a1, dmixed, ab_one, ab_two, context[0], context[1], sums],
        [((width, cols + cw + LANES), bf16 if ring else f32)] + piece(cols + cw + LANES),
        scratch=[pltpu.VMEM((LANES, width), f32)],
    )
    qkv_sum = Scatter("qkv", info, qkv_grad, qkv_fw, qkv_bw)
    mlp_sum.a, mlp_sum.b, qkv_sum.a, qkv_sum.b, rows_received = fence(
        mlp_sum.a, mlp_sum.b, qkv_sum.a, qkv_sum.b, rows_received
    )
    mlp_sum.step()
    qkv_sum.step()
    gathered = [swap_core(v) for v in isend]
    mine, sent = call(
        to_rows_kernel, "to_rows", (info,), [ikeep, *gathered], [((RB, width), f32), ((RB, width), bf16)]
    )
    across, dx = swap_x(sent), swap_x(dreused)
    qkv_sum.a, qkv_sum.b, sent = fence(qkv_sum.a, qkv_sum.b, sent)
    qkv_sum.step()
    (block_out,) = call(
        output_kernel,
        "output",
        (info,),
        [resid[0], resid[1], rows_mine, rows_received],
        [((RB, width), bf16)],
    )
    qkv_sum.a, qkv_sum.b, mlp_sum.a, block_out = fence(qkv_sum.a, qkv_sum.b, mlp_sum.a, block_out)
    qkv_sum.step()
    fc_new, down_new = update(
        ("fc", "down"),
        info,
        mlp_grad,
        mlp_sum.ends(),
        [fc_weight, fc_moment, fc_second],
        [down_weight.T, down_moment.T, down_second.T],
        False,
    )
    qkv_sum.a, qkv_sum.b, across, dx, *fc_new = fence(qkv_sum.a, qkv_sum.b, across, dx, *fc_new)
    down_new = tuple(v.T for v in down_new)
    qkv_sum.step()
    (input_grad,) = call(
        norm_one_kernel,
        "norm_one",
        (info,),
        [tokens, mine, across, dr_a, dr_b, norms],
        [((RB, width), f32)],
    )
    dx, dreused = fence(dx, dreused)
    dc, dxc = swap_core(dreused), swap_core(dx)
    (first_grad,) = call(
        functools.partial(first_kernel, heads),
        "first",
        (info, src),
        [dreused, dc, dx, dxc],
        [((cw, count), f32)],
    )
    qkv_sum.a, input_grad, first_grad = fence(qkv_sum.a, input_grad, first_grad)
    if ring:
        (sums,) = call(
            norm_sum_kernel,
            "norm_sum",
            (info,),
            [qkv_grad, *qkv_sum.ends()],
            [((8, LANES), f32)],
            scratch=[pltpu.VMEM((LANES, LANES), f32)],
        )
        (sums,) = call(sum_kernel, "sum", (), [sums, swap_core(sums)], [(sums.shape, f32)])
        received = swap_x(sums)
    qkv_new, proj_new = update(
        ("qkv", "proj"),
        info,
        qkv_grad,
        qkv_sum.ends(),
        [qkv_weight, qkv_moment, qkv_second],
        [proj_weight, proj_moment, proj_second],
        True,
    )
    if ring:
        norm_new = call(
            norm_adam_kernel,
            "adam_norm",
            (),
            [sums, received, norm_params, norm_moment, norm_second],
            [(norm_params.shape, f32)] * 3,
        )
    else:
        own = lax.psum_scatter(lax.psum(sums, "mp"), "dp", scatter_dimension=1, tiled=True)[:4]
        norm_new = adamw(norm_params, norm_moment, norm_second, own, RATES["norm"], 0.0)
    return (block_out, input_grad, first_grad.T, *qkv_new, *proj_new, *fc_new, *down_new, *norm_new)


def solution(mesh):
    both = P("dp", "mp")
    turned = P("mp", "dp")
    rows = P("dp", None)
    every = P(None, "dp")
    state = (both, turned, both, turned, every)
    return jax.shard_map(
        local,
        mesh=mesh,
        in_specs=(rows, both, P(), rows) + state * 3,
        out_specs=(P(("dp", "mp"), None), P(("dp", "mp"), None), both)
        + (both,) * 3
        + (turned,) * 3
        + (both,) * 3
        + (turned,) * 3
        + (every,) * 3,
        check_vma=False,
    )
```
